32 devices in a mesh: tile: 16 (over z, x, core), grp: 2 (over y).
Axes of the slice: x: 2, y: 2, z: 4, core: 2. Of those that a mesh axis runs over, the one named last changes fastest.
Arguments:
- traces: float32 [128, 16, 1500], P(('tile', 'grp')), may hold values from -6 to 6
- validity: int32 [128, 16], P(('tile', 'grp')), may hold values 0 or 1
- boundary_rows: int32 [32, 2, 4], P(('tile', 'grp')), may hold values from 0 to 3, as said below
- boundary_count: int32 [32, 2], P(('tile', 'grp')), may hold values from 1 to 4, as said below
- pair_mask: int32 [128, 24], P(('tile', 'grp')), may hold values from 0 to 1, as said below
Outputs:
- correlations: bfloat16 [128, 24, 2001], P(('tile', 'grp'))
The draws below stay inside these ranges and needn't reach their ends.
Inputs may be any that keep to these rules, and one draw needn't show every extreme that they name: `boundary_rows`: each device's list in each direction orders all of its 4 local stations, each once. `boundary_count`: in every draw some device sends all 4 of its stations in each direction. `pair_mask`: a station's column for itself is 0.
All inputs are finite; a program needn't handle non-finite values. No bound on the sum of `validity` on one device may be relied on, other than what follows from the above.
Results may differ from the reference program's by a relative error of at most 0.008.
Values may be sent and summed in bfloat16 or wider, within the bound.
No kernel may reach another device: no remote copies, remote signals or barrier semaphores. Data moves between devices by JAX's collectives and lax.ppermute only.
A program may use at most 64 MiB of HBM per device.

```python
import math
import jax
import jax.numpy as jnp
from jax import lax

SG = 4
SEG = 16
SAMP = 1500
NBIN = 144
MAXLAG = 1000
LAGS = 2001
TILE_ST = 8
COLS = 24
STATIONS = 128
N_TILE = 16
N_GRP = 2


def draw_boundary_rows(key, part):
    devices_all = N_TILE * N_GRP
    key_list = jax.random.split(key, devices_all * 2)
    orders = jax.vmap(lambda one_key: jax.random.permutation(one_key, SG))(key_list)
    return orders.reshape(devices_all, 2, SG).astype(jnp.int32)


def draw_boundary_count(key, part):
    devices_all = N_TILE * N_GRP
    counts_drawn = jax.random.randint(key, (devices_all, 2), 1, SG + 1)
    fullest = jax.random.randint(jax.random.fold_in(key, 7), (2,), 0, devices_all)
    device_number = jnp.arange(devices_all, dtype=jnp.int32)[:, None]
    return jnp.where(device_number == fullest[None, :], SG, counts_drawn).astype(jnp.int32)


def draw_pair_mask(key, part):
    flags = jax.random.randint(key, (STATIONS, COLS), 0, 4)
    station_number = jnp.arange(STATIONS, dtype=jnp.int32)[:, None]
    group_number = station_number % (SG * N_GRP) // SG
    self_column = group_number * 3 * SG + station_number % SG
    column_number = jnp.arange(COLS, dtype=jnp.int32)[None, :]
    keep = (flags > 0) & (column_number != self_column)
    return keep.astype(jnp.int32)


def set_ends(array, rng, smallest, top_value):
    dims = array.shape
    place = [jax.random.randint(jax.random.fold_in(rng, axis), (), 0, dims[axis]) for axis in range(len(dims))]
    array = array.at[tuple(place)].set(smallest)
    longest = dims.index(max(dims))
    place[longest] = (place[longest] + 1) % dims[longest]
    return array.at[tuple(place)].set(top_value)


def level_of(key, dims, cuts, smallest, largest):
    def one(axis_at, shards_of):
        steps = jax.random.uniform(jax.random.fold_in(jax.random.fold_in(key, 6), axis_at), (shards_of,), jnp.float32, smallest / len(cuts), largest / len(cuts))
        return jnp.repeat(jnp.exp(steps), dims[axis_at] // shards_of).reshape((-1,) + (1,) * (len(dims) - axis_at - 1))

    loudness = one(*cuts[0])
    for cut in cuts[1:]:
        loudness = loudness * one(*cut)
    return loudness


def normal_values(own_key, extent, deviation, most, pieces=(), kind=jnp.bfloat16):
    factor_of = level_of(own_key, extent, pieces, -0.22, 0.18) if pieces else 1.0
    values = jax.random.normal(own_key, extent, jnp.float32) * deviation * factor_of
    return jnp.minimum(jnp.maximum(values, -most), most).astype(kind)


def setup_inputs(seed: int = 0) -> dict:
    streams_of = jax.random.split(jax.random.key(seed), 6)
    return {
        "traces": normal_values(streams_of[0], (STATIONS, SEG, SAMP), 1.0, 6.0, ((0, 32),), jnp.float32),
        "validity": set_ends((jax.random.randint(streams_of[1], (STATIONS, SEG), 0, 5) < 3).astype(jnp.int32), jax.random.fold_in(streams_of[1], 1), 0, 1),
        "boundary_rows": draw_boundary_rows(jax.random.fold_in(streams_of[5], 71), 0),
        "boundary_count": draw_boundary_count(jax.random.fold_in(streams_of[5], 71), 0),
        "pair_mask": draw_pair_mask(jax.random.fold_in(streams_of[5], 71), 0),
    }


def whiten_all(traces, valid_float):
    sample_number = jnp.arange(SAMP, dtype=jnp.float32)
    hann_taper = 0.5 - 0.5 * jnp.cos(sample_number * (2.0 * jnp.pi / SAMP))
    spectrum = jnp.fft.rfft(traces * hann_taper, n=2 * SAMP, axis=-1)[..., 1:NBIN + 1]
    real_part = jnp.real(spectrum)
    imag_part = jnp.imag(spectrum)
    power_bins = real_part * real_part + imag_part * imag_part
    padded = jnp.pad(power_bins, ((0, 0), (0, 0), (4, 4)))
    smooth = sum((padded[:, :, offset:offset + NBIN] for offset in range(9))) / 9.0
    mean_power = lax.optimization_barrier(jnp.mean(power_bins, axis=2, keepdims=True))
    factor = valid_float[:, :, None] / jnp.sqrt(0.5 * smooth + 0.5 * mean_power + 1e-06)
    return jnp.stack([real_part * factor, imag_part * factor], axis=2).astype(jnp.bfloat16)

def reference(traces, validity, boundary_rows, boundary_count, pair_mask):
    valid_float = validity.astype(jnp.float32)
    spectra = whiten_all(traces, valid_float)
    spec_grid = spectra.reshape(N_TILE, N_GRP, SG, SEG, 2, NBIN)
    valid_grid = valid_float.reshape(N_TILE, N_GRP, SG, SEG)
    list_grid = boundary_rows.reshape(N_TILE, N_GRP, 2, SG).astype(jnp.int32)
    count_grid = boundary_count.reshape(N_TILE, N_GRP, 2)
    live_grid = (jnp.arange(SG, dtype=jnp.int32)[None, None, None, :] < count_grid[..., None]).astype(jnp.float32)

    def picked(direction):
        chosen = list_grid[:, :, direction]
        live_now = live_grid[:, :, direction]
        spec_sel = jnp.take_along_axis(spec_grid, chosen[:, :, :, None, None, None], axis=2)
        spec_sel = (spec_sel.astype(jnp.float32) * live_now[:, :, :, None, None, None]).astype(jnp.bfloat16)
        valid_sel = jnp.take_along_axis(valid_grid, chosen[:, :, :, None], axis=2) * live_now[:, :, :, None]
        return (spec_sel, valid_sel)
    sent_up, valid_up = picked(0)
    sent_down, valid_down = picked(1)
    below_spec = jnp.concatenate([jnp.zeros_like(sent_up[:1]), sent_up[:-1]], axis=0)
    below_valid = jnp.concatenate([jnp.zeros_like(valid_up[:1]), valid_up[:-1]], axis=0)
    above_spec = jnp.concatenate([sent_down[1:], jnp.zeros_like(sent_down[:1])], axis=0)
    above_valid = jnp.concatenate([valid_down[1:], jnp.zeros_like(valid_down[:1])], axis=0)
    column_spec = jnp.concatenate([spec_grid, below_spec, above_spec], axis=2).reshape(N_TILE, COLS, SEG, 2, NBIN)
    column_valid = jnp.concatenate([valid_grid, below_valid, above_valid], axis=2).reshape(N_TILE, COLS, SEG)
    own_spec = spectra.reshape(N_TILE, TILE_ST, SEG, 2, NBIN)
    own_valid = valid_float.reshape(N_TILE, TILE_ST, SEG)
    mask_grid = pair_mask.astype(jnp.float32).reshape(N_TILE, TILE_ST, COLS)
    lag_number = jnp.mod(jnp.arange(LAGS, dtype=jnp.int32) - MAXLAG, 2 * SAMP)

    def per_tile(inputs):
        left_spec, left_valid, right_spec, right_valid, mask_tile = inputs
        left_real = left_spec[:, :, 0].astype(jnp.float32)
        left_imag = left_spec[:, :, 1].astype(jnp.float32)
        right_real = right_spec[:, :, 0].astype(jnp.float32)
        right_imag = right_spec[:, :, 1].astype(jnp.float32)
        cross_real = jnp.einsum('iqf,jqf->ijf', left_real, right_real) + jnp.einsum('iqf,jqf->ijf', left_imag, right_imag)
        cross_imag = jnp.einsum('iqf,jqf->ijf', left_imag, right_real) - jnp.einsum('iqf,jqf->ijf', left_real, right_imag)
        pair_count = jnp.einsum('iq,jq->ij', left_valid, right_valid)
        divisor = jnp.maximum(pair_count, 1.0)[:, :, None]
        cross_real = (cross_real / divisor).astype(jnp.bfloat16).astype(jnp.float32)
        cross_imag = (cross_imag / divisor).astype(jnp.bfloat16).astype(jnp.float32)
        bins_full = cross_real + 1j * cross_imag
        bins_full = jnp.pad(bins_full, ((0, 0), (0, 0), (1, SAMP - NBIN)))
        series = jnp.fft.irfft(bins_full, n=2 * SAMP, axis=-1) * SAMP
        chosen_lags = jnp.take(series, lag_number, axis=-1)
        return (chosen_lags / math.sqrt(NBIN) * mask_tile[:, :, None]).astype(jnp.bfloat16)
    result = lax.map(per_tile, (own_spec, own_valid, column_spec, column_valid, mask_grid))
    return result.reshape(STATIONS, COLS, LAGS)
```

```python
import numpy as np
import ml_dtypes

import jax
import jax.numpy as jnp
from jax import lax
from jax.experimental import pallas as pl
from jax.experimental.pallas import tpu as pltpu
from jax.sharding import PartitionSpec as P

NBIN = 144
MAXLAG = 1000
LAGS = 2001
LANE = 128
TAIL = NBIN - LANE
HALF = 64
VALID = 16
WIDE = 3 * LANE
F32 = jnp.float32
BF16 = jnp.bfloat16


def split(table):
    high = table.astype(ml_dtypes.bfloat16)
    low = (table - high.astype(np.float64)).astype(ml_dtypes.bfloat16)
    return high, low


def in_lanes(real, imag):
    out = np.zeros((real.shape[0], WIDE))
    out[:, :LANE] = real[:, :LANE]
    out[:, LANE : 2 * LANE] = imag[:, :LANE]
    out[:, 2 * LANE : 2 * LANE + TAIL] = real[:, LANE:]
    out[:, 2 * LANE + HALF : 2 * LANE + HALF + TAIL] = imag[:, LANE:]
    return out


def fourier_table(samples):
    number = np.arange(samples)
    bins = np.arange(1, NBIN + 1)
    angle = np.mod(number[:, None] * bins[None, :], 2 * samples) * (np.pi / samples)
    taper = (0.5 - 0.5 * np.cos(number * (2.0 * np.pi / samples)))[:, None]
    table = in_lanes(taper * np.cos(angle), -taper * np.sin(angle))
    return split(np.pad(table, ((0, -samples % (2 * LANE)), (0, 0))))


def lag_table(samples):
    lags = np.arange(LAGS) - MAXLAG
    bins = np.arange(1, NBIN + 1)
    angle = np.mod(lags[:, None] * bins[None, :], 2 * samples) * (np.pi / samples)
    scale = 1.0 / np.sqrt(NBIN)
    high, low = split(in_lanes(scale * np.cos(angle), -scale * np.sin(angle)))
    return np.concatenate([high.T, low.T], axis=0)


def iota(shape, dim):
    return lax.broadcasted_iota(jnp.int32, shape, dim)


def spectra_kernel(
    per, seg, samples, rows_ref, count_ref, valid_ref, traces_hbm, high_hbm, low_hbm,
    own_ref, near_ref, far_ref, traces, high, low, sems,
):
    lines = per * seg
    step = 2 * LANE
    cuts = range(0, samples, step)
    copies = []
    first = pltpu.make_async_copy(traces_hbm, traces, sems.at[0])
    first.start()
    for i, at in enumerate(cuts):
        here = pl.ds(at, step)
        a = pltpu.make_async_copy(high_hbm.at[here], high.at[here], sems.at[1 + 2 * i])
        b = pltpu.make_async_copy(low_hbm.at[here], low.at[here], sems.at[2 + 2 * i])
        a.start()
        b.start()
        copies.append((a, b))

    odd = lax.rem(lax.axis_index("tile"), 2)
    col = iota((2 * LANE, 2 * LANE), 0)
    row = iota((2 * LANE, 2 * LANE), 1)

    def bin_of(lane):
        tail = lax.rem(lane, HALF)
        known = (lane < LANE) | (tail < TAIL)
        return known, jnp.where(lane < LANE, lane, LANE + tail)

    known_in, bin_in = bin_of(col)
    known_out, bin_out = bin_of(row)
    near_bins = jnp.abs(bin_in - bin_out) <= 4
    window = jnp.where(known_in & known_out, jnp.where(near_bins, 17.0, 1.0), 0.0).astype(BF16)

    target = iota((lines, lines), 0)
    source = iota((lines, lines), 1)
    slot = lax.rem(target, per)
    part = lax.div(target, per)

    def choice(station):
        return jnp.where(source == station * seg + part, 1.0, 0.0).astype(BF16)

    def listed(direction):
        station = jnp.full((lines, lines), -seg, jnp.int32)
        for j in range(per):
            live = j < count_ref[0, direction]
            pick = jnp.where(live, rows_ref[0, direction, j], -seg)
            station = jnp.where(slot == j, pick, station)
        return choice(station)

    picks = jnp.concatenate([choice(slot), listed(odd), listed(1 - odd)], axis=0)

    numbers = valid_ref[...].astype(F32)
    spread = jnp.concatenate(
        [jnp.broadcast_to(numbers[s : s + 1], (seg, seg)) for s in range(per)], axis=0
    )
    here = lax.rem(iota((lines, seg), 0), seg) == iota((lines, seg), 1)
    usable = jnp.sum(jnp.where(here, spread, 0.0), axis=1, keepdims=True)

    first.wait()
    total = jnp.zeros((lines, WIDE), F32)
    for at, (a, b) in zip(cuts, copies):
        x = traces[:, at : min(at + step, samples)]
        if at + step > samples:
            x = jnp.concatenate([x, jnp.zeros((lines, at + step - samples), F32)], axis=1)
        x_high = x.astype(BF16)
        x_low = (x - x_high.astype(F32)).astype(BF16)
        both = jnp.concatenate([x_high, x_low], axis=0)
        a.wait()
        wide = jnp.dot(both, high[at : at + step, :], preferred_element_type=F32)
        total = total + wide[:lines] + wide[lines:]
        b.wait()
        total = total + jnp.dot(x_high, low[at : at + step, :], preferred_element_type=F32)

    real, imag, tail = total[:, :LANE], total[:, LANE : 2 * LANE], total[:, 2 * LANE :]
    power = jnp.concatenate([real * real + imag * imag, tail * tail], axis=1)
    p_high = power.astype(BF16)
    p_low = (power - p_high.astype(F32)).astype(BF16)
    level = jnp.dot(p_high, window, preferred_element_type=F32)
    level = level + jnp.dot(p_low, window, preferred_element_type=F32)
    factor = usable / jnp.sqrt(level * (1.0 / (2 * NBIN)) + 1e-06)
    tail = tail * factor[:, LANE:]
    tail = jnp.where(iota((lines, LANE), 1) == VALID, usable, tail)
    white = jnp.concatenate([real * factor[:, :LANE], imag * factor[:, :LANE], tail], axis=1)
    chosen = jnp.dot(picks, white.astype(BF16), preferred_element_type=F32).astype(BF16)
    own_ref[...] = chosen[:lines]
    near_ref[...] = chosen[lines : 2 * lines]
    far_ref[...] = chosen[2 * lines :]


def lags_kernel(per, seg, grps, tiles, *refs):
    mask_ref, table_ref, own_ref = refs[:3]
    own_cols = [own_ref, *refs[3 : 2 + grps]]
    near_cols = refs[2 + grps : 2 + 2 * grps]
    far_cols = refs[2 + 2 * grps : 2 + 3 * grps]
    out_ref, spread, cross, result, sems = refs[2 + 3 * grps :]
    lines = per * seg
    columns = 3 * grps * per
    tile = lax.axis_index("tile")
    grp = lax.axis_index("grp")
    odd = lax.rem(tile, 2)
    inside = jnp.where(odd == 1, tile < tiles - 1, tile > 0)

    target = iota((per * lines, lines), 0)
    source = iota((per * lines, lines), 1)
    station = lax.div(target, lines)
    part = lax.div(lax.rem(target, lines), per)
    pick = jnp.where(source == part * per + station, 1.0, 0.0).astype(BF16)
    spread[...] = jnp.dot(pick, own_ref[...], preferred_element_type=F32)

    def stacked(ref):
        sums = [[None] * 4 for _ in range(per)]

        def add(s, i, value):
            sums[s][i] = value if sums[s][i] is None else sums[s][i] + value

        for at in range(0, lines, 16):
            both = ref[at : at + 16, :].astype(F32)
            for half in range(2):
                one = both[8 * half : 8 * half + 8]
                c_re, c_im, c_tail = one[:, :LANE], one[:, LANE : 2 * LANE], one[:, 2 * LANE :]
                c_turn = pltpu.roll(c_tail, HALF, 1)
                for s in range(per):
                    first = s * lines + at + 8 * half
                    left = spread[first : first + 8, :]
                    l_re, l_im, l_tail = left[:, :LANE], left[:, LANE : 2 * LANE], left[:, 2 * LANE :]
                    add(s, 0, l_re * c_re + l_im * c_im)
                    add(s, 1, l_im * c_re - l_re * c_im)
                    add(s, 2, l_tail * c_tail)
                    add(s, 3, l_tail * c_turn)
        low_lanes = iota((8, LANE), 1) < HALF
        out = []
        for s in range(per):
            straight, turned = sums[s][2], sums[s][3]
            straight = straight + pltpu.roll(straight, HALF, 1)
            turned = turned - pltpu.roll(turned, HALF, 1)
            all_lanes = [sums[s][0], sums[s][1], jnp.where(low_lanes, straight, turned)]
            out.append([v + pltpu.roll(v, 4, 0) for v in all_lanes])
        return out

    def by_place(pieces):
        places = []
        for g in range(grps):
            value = pieces[0]
            for d in range(1, grps):
                here = lax.rem(grp + (grps - d), grps) == g
                value = [[jnp.where(here, p, v) for p, v in zip(ps, vs)] for ps, vs in zip(pieces[d], value)]
            places.append(value)
        return places

    def of(cols):
        return by_place([stacked(c) for c in cols])

    own, near, far = of(own_cols), of(near_cols), of(far_cols)
    upper = iota((8, LANE), 0) < 4
    for s in range(per):
        slots = []
        for g in range(grps):
            n = near[g][s]
            f = [jnp.where(inside, v, 0.0) for v in far[g][s]]
            below = [jnp.where(odd == 1, a, b) for a, b in zip(n, f)]
            above = [jnp.where(odd == 1, b, a) for a, b in zip(n, f)]
            slots += [own[g][s], below, above]
        for i in range(0, len(slots), 2):
            rows = [jnp.where(upper, a, b) for a, b in zip(slots[i], slots[i + 1])]
            count = jnp.maximum(rows[2][:, VALID : VALID + 1], 1.0)
            at = s * columns + 4 * i
            for j in range(3):
                cross[at : at + 8, j * LANE : (j + 1) * LANE] = rows[j] / count

    masks = mask_ref[...].astype(F32)
    spread_mask = jnp.concatenate(
        [jnp.broadcast_to(masks[s : s + 1], (columns, columns)) for s in range(per)], axis=0
    )
    here = lax.rem(iota((per * columns, columns), 0), columns) == iota((per * columns, columns), 1)
    keep = jnp.sum(jnp.where(here, spread_mask, 0.0), axis=1, keepdims=True)
    left = (cross[...] * keep).astype(BF16)
    left = jnp.concatenate([left, left], axis=1)
    step = 4 * LANE
    for lo in range(0, LAGS, step):
        hi = min(lo + step, LAGS)
        series = jnp.dot(left, table_ref[:, lo:hi], preferred_element_type=F32).astype(BF16)
        for s in range(per):
            result[s, :, lo:hi] = series[s * columns : (s + 1) * columns]
    copy = pltpu.make_async_copy(result, out_ref, sems.at[0])
    copy.start()
    copy.wait()


def solution(mesh):
    tiles, grps = mesh.shape["tile"], mesh.shape["grp"]
    axes = ("tile", "grp")
    vmem = pl.BlockSpec(memory_space=pltpu.VMEM)
    smem = pl.BlockSpec(memory_space=pltpu.SMEM)
    hbm = pl.BlockSpec(memory_space=pl.ANY)

    def exchange(array, way, by):
        pairs = []
        for t in range(tiles):
            to = (t, t ^ 1, ((t + 1) ^ 1) - 1)[way]
            for g in range(grps):
                if 0 <= to < tiles:
                    goal = to * grps + (g + by) % grps
                else:
                    goal = t * grps + (g + max(by, 1)) % grps
                pairs.append((t * grps + g, goal))
        return lax.ppermute(array, axes, pairs)

    def on_device(traces, validity, boundary_rows, boundary_count, pair_mask):
        per, seg, samples = traces.shape
        lines = per * seg
        columns = pair_mask.shape[1]
        high, low = fourier_table(samples)
        table = lag_table(samples)
        payload = pltpu.VMEM((lines, WIDE), BF16)
        cuts = pl.cdiv(samples, 2 * LANE)
        own, near, far = pl.pallas_call(
            lambda *refs: spectra_kernel(per, seg, samples, *refs),
            out_shape=(payload, payload, payload),
            in_specs=[smem, smem, vmem, hbm, hbm, hbm],
            out_specs=(vmem, vmem, vmem),
            scratch_shapes=[
                pltpu.VMEM((lines, samples), F32),
                pltpu.VMEM(high.shape, BF16),
                pltpu.VMEM(low.shape, BF16),
                pltpu.SemaphoreType.DMA((1 + 2 * cuts,)),
            ],
            compiler_params=pltpu.CompilerParams(vmem_limit_bytes=32 << 20),
            name="spectra",
        )(boundary_rows, boundary_count, validity, traces.reshape(lines, samples), jnp.asarray(high), jnp.asarray(low))
        own_cols = [exchange(own, 0, d) for d in range(1, grps)]
        near_cols = [exchange(near, 1, d) for d in range(grps)]
        far_cols = [exchange(far, 2, d) for d in range(grps)]
        inputs = [jnp.asarray(table), own, *own_cols, *near_cols, *far_cols]
        inputs = [pltpu.with_memory_space_constraint(x, pltpu.VMEM) for x in inputs]
        return pl.pallas_call(
            lambda *refs: lags_kernel(per, seg, grps, tiles, *refs),
            out_shape=jax.ShapeDtypeStruct((per, columns, LAGS), BF16),
            in_specs=[vmem] * (1 + len(inputs)),
            out_specs=hbm,
            scratch_shapes=[
                pltpu.VMEM((per * lines, WIDE), F32),
                pltpu.VMEM((per * columns, WIDE), F32),
                pltpu.VMEM((per, columns, LAGS), BF16),
                pltpu.SemaphoreType.DMA((1,)),
            ],
            compiler_params=pltpu.CompilerParams(vmem_limit_bytes=48 << 20),
            name="lags",
        )(pair_mask, *inputs)

    return jax.shard_map(
        on_device,
        mesh=mesh,
        in_specs=(P(axes, None, None), P(axes, None), P(axes, None, None), P(axes, None), P(axes, None)),
        out_specs=P(axes, None, None),
        check_vma=False,
    )
```

```python
import numpy as np
import ml_dtypes

import jax
import jax.numpy as jnp
from jax import lax
from jax.experimental import pallas as pl
from jax.experimental.pallas import tpu as pltpu
from jax.sharding import PartitionSpec as P

NBIN = 144
MAXLAG = 1000
LAGS = 2001
LANE = 128
TAIL = NBIN - LANE
HALF = 64
VALID = 16
WIDE = 3 * LANE
F32 = jnp.float32
BF16 = jnp.bfloat16


def split(table):
    high = table.astype(ml_dtypes.bfloat16)
    low = (table - high.astype(np.float64)).astype(ml_dtypes.bfloat16)
    return high, low


def in_lanes(real, imag):
    out = np.zeros((real.shape[0], WIDE))
    out[:, :LANE] = real[:, :LANE]
    out[:, LANE : 2 * LANE] = imag[:, :LANE]
    out[:, 2 * LANE : 2 * LANE + TAIL] = real[:, LANE:]
    out[:, 2 * LANE + HALF : 2 * LANE + HALF + TAIL] = imag[:, LANE:]
    return out


def fourier_table(samples):
    number = np.arange(samples)
    bins = np.arange(1, NBIN + 1)
    angle = np.mod(number[:, None] * bins[None, :], 2 * samples) * (np.pi / samples)
    taper = (0.5 - 0.5 * np.cos(number * (2.0 * np.pi / samples)))[:, None]
    table = in_lanes(taper * np.cos(angle), -taper * np.sin(angle))
    return split(np.pad(table, ((0, -samples % (2 * LANE)), (0, 0))))


def lag_table(samples):
    lags = np.arange(LAGS) - MAXLAG
    bins = np.arange(1, NBIN + 1)
    angle = np.mod(lags[:, None] * bins[None, :], 2 * samples) * (np.pi / samples)
    scale = 1.0 / np.sqrt(NBIN)
    high, low = split(in_lanes(scale * np.cos(angle), -scale * np.sin(angle)))
    return np.concatenate([high.T, low.T], axis=0)


def iota(shape, dim):
    return lax.broadcasted_iota(jnp.int32, shape, dim)


def divided(value, by):
    if by & (by - 1) == 0:
        return value >> (by.bit_length() - 1), value & (by - 1)
    return lax.div(value, by), lax.rem(value, by)


def column_of(rows):
    n, m = rows.shape
    diagonal = iota((m, m), 0) == iota((m, m), 1)
    return [
        jnp.sum(jnp.where(diagonal, jnp.broadcast_to(rows[i : i + 1], (m, m)), 0.0), axis=1, keepdims=True)
        for i in range(n)
    ]


def spectra_kernel(
    per, seg, samples, rows_hbm, count_hbm, valid_hbm, traces_hbm, high_hbm, low_hbm,
    own_ref, near_ref, far_ref, rows_ref, count_ref, valid_ref, traces, high, low, sems, small_sems,
):
    lines = per * seg
    step = 2 * LANE
    cuts = range(0, samples, step)
    copies = []
    small = [
        pltpu.make_async_copy(src, dst, small_sems.at[i])
        for i, (src, dst) in enumerate(((rows_hbm, rows_ref), (count_hbm, count_ref), (valid_hbm, valid_ref)))
    ]
    for copy in small:
        copy.start()
    first = pltpu.make_async_copy(traces_hbm, traces, sems.at[0])
    first.start()
    for i, at in enumerate(cuts):
        here = pl.ds(at, step)
        a = pltpu.make_async_copy(high_hbm.at[here], high.at[here], sems.at[1 + 2 * i])
        b = pltpu.make_async_copy(low_hbm.at[here], low.at[here], sems.at[2 + 2 * i])
        a.start()
        b.start()
        copies.append((a, b))

    odd = lax.rem(lax.axis_index("tile"), 2)
    col = iota((2 * LANE, 2 * LANE), 0)
    row = iota((2 * LANE, 2 * LANE), 1)

    def bin_of(lane):
        tail = lane & (HALF - 1)
        known = (lane < LANE) | (tail < TAIL)
        return known, jnp.where(lane < LANE, lane, LANE + tail)

    known_in, bin_in = bin_of(col)
    known_out, bin_out = bin_of(row)
    near_bins = jnp.abs(bin_in - bin_out) <= 4
    window = jnp.where(known_in & known_out, jnp.where(near_bins, 17.0, 1.0), 0.0).astype(BF16)

    target = iota((lines, lines), 0)
    source = iota((lines, lines), 1)
    part, slot = divided(target, per)
    for copy in small:
        copy.wait()

    def choice(station):
        return jnp.where(source == station * seg + part, 1.0, 0.0).astype(BF16)

    def listed(direction):
        station = jnp.full((lines, lines), -seg, jnp.int32)
        for j in range(per):
            live = j < count_ref[0, direction]
            pick = jnp.where(live, rows_ref[0, direction, j], -seg)
            station = jnp.where(slot == j, pick, station)
        return choice(station)

    picks = jnp.concatenate([choice(slot), listed(odd), listed(1 - odd)], axis=0)

    usable = jnp.concatenate(column_of(valid_ref[...].astype(F32)), axis=0)

    first.wait()
    total = jnp.zeros((lines, WIDE), F32)
    for at, (a, b) in zip(cuts, copies):
        x = traces[:, at : min(at + step, samples)]
        if at + step > samples:
            x = jnp.concatenate([x, jnp.zeros((lines, at + step - samples), F32)], axis=1)
        x_high = x.astype(BF16)
        x_low = (x - x_high.astype(F32)).astype(BF16)
        both = jnp.concatenate([x_high, x_low], axis=0)
        a.wait()
        wide = jnp.dot(both, high[at : at + step, :], preferred_element_type=F32)
        total = total + wide[:lines] + wide[lines:]
        b.wait()
        total = total + jnp.dot(x_high, low[at : at + step, :], preferred_element_type=F32)

    real, imag, tail = total[:, :LANE], total[:, LANE : 2 * LANE], total[:, 2 * LANE :]
    power = jnp.concatenate([real * real + imag * imag, tail * tail], axis=1)
    p_high = power.astype(BF16)
    p_low = (power - p_high.astype(F32)).astype(BF16)
    level = jnp.dot(p_high, window, preferred_element_type=F32)
    level = level + jnp.dot(p_low, window, preferred_element_type=F32)
    factor = usable / jnp.sqrt(level * (1.0 / (2 * NBIN)) + 1e-06)
    tail = tail * factor[:, LANE:]
    tail = jnp.where(iota((lines, LANE), 1) == VALID, usable, tail)
    white = jnp.concatenate([real * factor[:, :LANE], imag * factor[:, :LANE], tail], axis=1)
    chosen = jnp.dot(picks, white.astype(BF16), preferred_element_type=F32).astype(BF16)
    own_ref[...] = chosen[:lines]
    near_ref[...] = chosen[lines : 2 * lines]
    far_ref[...] = chosen[2 * lines :]


def ready_kernel(per, seg, mask_hbm, table_hbm, own_ref, mask_ref, table_ref, spread_ref, sems):
    copies = [
        pltpu.make_async_copy(table_hbm, table_ref, sems.at[0]),
        pltpu.make_async_copy(mask_hbm, mask_ref, sems.at[1]),
    ]
    for copy in copies:
        copy.start()
    lines = per * seg
    part, _ = divided(iota((lines, lines), 0), per)
    source = iota((lines, lines), 1)
    pick = [jnp.where(source == part * per + s, 1.0, 0.0).astype(BF16) for s in range(per)]
    spread_ref[...] = jnp.dot(jnp.concatenate(pick, axis=0), own_ref[...], preferred_element_type=F32)
    for copy in copies:
        copy.wait()


def lags_kernel(per, seg, grps, tiles, *refs):
    mask_ref, table_ref, spread = refs[:3]
    refs = refs[3:]
    own_cols, near_cols, far_cols = (refs[i * grps : (i + 1) * grps] for i in range(3))
    out_ref, cross, result, sems = refs[3 * grps :]
    lines = per * seg
    columns = 3 * grps * per
    tile = lax.axis_index("tile")
    grp = lax.axis_index("grp")
    odd = lax.rem(tile, 2)
    inside = jnp.where(odd == 1, tile < tiles - 1, tile > 0)

    def stacked(ref):
        sums = [[None] * 4 for _ in range(per)]

        def add(s, i, value):
            sums[s][i] = value if sums[s][i] is None else sums[s][i] + value

        for at in range(0, lines, 16):
            both = ref[at : at + 16, :].astype(F32)
            for half in range(2):
                one = both[8 * half : 8 * half + 8]
                c_re, c_im, c_tail = one[:, :LANE], one[:, LANE : 2 * LANE], one[:, 2 * LANE :]
                c_turn = pltpu.roll(c_tail, HALF, 1)
                for s in range(per):
                    first = s * lines + at + 8 * half
                    left = spread[first : first + 8, :]
                    l_re, l_im, l_tail = left[:, :LANE], left[:, LANE : 2 * LANE], left[:, 2 * LANE :]
                    add(s, 0, l_re * c_re + l_im * c_im)
                    add(s, 1, l_im * c_re - l_re * c_im)
                    add(s, 2, l_tail * c_tail)
                    add(s, 3, l_tail * c_turn)
        low_lanes = iota((8, LANE), 1) < HALF
        out = []
        for s in range(per):
            straight, turned = sums[s][2], sums[s][3]
            straight = straight + pltpu.roll(straight, HALF, 1)
            turned = turned - pltpu.roll(turned, HALF, 1)
            all_lanes = [sums[s][0], sums[s][1], jnp.where(low_lanes, straight, turned)]
            out.append([v + pltpu.roll(v, 4, 0) for v in all_lanes])
        return out

    def by_place(pieces):
        places = []
        for g in range(grps):
            value = pieces[0]
            for d in range(1, grps):
                here = lax.rem(grp + (grps - d), grps) == g
                value = [[jnp.where(here, p, v) for p, v in zip(ps, vs)] for ps, vs in zip(pieces[d], value)]
            places.append(value)
        return places

    def of(cols):
        return by_place([stacked(c) for c in cols])

    own, near, far = of(own_cols), of(near_cols), of(far_cols)
    upper = iota((8, LANE), 0) < 4
    for s in range(per):
        slots = []
        for g in range(grps):
            n = near[g][s]
            f = [jnp.where(inside, v, 0.0) for v in far[g][s]]
            below = [jnp.where(odd == 1, a, b) for a, b in zip(n, f)]
            above = [jnp.where(odd == 1, b, a) for a, b in zip(n, f)]
            slots += [own[g][s], below, above]
        for i in range(0, len(slots), 2):
            rows = [jnp.where(upper, a, b) for a, b in zip(slots[i], slots[i + 1])]
            count = jnp.maximum(rows[2][:, VALID : VALID + 1], 1.0)
            at = s * columns + 4 * i
            for j in range(3):
                cross[at : at + 8, j * LANE : (j + 1) * LANE] = rows[j] / count

    keep = jnp.concatenate(column_of(mask_ref[...].astype(F32)), axis=0)
    left = (cross[...] * keep).astype(BF16)
    left = jnp.concatenate([left, left], axis=1)
    step = 4 * LANE
    for lo in range(0, LAGS, step):
        hi = min(lo + step, LAGS)
        series = jnp.dot(left, table_ref[:, lo:hi], preferred_element_type=F32).astype(BF16)
        for s in range(per):
            result[s, :, lo:hi] = series[s * columns : (s + 1) * columns]
    copy = pltpu.make_async_copy(result, out_ref, sems.at[0])
    copy.start()
    copy.wait()


def solution(mesh):
    tiles, grps = mesh.shape["tile"], mesh.shape["grp"]
    axes = ("tile", "grp")
    vmem = pl.BlockSpec(memory_space=pltpu.VMEM)
    hbm = pl.BlockSpec(memory_space=pltpu.HBM)
    placed = pltpu.with_memory_space_constraint

    def exchange(array, way, by):
        pairs = []
        for t in range(tiles):
            to = (t, t ^ 1, ((t + 1) ^ 1) - 1)[way]
            for g in range(grps):
                if 0 <= to < tiles:
                    goal = to * grps + (g + by) % grps
                else:
                    goal = t * grps + (g + max(by, 1)) % grps
                pairs.append((t * grps + g, goal))
        return lax.ppermute(array, axes, pairs)

    def on_device(traces, validity, boundary_rows, boundary_count, pair_mask):
        per, seg, samples = traces.shape
        lines = per * seg
        columns = pair_mask.shape[1]
        high, low = map(jnp.asarray, fourier_table(samples))
        table = jnp.asarray(lag_table(samples))
        payload = pltpu.VMEM((lines, WIDE), BF16)
        cuts = pl.cdiv(samples, 2 * LANE)
        inputs = [boundary_rows, boundary_count, validity, traces.reshape(lines, samples), high, low]
        own, near, far = pl.pallas_call(
            lambda *refs: spectra_kernel(per, seg, samples, *refs),
            out_shape=(payload, payload, payload),
            in_specs=[hbm] * len(inputs),
            out_specs=(vmem, vmem, vmem),
            scratch_shapes=[
                pltpu.SMEM(boundary_rows.shape, jnp.int32),
                pltpu.SMEM(boundary_count.shape, jnp.int32),
                pltpu.VMEM(validity.shape, jnp.int32),
                pltpu.VMEM((lines, samples), F32),
                pltpu.VMEM(high.shape, BF16),
                pltpu.VMEM(low.shape, BF16),
                pltpu.SemaphoreType.DMA((1 + 2 * cuts,)),
                pltpu.SemaphoreType.DMA((3,)),
            ],
            compiler_params=pltpu.CompilerParams(vmem_limit_bytes=32 << 20),
            name="spectra",
        )(*[placed(x, pltpu.HBM) for x in inputs])
        own_cols = [exchange(own, 0, d) for d in range(1, grps)]
        near_cols = [exchange(near, 1, d) for d in range(grps)]
        far_cols = [exchange(far, 2, d) for d in range(grps)]
        mask, table, spread = pl.pallas_call(
            lambda *refs: ready_kernel(per, seg, *refs),
            out_shape=(
                pltpu.VMEM(pair_mask.shape, jnp.int32),
                pltpu.VMEM(table.shape, BF16),
                pltpu.VMEM((per * lines, WIDE), F32),
            ),
            in_specs=[hbm, hbm, vmem],
            out_specs=(vmem, vmem, vmem),
            scratch_shapes=[pltpu.SemaphoreType.DMA((2,))],
            compiler_params=pltpu.CompilerParams(vmem_limit_bytes=32 << 20),
            name="ready",
        )(placed(pair_mask, pltpu.HBM), placed(table, pltpu.HBM), placed(own, pltpu.VMEM))
        inputs = [mask, table, spread, own, *own_cols, *near_cols, *far_cols]
        return pl.pallas_call(
            lambda *refs: lags_kernel(per, seg, grps, tiles, *refs),
            out_shape=jax.ShapeDtypeStruct((per, columns, LAGS), BF16),
            in_specs=[vmem] * len(inputs),
            out_specs=hbm,
            scratch_shapes=[
                pltpu.VMEM((per * columns, WIDE), F32),
                pltpu.VMEM((per, columns, LAGS), BF16),
                pltpu.SemaphoreType.DMA((1,)),
            ],
            compiler_params=pltpu.CompilerParams(vmem_limit_bytes=32 << 20),
            name="lags",
        )(*[placed(x, pltpu.VMEM) for x in inputs])

    return jax.shard_map(
        on_device,
        mesh=mesh,
        in_specs=(P(axes, None, None), P(axes, None), P(axes, None, None), P(axes, None), P(axes, None)),
        out_specs=P(axes, None, None),
        check_vma=False,
    )
```

```python
import numpy as np
import ml_dtypes

import jax
import jax.numpy as jnp
from jax import lax
from jax.experimental import pallas as pl
from jax.experimental.pallas import tpu as pltpu
from jax.sharding import PartitionSpec as P

NBIN = 144
MAXLAG = 1000
LAGS = 2001
LANE = 128
TAIL = NBIN - LANE
HALF = 64
VALID = 16
WIDE = 3 * LANE
LAG_STEP = 4 * LANE
STEP = 2 * LANE
F32 = jnp.float32
BF16 = jnp.bfloat16


def split(table):
    high = table.astype(ml_dtypes.bfloat16)
    low = (table - high.astype(np.float64)).astype(ml_dtypes.bfloat16)
    return high, low


def in_lanes(real, imag):
    out = np.zeros((real.shape[0], WIDE))
    out[:, :LANE] = real[:, :LANE]
    out[:, LANE : 2 * LANE] = imag[:, :LANE]
    out[:, 2 * LANE : 2 * LANE + TAIL] = real[:, LANE:]
    out[:, 2 * LANE + HALF : 2 * LANE + HALF + TAIL] = imag[:, LANE:]
    return out


def fourier_tables(samples):
    bins = np.arange(1, NBIN + 1)
    turn = np.pi / samples
    angle = np.mod(np.arange(STEP)[:, None] * bins[None, :], 2 * samples) * turn
    high, low = split(in_lanes(np.cos(angle), -np.sin(angle)))
    stretches = -(-samples // STEP)
    angle = np.mod(np.arange(stretches)[:, None] * STEP * bins[None, :], 2 * samples) * turn
    turns = np.stack([in_lanes(np.cos(angle), np.cos(angle)), in_lanes(np.sin(angle), -np.sin(angle))])
    number = np.arange(stretches * STEP)
    taper = np.where(number < samples, 0.5 - 0.5 * np.cos(number * (2.0 * np.pi / samples)), 0.0)
    rows = np.concatenate([taper.reshape(stretches, STEP), np.zeros((stretches, WIDE - STEP))], axis=1)
    factors = np.concatenate([rows[None], turns]).astype(np.float32)
    return np.concatenate([high, high, low]), factors


def lag_table(samples):
    lags = np.arange(LAGS) - MAXLAG
    bins = np.arange(1, NBIN + 1)
    angle = np.mod(lags[:, None] * bins[None, :], 2 * samples) * (np.pi / samples)
    scale = 1.0 / np.sqrt(NBIN)
    high, low = split(in_lanes(scale * np.cos(angle), -scale * np.sin(angle)))
    return np.concatenate([high.T, low.T], axis=0)


def iota(shape, dim):
    return lax.broadcasted_iota(jnp.int32, shape, dim)


def divided(value, by):
    if by & (by - 1) == 0:
        return value >> (by.bit_length() - 1), value & (by - 1)
    return lax.div(value, by), lax.rem(value, by)


def column_of(rows):
    n, m = rows.shape
    diagonal = iota((m, m), 0) == iota((m, m), 1)
    return [
        jnp.sum(jnp.where(diagonal, jnp.broadcast_to(rows[i : i + 1], (m, m)), 0.0), axis=1, keepdims=True)
        for i in range(n)
    ]


def spectra_kernel(
    per, seg, samples, rows_hbm, count_hbm, valid_hbm, traces_hbm, table_hbm, factors_hbm,
    own_ref, near_ref, far_ref, rows_ref, count_ref, valid_ref, traces, table, factors, sems,
):
    lines = per * seg
    pairs = [
        (traces_hbm, traces), (table_hbm, table), (factors_hbm, factors),
        (rows_hbm, rows_ref), (count_hbm, count_ref), (valid_hbm, valid_ref),
    ]
    copies = [pltpu.make_async_copy(src, dst, sems.at[i]) for i, (src, dst) in enumerate(pairs)]
    for copy in copies:
        copy.start()

    odd = lax.rem(lax.axis_index("tile"), 2)
    col = iota((STEP, STEP), 0)
    row = iota((STEP, STEP), 1)

    def bin_of(lane):
        tail = lane & (HALF - 1)
        known = (lane < LANE) | (tail < TAIL)
        return known, jnp.where(lane < LANE, lane, LANE + tail)

    known_in, bin_in = bin_of(col)
    known_out, bin_out = bin_of(row)
    near_bins = jnp.abs(bin_in - bin_out) <= 4
    window = jnp.where(known_in & known_out, jnp.where(near_bins, 17.0, 1.0), 0.0).astype(BF16)

    target = iota((lines, lines), 0)
    source = iota((lines, lines), 1)
    part, slot = divided(target, per)
    for copy in copies[-3:]:
        copy.wait()

    def choice(station):
        return jnp.where(source == station * seg + part, 1.0, 0.0).astype(BF16)

    def listed(direction):
        station = jnp.full((lines, lines), -seg, jnp.int32)
        for j in range(per):
            live = j < count_ref[0, direction]
            pick = jnp.where(live, rows_ref[0, direction, j], -seg)
            station = jnp.where(slot == j, pick, station)
        return choice(station)

    picks = jnp.concatenate([choice(slot), listed(odd), listed(1 - odd)], axis=0)

    usable = jnp.concatenate(column_of(valid_ref[...].astype(F32)), axis=0)

    for copy in copies[:3]:
        copy.wait()
    stretches = factors.shape[1]
    left = []
    for j in range(stretches):
        at = j * STEP
        x = traces[:, at : min(at + STEP, samples)]
        if at + STEP > samples:
            x = jnp.concatenate([x, jnp.zeros((lines, at + STEP - samples), F32)], axis=1)
        x = x * factors[0, j : j + 1, :STEP]
        x_high = x.astype(BF16)
        x_low = (x - x_high.astype(F32)).astype(BF16)
        left.append(jnp.concatenate([x_high, x_low, x_high], axis=1))
    parts = jnp.dot(jnp.concatenate(left, axis=0), table[...], preferred_element_type=F32)
    real, imag, tail = (parts[:lines, k * LANE : (k + 1) * LANE] for k in range(3))
    for j in range(1, stretches):
        p_re, p_im, p_tail = (parts[j * lines : (j + 1) * lines, k * LANE : (k + 1) * LANE] for k in range(3))
        turn = factors[1, j : j + 1, :]
        swap = factors[2, j : j + 1, :]
        real = real + p_re * turn[:, :LANE] + p_im * swap[:, :LANE]
        imag = imag + p_im * turn[:, LANE : 2 * LANE] + p_re * swap[:, LANE : 2 * LANE]
        tail = tail + p_tail * turn[:, 2 * LANE :] + pltpu.roll(p_tail, HALF, 1) * swap[:, 2 * LANE :]

    power = jnp.concatenate([real * real + imag * imag, tail * tail], axis=1)
    p_high = power.astype(BF16)
    p_low = (power - p_high.astype(F32)).astype(BF16)
    level = jnp.dot(p_high, window, preferred_element_type=F32)
    level = level + jnp.dot(p_low, window, preferred_element_type=F32)
    factor = usable / jnp.sqrt(level * (1.0 / (2 * NBIN)) + 1e-06)
    tail = tail * factor[:, LANE:]
    tail = jnp.where(iota((lines, LANE), 1) == VALID, usable, tail)
    white = jnp.concatenate([real * factor[:, :LANE], imag * factor[:, :LANE], tail], axis=1)
    chosen = jnp.dot(picks, white.astype(BF16), preferred_element_type=F32).astype(BF16)
    own_ref[...] = chosen[:lines]
    near_ref[...] = chosen[lines : 2 * lines]
    far_ref[...] = chosen[2 * lines :]


def ready_kernel(per, seg, mask_hbm, table_hbm, own_ref, mask_ref, table_ref, spread_ref, sems):
    copies = [
        pltpu.make_async_copy(table_hbm, table_ref, sems.at[0]),
        pltpu.make_async_copy(mask_hbm, mask_ref, sems.at[1]),
    ]
    for copy in copies:
        copy.start()
    lines = per * seg
    part, _ = divided(iota((lines, lines), 0), per)
    source = iota((lines, lines), 1)
    pick = [jnp.where(source == part * per + s, 1.0, 0.0).astype(BF16) for s in range(per)]
    spread_ref[...] = jnp.dot(jnp.concatenate(pick, axis=0), own_ref[...], preferred_element_type=F32)
    for copy in copies:
        copy.wait()


def lags_kernel(per, seg, grps, tiles, *refs):
    mask_ref, table_ref, spread = refs[:3]
    refs = refs[3:]
    own_cols, near_cols, far_cols = (refs[i * grps : (i + 1) * grps] for i in range(3))
    out_ref, cross, result, sems = refs[3 * grps :]
    lines = per * seg
    columns = 3 * grps * per
    tile = lax.axis_index("tile")
    grp = lax.axis_index("grp")
    odd = lax.rem(tile, 2)
    inside = jnp.where(odd == 1, tile < tiles - 1, tile > 0)

    def stacked(ref):
        sums = [[None] * 4 for _ in range(per)]

        def add(s, i, value):
            sums[s][i] = value if sums[s][i] is None else sums[s][i] + value

        for at in range(0, lines, 16):
            both = ref[at : at + 16, :].astype(F32)
            for half in range(2):
                one = both[8 * half : 8 * half + 8]
                c_re, c_im, c_tail = one[:, :LANE], one[:, LANE : 2 * LANE], one[:, 2 * LANE :]
                c_turn = pltpu.roll(c_tail, HALF, 1)
                for s in range(per):
                    first = s * lines + at + 8 * half
                    left = spread[first : first + 8, :]
                    l_re, l_im, l_tail = left[:, :LANE], left[:, LANE : 2 * LANE], left[:, 2 * LANE :]
                    add(s, 0, l_re * c_re + l_im * c_im)
                    add(s, 1, l_im * c_re - l_re * c_im)
                    add(s, 2, l_tail * c_tail)
                    add(s, 3, l_tail * c_turn)
        low_lanes = iota((8, LANE), 1) < HALF
        out = []
        for s in range(per):
            straight, turned = sums[s][2], sums[s][3]
            straight = straight + pltpu.roll(straight, HALF, 1)
            turned = turned - pltpu.roll(turned, HALF, 1)
            all_lanes = [sums[s][0], sums[s][1], jnp.where(low_lanes, straight, turned)]
            out.append([v + pltpu.roll(v, 4, 0) for v in all_lanes])
        return out

    def by_place(pieces):
        places = []
        for g in range(grps):
            value = pieces[0]
            for d in range(1, grps):
                here = lax.rem(grp + (grps - d), grps) == g
                value = [[jnp.where(here, p, v) for p, v in zip(ps, vs)] for ps, vs in zip(pieces[d], value)]
            places.append(value)
        return places

    def of(cols):
        return by_place([stacked(c) for c in cols])

    own, near, far = of(own_cols), of(near_cols), of(far_cols)
    upper = iota((8, LANE), 0) < 4
    for s in range(per):
        slots = []
        for g in range(grps):
            n = near[g][s]
            f = [jnp.where(inside, v, 0.0) for v in far[g][s]]
            below = [jnp.where(odd == 1, a, b) for a, b in zip(n, f)]
            above = [jnp.where(odd == 1, b, a) for a, b in zip(n, f)]
            slots += [own[g][s], below, above]
        for i in range(0, len(slots), 2):
            rows = [jnp.where(upper, a, b) for a, b in zip(slots[i], slots[i + 1])]
            count = jnp.maximum(rows[2][:, VALID : VALID + 1], 1.0)
            at = s * columns + 4 * i
            for j in range(3):
                cross[at : at + 8, j * LANE : (j + 1) * LANE] = rows[j] / count

    keep = jnp.concatenate(column_of(mask_ref[...].astype(F32)), axis=0)
    left = (cross[...] * keep).astype(BF16)
    left = jnp.concatenate([left, left], axis=1)
    copies = []
    for i, lo in enumerate(range(0, LAGS, LAG_STEP)):
        hi = min(lo + LAG_STEP, LAGS)
        series = jnp.dot(left, table_ref[:, lo:hi], preferred_element_type=F32).astype(BF16)
        for s in range(per):
            result[s, :, lo:hi] = series[s * columns : (s + 1) * columns]
        here = (slice(None), slice(None), slice(lo, hi))
        copies.append(pltpu.make_async_copy(result.at[here], out_ref.at[here], sems.at[i]))
        copies[-1].start()
    for copy in copies:
        copy.wait()


def solution(mesh):
    tiles, grps = mesh.shape["tile"], mesh.shape["grp"]
    axes = ("tile", "grp")
    vmem = pl.BlockSpec(memory_space=pltpu.VMEM)
    hbm = pl.BlockSpec(memory_space=pltpu.HBM)
    placed = pltpu.with_memory_space_constraint

    def exchange(array, way, by):
        pairs = []
        for t in range(tiles):
            to = (t, t ^ 1, ((t + 1) ^ 1) - 1)[way]
            for g in range(grps):
                if 0 <= to < tiles:
                    goal = to * grps + (g + by) % grps
                else:
                    goal = t * grps + (g + max(by, 1)) % grps
                pairs.append((t * grps + g, goal))
        return lax.ppermute(array, axes, pairs)

    def on_device(traces, validity, boundary_rows, boundary_count, pair_mask):
        per, seg, samples = traces.shape
        lines = per * seg
        columns = pair_mask.shape[1]
        table, factors = map(jnp.asarray, fourier_tables(samples))
        lag_basis = jnp.asarray(lag_table(samples))
        payload = pltpu.VMEM((lines, WIDE), BF16)
        inputs = [boundary_rows, boundary_count, validity, traces.reshape(lines, samples), table, factors]
        own, near, far = pl.pallas_call(
            lambda *refs: spectra_kernel(per, seg, samples, *refs),
            out_shape=(payload, payload, payload),
            in_specs=[hbm] * len(inputs),
            out_specs=(vmem, vmem, vmem),
            scratch_shapes=[
                pltpu.SMEM(boundary_rows.shape, jnp.int32),
                pltpu.SMEM(boundary_count.shape, jnp.int32),
                pltpu.VMEM(validity.shape, jnp.int32),
                pltpu.VMEM((lines, samples), F32),
                pltpu.VMEM(table.shape, BF16),
                pltpu.VMEM(factors.shape, F32),
                pltpu.SemaphoreType.DMA((6,)),
            ],
            compiler_params=pltpu.CompilerParams(vmem_limit_bytes=32 << 20),
            name="spectra",
        )(*[placed(x, pltpu.HBM) for x in inputs])
        own_cols = [exchange(own, 0, d) for d in range(1, grps)]
        near_cols = [exchange(near, 1, d) for d in range(grps)]
        far_cols = [exchange(far, 2, d) for d in range(grps)]
        mask, basis, spread = pl.pallas_call(
            lambda *refs: ready_kernel(per, seg, *refs),
            out_shape=(
                pltpu.VMEM(pair_mask.shape, jnp.int32),
                pltpu.VMEM(lag_basis.shape, BF16),
                pltpu.VMEM((per * lines, WIDE), F32),
            ),
            in_specs=[hbm, hbm, vmem],
            out_specs=(vmem, vmem, vmem),
            scratch_shapes=[pltpu.SemaphoreType.DMA((2,))],
            compiler_params=pltpu.CompilerParams(vmem_limit_bytes=32 << 20),
            name="ready",
        )(placed(pair_mask, pltpu.HBM), placed(lag_basis, pltpu.HBM), placed(own, pltpu.VMEM))
        inputs = [mask, basis, spread, own, *own_cols, *near_cols, *far_cols]
        return pl.pallas_call(
            lambda *refs: lags_kernel(per, seg, grps, tiles, *refs),
            out_shape=jax.ShapeDtypeStruct((per, columns, LAGS), BF16),
            in_specs=[vmem] * len(inputs),
            out_specs=hbm,
            scratch_shapes=[
                pltpu.VMEM((per * columns, WIDE), F32),
                pltpu.VMEM((per, columns, LAGS), BF16),
                pltpu.SemaphoreType.DMA((pl.cdiv(LAGS, LAG_STEP),)),
            ],
            compiler_params=pltpu.CompilerParams(vmem_limit_bytes=32 << 20),
            name="lags",
        )(*[placed(x, pltpu.VMEM) for x in inputs])

    return jax.shard_map(
        on_device,
        mesh=mesh,
        in_specs=(P(axes, None, None), P(axes, None), P(axes, None, None), P(axes, None), P(axes, None)),
        out_specs=P(axes, None, None),
        check_vma=False,
    )
```

```python
import numpy as np
import ml_dtypes

import jax
import jax.numpy as jnp
from jax import lax
from jax.experimental import pallas as pl
from jax.experimental.pallas import tpu as pltpu
from jax.sharding import PartitionSpec as P

NBIN = 144
MAXLAG = 1000
LAGS = 2001
LANE = 128
TAIL = NBIN - LANE
HALF = 64
LAST = ((0, 1), (1, 0))
VALID = 16
WIDE = 3 * LANE
LAG_STEP = 4 * LANE
STEP = 2 * LANE
F32 = jnp.float32
BF16 = jnp.bfloat16


def split(table):
    high = table.astype(ml_dtypes.bfloat16)
    low = (table - high.astype(np.float64)).astype(ml_dtypes.bfloat16)
    return high, low


def in_lanes(real, imag):
    out = np.zeros((real.shape[0], WIDE))
    out[:, :LANE] = real[:, :LANE]
    out[:, LANE : 2 * LANE] = imag[:, :LANE]
    out[:, 2 * LANE : 2 * LANE + TAIL] = real[:, LANE:]
    out[:, 2 * LANE + HALF : 2 * LANE + HALF + TAIL] = imag[:, LANE:]
    return out


def fourier_tables(samples):
    bins = np.arange(1, NBIN + 1)
    turn = np.pi / samples
    angle = np.mod(np.arange(STEP)[:, None] * bins[None, :], 2 * samples) * turn
    high, low = split(in_lanes(np.cos(angle), -np.sin(angle)))
    stretches = -(-samples // STEP)
    angle = np.mod(np.arange(stretches)[:, None] * STEP * bins[None, :], 2 * samples) * turn
    turns = np.stack([in_lanes(np.cos(angle), np.cos(angle)), in_lanes(np.sin(angle), -np.sin(angle))])
    number = np.arange(stretches * STEP)
    taper = np.where(number < samples, 0.5 - 0.5 * np.cos(number * (2.0 * np.pi / samples)), 0.0)
    rows = np.concatenate([taper.reshape(stretches, STEP), np.zeros((stretches, WIDE - STEP))], axis=1)
    factors = np.concatenate([rows[None], turns]).astype(np.float32)
    return np.concatenate([high, high, low]), factors


def lag_table(samples):
    lags = np.arange(LAGS) - MAXLAG
    bins = np.arange(1, NBIN + 1)
    angle = np.mod(lags[:, None] * bins[None, :], 2 * samples) * (np.pi / samples)
    scale = 1.0 / np.sqrt(NBIN)
    high, low = split(in_lanes(scale * np.cos(angle), -scale * np.sin(angle)))
    return np.concatenate([high.T, low.T], axis=0)


def iota(shape, dim):
    return lax.broadcasted_iota(jnp.int32, shape, dim)


def divided(value, by):
    if by & (by - 1) == 0:
        return value >> (by.bit_length() - 1), value & (by - 1)
    return lax.div(value, by), lax.rem(value, by)


def column_of(rows):
    n, m = rows.shape
    diagonal = iota((m, m), 0) == iota((m, m), 1)
    return [
        jnp.sum(jnp.where(diagonal, jnp.broadcast_to(rows[i : i + 1], (m, m)), 0.0), axis=1, keepdims=True)
        for i in range(n)
    ]


def spectra_kernel(
    per, seg, samples, ways, rows_hbm, count_hbm, valid_hbm, traces_hbm, table_hbm, factors_hbm,
    *refs,
):
    mine_ref, *outs, rows_ref, count_ref, valid_ref, traces, table, factors, sems = refs
    lines = per * seg
    pairs = [
        (traces_hbm, traces), (table_hbm, table), (factors_hbm, factors),
        (rows_hbm, rows_ref), (count_hbm, count_ref), (valid_hbm, valid_ref),
    ]
    copies = [pltpu.make_async_copy(src, dst, sems.at[i]) for i, (src, dst) in enumerate(pairs)]
    for copy in copies:
        copy.start()

    odd = lax.rem(lax.axis_index("tile"), 2)
    col = iota((STEP, STEP), 0)
    row = iota((STEP, STEP), 1)

    def bin_of(lane):
        tail = lane & (HALF - 1)
        known = (lane < LANE) | (tail < TAIL)
        return known, jnp.where(lane < LANE, lane, LANE + tail)

    known_in, bin_in = bin_of(col)
    known_out, bin_out = bin_of(row)
    near_bins = jnp.abs(bin_in - bin_out) <= 4
    window = jnp.where(known_in & known_out, jnp.where(near_bins, 17.0, 1.0), 0.0).astype(BF16)

    target = iota((lines, lines), 0)
    source = iota((lines, lines), 1)
    part, slot = divided(target, per)
    for copy in copies[-3:]:
        copy.wait()

    def choice(station):
        return jnp.where(source == station * seg + part, 1.0, 0.0).astype(BF16)

    def listed(direction):
        station = jnp.full((lines, lines), -seg, jnp.int32)
        for j in range(per):
            live = j < count_ref[0, direction]
            pick = jnp.where(live, rows_ref[0, direction, j], -seg)
            station = jnp.where(slot == j, pick, station)
        return choice(station)

    picks = jnp.concatenate([choice(slot), listed(odd), listed(1 - odd)], axis=0)

    usable = jnp.concatenate(column_of(valid_ref[...].astype(F32)), axis=0)

    for copy in copies[:3]:
        copy.wait()
    stretches = factors.shape[1]
    left = []
    for j in range(stretches):
        at = j * STEP
        x = traces[:, at : min(at + STEP, samples)]
        if at + STEP > samples:
            x = jnp.concatenate([x, jnp.zeros((lines, at + STEP - samples), F32)], axis=1)
        x = x * factors[0, j : j + 1, :STEP]
        x_high = x.astype(BF16)
        x_low = (x - x_high.astype(F32)).astype(BF16)
        left.append(jnp.concatenate([x_high, x_low, x_high], axis=1))
    parts = jnp.dot(jnp.concatenate(left, axis=0), table[...], preferred_element_type=F32)
    real, imag, tail = (parts[:lines, k * LANE : (k + 1) * LANE] for k in range(3))
    for j in range(1, stretches):
        p_re, p_im, p_tail = (parts[j * lines : (j + 1) * lines, k * LANE : (k + 1) * LANE] for k in range(3))
        turn = factors[1, j : j + 1, :]
        swap = factors[2, j : j + 1, :]
        real = real + p_re * turn[:, :LANE] + p_im * swap[:, :LANE]
        imag = imag + p_im * turn[:, LANE : 2 * LANE] + p_re * swap[:, LANE : 2 * LANE]
        tail = tail + p_tail * turn[:, 2 * LANE :] + pltpu.roll(p_tail, HALF, 1) * swap[:, 2 * LANE :]

    power = jnp.concatenate([real * real + imag * imag, tail * tail], axis=1)
    p_high = power.astype(BF16)
    p_low = (power - p_high.astype(F32)).astype(BF16)
    level = jnp.dot(p_high, window, preferred_element_type=F32)
    level = level + jnp.dot(p_low, window, preferred_element_type=F32)
    factor = usable / jnp.sqrt(level * (1.0 / (2 * NBIN)) + 1e-06)
    tail = tail * factor[:, LANE:]
    tail = jnp.where(iota((lines, LANE), 1) == VALID, usable, tail)
    white = jnp.concatenate([real * factor[:, :LANE], imag * factor[:, :LANE], tail], axis=1)
    chosen = jnp.dot(picks, white.astype(BF16), preferred_element_type=F32).astype(BF16)
    mine_ref[...] = chosen[:lines]
    for ref, way in zip(outs, ways):
        ref[...] = chosen[way * lines : (way + 1) * lines]


def stacked(per, lines, spread, ref):
    sums = [[None] * 4 for _ in range(per)]

    def add(s, i, value):
        sums[s][i] = value if sums[s][i] is None else sums[s][i] + value

    for at in range(0, lines, 16):
        both = ref[at : at + 16, :].astype(F32)
        for half in range(2):
            one = both[8 * half : 8 * half + 8]
            c_re, c_im, c_tail = one[:, :LANE], one[:, LANE : 2 * LANE], one[:, 2 * LANE :]
            c_turn = pltpu.roll(c_tail, HALF, 1)
            for s in range(per):
                here = s * lines + at + 8 * half
                left = spread[here : here + 8, :]
                l_re, l_im, l_tail = left[:, :LANE], left[:, LANE : 2 * LANE], left[:, 2 * LANE :]
                add(s, 0, l_re * c_re + l_im * c_im)
                add(s, 1, l_im * c_re - l_re * c_im)
                add(s, 2, l_tail * c_tail)
                add(s, 3, l_tail * c_turn)
    low_lanes = iota((8, LANE), 1) < HALF
    out = []
    for s in range(per):
        straight, turned = sums[s][2], sums[s][3]
        straight = straight + pltpu.roll(straight, HALF, 1)
        turned = turned - pltpu.roll(turned, HALF, 1)
        all_lanes = [sums[s][0], sums[s][1], jnp.where(low_lanes, straight, turned)]
        out.append([v + pltpu.roll(v, 4, 0) for v in all_lanes])
    return out


def store_sums(per, ref, i, pieces):
    for s, sums in enumerate(pieces):
        at = (i * per + s) * 8
        for k in range(3):
            ref[at : at + 8, k * LANE : (k + 1) * LANE] = sums[k]


def load_sums(per, ref, i):
    rows = [ref[(i * per + s) * 8 : (i * per + s) * 8 + 8, :] for s in range(per)]
    return [[row[:, k * LANE : (k + 1) * LANE] for k in range(3)] for row in rows]


def ready_kernel(per, seg, mask_hbm, basis_hbm, mine_ref, mask_ref, basis_ref, spread_ref, sums_ref, sems):
    copies = [
        pltpu.make_async_copy(basis_hbm, basis_ref, sems.at[0]),
        pltpu.make_async_copy(mask_hbm, mask_ref, sems.at[1]),
    ]
    for copy in copies:
        copy.start()
    lines = per * seg
    part, _ = divided(iota((lines, lines), 0), per)
    source = iota((lines, lines), 1)
    pick = [jnp.where(source == part * per + s, 1.0, 0.0).astype(BF16) for s in range(per)]
    spread_ref[...] = jnp.dot(jnp.concatenate(pick, axis=0), mine_ref[...], preferred_element_type=F32)
    store_sums(per, sums_ref, 0, stacked(per, lines, spread_ref, mine_ref))
    for copy in copies:
        copy.wait()


def early_kernel(per, seg, spread_ref, *refs):
    for i, ref in enumerate(refs[:-1]):
        store_sums(per, refs[-1], i, stacked(per, per * seg, spread_ref, ref))


def lags_kernel(per, seg, grps, tiles, order, *refs):
    mask_ref, basis_ref, spread_ref, mine_ref, early_ref = refs[:5]
    out_ref, cross, result, sems = refs[-4:]
    lines = per * seg
    columns = 3 * grps * per
    tile = lax.axis_index("tile")
    grp = lax.axis_index("grp")
    odd = lax.rem(tile, 2)
    inside = jnp.where(odd == 1, tile < tiles - 1, tile > 0)

    def by_place(pieces):
        places = []
        for g in range(grps):
            value = pieces[0]
            for d in range(1, grps):
                here = lax.rem(grp + (grps - d), grps) == g
                value = [[jnp.where(here, p, v) for p, v in zip(ps, vs)] for ps, vs in zip(pieces[d], value)]
            places.append(value)
        return places

    soon, names = order
    sums = {(0, 0): load_sums(per, mine_ref, 0)}
    for i, name in enumerate(names):
        if i < soon:
            sums[name] = load_sums(per, early_ref, i)
        else:
            sums[name] = stacked(per, lines, spread_ref, refs[5 + i - soon])
    own, near, far = (by_place([sums[way, d] for d in range(grps)]) for way in range(3))
    upper = iota((8, LANE), 0) < 4
    for s in range(per):
        slots = []
        for g in range(grps):
            n = near[g][s]
            f = [jnp.where(inside, v, 0.0) for v in far[g][s]]
            below = [jnp.where(odd == 1, a, b) for a, b in zip(n, f)]
            above = [jnp.where(odd == 1, b, a) for a, b in zip(n, f)]
            slots += [own[g][s], below, above]
        for i in range(0, len(slots), 2):
            rows = [jnp.where(upper, a, b) for a, b in zip(slots[i], slots[i + 1])]
            count = jnp.maximum(rows[2][:, VALID : VALID + 1], 1.0)
            at = s * columns + 4 * i
            for j in range(3):
                cross[at : at + 8, j * LANE : (j + 1) * LANE] = rows[j] / count

    keep = jnp.concatenate(column_of(mask_ref[...].astype(F32)), axis=0)
    left = (cross[...] * keep).astype(BF16)
    left = jnp.concatenate([left, left], axis=1)
    copies = []
    for i, lo in enumerate(range(0, LAGS, LAG_STEP)):
        hi = min(lo + LAG_STEP, LAGS)
        series = jnp.dot(left, basis_ref[:, lo:hi], preferred_element_type=F32).astype(BF16)
        for s in range(per):
            result[s, :, lo:hi] = series[s * columns : (s + 1) * columns]
        here = (slice(None), slice(None), slice(lo, hi))
        copies.append(pltpu.make_async_copy(result.at[here], out_ref.at[here], sems.at[i]))
        copies[-1].start()
    for copy in copies:
        copy.wait()


def solution(mesh):
    tiles, grps = mesh.shape["tile"], mesh.shape["grp"]
    axes = ("tile", "grp")
    vmem = pl.BlockSpec(memory_space=pltpu.VMEM)
    hbm = pl.BlockSpec(memory_space=pltpu.HBM)
    placed = pltpu.with_memory_space_constraint

    def exchange(array, way, by):
        pairs = []
        for t in range(tiles):
            to = (t, t ^ 1, ((t + 1) ^ 1) - 1)[way]
            for g in range(grps):
                if 0 <= to < tiles:
                    goal = to * grps + (g + by) % grps
                else:
                    goal = t * grps + (g + max(by, 1)) % grps
                pairs.append((t * grps + g, goal))
        return lax.ppermute(array, axes, pairs)

    def on_device(traces, validity, boundary_rows, boundary_count, pair_mask):
        per, seg, samples = traces.shape
        lines = per * seg
        columns = pair_mask.shape[1]
        table, factors = map(jnp.asarray, fourier_tables(samples))
        lag_basis = jnp.asarray(lag_table(samples))
        payload = pltpu.VMEM((lines, WIDE), BF16)
        names = [(2, d) for d in reversed(range(grps))]
        names += [(1, d) for d in range(1, grps)] + [(0, d) for d in range(1, grps)] + [(1, 0)]
        soon = [name for name in names if name not in LAST]
        late = [name for name in names if name in LAST]
        inputs = [boundary_rows, boundary_count, validity, traces.reshape(lines, samples), table, factors]
        mine, *rest = pl.pallas_call(
            lambda *refs: spectra_kernel(per, seg, samples, [way for way, _ in names], *refs),
            out_shape=(payload,) * (1 + len(names)),
            in_specs=[hbm] * len(inputs),
            out_specs=(vmem,) * (1 + len(names)),
            scratch_shapes=[
                pltpu.SMEM(boundary_rows.shape, jnp.int32),
                pltpu.SMEM(boundary_count.shape, jnp.int32),
                pltpu.VMEM(validity.shape, jnp.int32),
                pltpu.VMEM((lines, samples), F32),
                pltpu.VMEM(table.shape, BF16),
                pltpu.VMEM(factors.shape, F32),
                pltpu.SemaphoreType.DMA((6,)),
            ],
            compiler_params=pltpu.CompilerParams(vmem_limit_bytes=32 << 20),
            name="spectra",
        )(*[placed(x, pltpu.HBM) for x in inputs])
        came = {name: exchange(array, *name) for name, array in zip(names, rest)}
        mask, basis, spread, first = pl.pallas_call(
            lambda *refs: ready_kernel(per, seg, *refs),
            out_shape=(
                pltpu.VMEM(pair_mask.shape, jnp.int32),
                pltpu.VMEM(lag_basis.shape, BF16),
                pltpu.VMEM((per * lines, WIDE), F32),
                pltpu.VMEM((per * 8, WIDE), F32),
            ),
            in_specs=[hbm, hbm, vmem],
            out_specs=(vmem,) * 4,
            scratch_shapes=[pltpu.SemaphoreType.DMA((2,))],
            compiler_params=pltpu.CompilerParams(vmem_limit_bytes=32 << 20),
            name="ready",
        )(placed(pair_mask, pltpu.HBM), placed(lag_basis, pltpu.HBM), placed(mine, pltpu.VMEM))
        inputs = [placed(x, pltpu.VMEM) for x in (spread, *(came[name] for name in soon))]
        early = pl.pallas_call(
            lambda *refs: early_kernel(per, seg, *refs),
            out_shape=pltpu.VMEM((len(soon) * per * 8, WIDE), F32),
            in_specs=[vmem] * len(inputs),
            out_specs=vmem,
            compiler_params=pltpu.CompilerParams(vmem_limit_bytes=32 << 20),
            name="early",
        )(*inputs)
        order = len(soon), soon + late
        inputs = [mask, basis, spread, first, early, *(came[name] for name in late)]
        return pl.pallas_call(
            lambda *refs: lags_kernel(per, seg, grps, tiles, order, *refs),
            out_shape=jax.ShapeDtypeStruct((per, columns, LAGS), BF16),
            in_specs=[vmem] * len(inputs),
            out_specs=hbm,
            scratch_shapes=[
                pltpu.VMEM((per * columns, WIDE), F32),
                pltpu.VMEM((per, columns, LAGS), BF16),
                pltpu.SemaphoreType.DMA((pl.cdiv(LAGS, LAG_STEP),)),
            ],
            compiler_params=pltpu.CompilerParams(vmem_limit_bytes=32 << 20),
            name="lags",
        )(*[placed(x, pltpu.VMEM) for x in inputs])

    return jax.shard_map(
        on_device,
        mesh=mesh,
        in_specs=(P(axes, None, None), P(axes, None), P(axes, None, None), P(axes, None), P(axes, None)),
        out_specs=P(axes, None, None),
        check_vma=False,
    )
```

```python
import numpy as np
import ml_dtypes

import jax
import jax.numpy as jnp
from jax import lax
from jax.experimental import pallas as pl
from jax.experimental.pallas import tpu as pltpu
from jax.sharding import PartitionSpec as P

NBIN = 144
MAXLAG = 1000
LAGS = 2001
LANE = 128
TAIL = NBIN - LANE
HALF = 64
LAST = ((0, 1), (1, 0))
VALID = 16
WIDE = 3 * LANE
LAG_STEP = 4 * LANE
STEP = 2 * LANE
F32 = jnp.float32
BF16 = jnp.bfloat16


def split(table):
    high = table.astype(ml_dtypes.bfloat16)
    low = (table - high.astype(np.float64)).astype(ml_dtypes.bfloat16)
    return high, low


def in_lanes(real, imag):
    out = np.zeros((real.shape[0], WIDE))
    out[:, :LANE] = real[:, :LANE]
    out[:, LANE : 2 * LANE] = imag[:, :LANE]
    out[:, 2 * LANE : 2 * LANE + TAIL] = real[:, LANE:]
    out[:, 2 * LANE + HALF : 2 * LANE + HALF + TAIL] = imag[:, LANE:]
    return out


def fourier_tables(samples):
    bins = np.arange(1, NBIN + 1)
    turn = np.pi / samples
    angle = np.mod(np.arange(STEP)[:, None] * bins[None, :], 2 * samples) * turn
    high, low = split(in_lanes(np.cos(angle), -np.sin(angle)))
    stretches = -(-samples // STEP)
    angle = np.mod(np.arange(stretches)[:, None] * STEP * bins[None, :], 2 * samples) * turn
    turns = np.stack([in_lanes(np.cos(angle), np.cos(angle)), in_lanes(np.sin(angle), -np.sin(angle))])
    number = np.arange(stretches * STEP)
    taper = np.where(number < samples, 0.5 - 0.5 * np.cos(number * (2.0 * np.pi / samples)), 0.0)
    rows = np.concatenate([taper.reshape(stretches, STEP), np.zeros((stretches, WIDE - STEP))], axis=1)
    factors = np.concatenate([rows[None], turns]).astype(np.float32)
    return np.concatenate([high, high, low]), factors


def lag_table(samples):
    lags = np.arange(LAGS) - MAXLAG
    bins = np.arange(1, NBIN + 1)
    angle = np.mod(lags[:, None] * bins[None, :], 2 * samples) * (np.pi / samples)
    scale = 1.0 / np.sqrt(NBIN)
    return in_lanes(scale * np.cos(angle), -scale * np.sin(angle)).T.astype(ml_dtypes.bfloat16)


def iota(shape, dim):
    return lax.broadcasted_iota(jnp.int32, shape, dim)


def divided(value, by):
    if by & (by - 1) == 0:
        return value >> (by.bit_length() - 1), value & (by - 1)
    return lax.div(value, by), lax.rem(value, by)


def column_of(rows):
    n, m = rows.shape
    diagonal = iota((m, m), 0) == iota((m, m), 1)
    return [
        jnp.sum(jnp.where(diagonal, jnp.broadcast_to(rows[i : i + 1], (m, m)), 0.0), axis=1, keepdims=True)
        for i in range(n)
    ]


def spectra_kernel(
    per, seg, samples, ways, rows_hbm, count_hbm, valid_hbm, traces_hbm, table_hbm, factors_hbm,
    *refs,
):
    mine_ref, *outs, rows_ref, count_ref, valid_ref, traces, table, factors, sems = refs
    lines = per * seg
    pairs = [
        (traces_hbm, traces), (table_hbm, table), (factors_hbm, factors),
        (rows_hbm, rows_ref), (count_hbm, count_ref), (valid_hbm, valid_ref),
    ]
    copies = [pltpu.make_async_copy(src, dst, sems.at[i]) for i, (src, dst) in enumerate(pairs)]
    for copy in copies:
        copy.start()

    odd = lax.rem(lax.axis_index("tile"), 2)
    col = iota((STEP, STEP), 0)
    row = iota((STEP, STEP), 1)

    def bin_of(lane):
        tail = lane & (HALF - 1)
        known = (lane < LANE) | (tail < TAIL)
        return known, jnp.where(lane < LANE, lane, LANE + tail)

    known_in, bin_in = bin_of(col)
    known_out, bin_out = bin_of(row)
    near_bins = jnp.abs(bin_in - bin_out) <= 4
    window = jnp.where(known_in & known_out, jnp.where(near_bins, 17.0, 1.0), 0.0).astype(BF16)

    target = iota((lines, lines), 0)
    source = iota((lines, lines), 1)
    part, slot = divided(target, per)
    for copy in copies[-3:]:
        copy.wait()

    def choice(station):
        return jnp.where(source == station * seg + part, 1.0, 0.0).astype(BF16)

    def listed(direction):
        station = jnp.full((lines, lines), -seg, jnp.int32)
        for j in range(per):
            live = j < count_ref[0, direction]
            pick = jnp.where(live, rows_ref[0, direction, j], -seg)
            station = jnp.where(slot == j, pick, station)
        return choice(station)

    picks = jnp.concatenate([choice(slot), listed(odd), listed(1 - odd)], axis=0)

    usable = jnp.concatenate(column_of(valid_ref[...].astype(F32)), axis=0)

    for copy in copies[:3]:
        copy.wait()
    stretches = factors.shape[1]
    left = []
    for j in range(stretches):
        at = j * STEP
        x = traces[:, at : min(at + STEP, samples)]
        if at + STEP > samples:
            x = jnp.concatenate([x, jnp.zeros((lines, at + STEP - samples), F32)], axis=1)
        x = x * factors[0, j : j + 1, :STEP]
        x_high = x.astype(BF16)
        x_low = (x - x_high.astype(F32)).astype(BF16)
        left.append(jnp.concatenate([x_high, x_low, x_high], axis=1))
    parts = jnp.dot(jnp.concatenate(left, axis=0), table[...], preferred_element_type=F32)
    real, imag, tail = (parts[:lines, k * LANE : (k + 1) * LANE] for k in range(3))
    for j in range(1, stretches):
        p_re, p_im, p_tail = (parts[j * lines : (j + 1) * lines, k * LANE : (k + 1) * LANE] for k in range(3))
        turn = factors[1, j : j + 1, :]
        swap = factors[2, j : j + 1, :]
        real = real + p_re * turn[:, :LANE] + p_im * swap[:, :LANE]
        imag = imag + p_im * turn[:, LANE : 2 * LANE] + p_re * swap[:, LANE : 2 * LANE]
        tail = tail + p_tail * turn[:, 2 * LANE :] + pltpu.roll(p_tail, HALF, 1) * swap[:, 2 * LANE :]

    power = jnp.concatenate([real * real + imag * imag, tail * tail], axis=1)
    p_high = power.astype(BF16)
    p_low = (power - p_high.astype(F32)).astype(BF16)
    level = jnp.dot(p_high, window, preferred_element_type=F32)
    level = level + jnp.dot(p_low, window, preferred_element_type=F32)
    factor = usable / jnp.sqrt(level * (1.0 / (2 * NBIN)) + 1e-06)
    tail = tail * factor[:, LANE:]
    tail = jnp.where(iota((lines, LANE), 1) == VALID, usable, tail)
    white = jnp.concatenate([real * factor[:, :LANE], imag * factor[:, :LANE], tail], axis=1)
    chosen = jnp.dot(picks, white.astype(BF16), preferred_element_type=F32).astype(BF16)
    mine_ref[...] = chosen[:lines]
    for ref, way in zip(outs, ways):
        ref[...] = chosen[way * lines : (way + 1) * lines]


def stacked(per, lines, spread, ref):
    sums = [[None] * 4 for _ in range(per)]

    def add(s, i, value):
        sums[s][i] = value if sums[s][i] is None else sums[s][i] + value

    for at in range(0, lines, 16):
        both = ref[at : at + 16, :].astype(F32)
        for half in range(2):
            one = both[8 * half : 8 * half + 8]
            c_re, c_im, c_tail = one[:, :LANE], one[:, LANE : 2 * LANE], one[:, 2 * LANE :]
            c_turn = pltpu.roll(c_tail, HALF, 1)
            for s in range(per):
                here = s * lines + at + 8 * half
                left = spread[here : here + 8, :]
                l_re, l_im, l_tail = left[:, :LANE], left[:, LANE : 2 * LANE], left[:, 2 * LANE :]
                add(s, 0, l_re * c_re + l_im * c_im)
                add(s, 1, l_im * c_re - l_re * c_im)
                add(s, 2, l_tail * c_tail)
                add(s, 3, l_tail * c_turn)
    low_lanes = iota((8, LANE), 1) < HALF
    out = []
    for s in range(per):
        straight, turned = sums[s][2], sums[s][3]
        straight = straight + pltpu.roll(straight, HALF, 1)
        turned = turned - pltpu.roll(turned, HALF, 1)
        all_lanes = [sums[s][0], sums[s][1], jnp.where(low_lanes, straight, turned)]
        out.append([v + pltpu.roll(v, 4, 0) for v in all_lanes])
    return out


def store_sums(per, ref, i, pieces):
    for s, sums in enumerate(pieces):
        at = (i * per + s) * 8
        for k in range(3):
            ref[at : at + 8, k * LANE : (k + 1) * LANE] = sums[k]


def load_sums(per, ref, i):
    rows = [ref[(i * per + s) * 8 : (i * per + s) * 8 + 8, :] for s in range(per)]
    return [[row[:, k * LANE : (k + 1) * LANE] for k in range(3)] for row in rows]


def ready_kernel(per, seg, mask_hbm, basis_hbm, mine_ref, basis_ref, keep_ref, spread_ref, sums_ref, mask_ref, sems):
    copies = [
        pltpu.make_async_copy(mask_hbm, mask_ref, sems.at[0]),
        pltpu.make_async_copy(basis_hbm, basis_ref, sems.at[1]),
    ]
    for copy in copies:
        copy.start()
    lines = per * seg
    part, _ = divided(iota((lines, lines), 0), per)
    source = iota((lines, lines), 1)
    pick = [jnp.where(source == part * per + s, 1.0, 0.0).astype(BF16) for s in range(per)]
    spread_ref[...] = jnp.dot(jnp.concatenate(pick, axis=0), mine_ref[...], preferred_element_type=F32)
    store_sums(per, sums_ref, 0, stacked(per, lines, spread_ref, mine_ref))
    copies[0].wait()
    keep = jnp.concatenate(column_of(mask_ref[...].astype(F32)), axis=0)
    keep_ref[...] = jnp.broadcast_to(keep, keep_ref.shape)
    copies[1].wait()


def place_of(name, grps, tiles):
    way, by = name
    tile = lax.axis_index("tile")
    odd = lax.rem(tile, 2)
    source = lax.rem(lax.axis_index("grp") + (grps - by), grps)
    kind = (0, 2 - odd, 1 + odd)[way]
    there = jnp.where(odd == 1, tile < tiles - 1, tile > 0) if way == 2 else None
    return 3 * source + kind, there


def over_count(rows):
    scale = 1.0 / jnp.maximum(rows[2][:, VALID : VALID + 1], 1.0)
    return jnp.concatenate([row * scale for row in rows], axis=1).astype(BF16)


def early_kernel(per, seg, grps, tiles, names, basis_ref, spread_ref, mine_ref, *refs):
    series_ref, left = refs[-2:]
    sums = [load_sums(per, mine_ref, 0)]
    sums += [stacked(per, per * seg, spread_ref, ref) for ref in refs[:-2]]
    places = [place_of(name, grps, tiles) for name in ((0, 0), *names)]
    half = iota((8, LANE), 0) >> 2
    blocks = 3 * grps // 2
    for b in range(blocks):
        fits = []
        for place, there in places:
            fit = (half + 2 * b) == place
            fits.append(fit if there is None else fit & there)
        for s in range(per):
            rows = [jnp.zeros((8, LANE), F32)] * 3
            for fit, piece in zip(fits, sums):
                rows = [jnp.where(fit, new, row) for new, row in zip(piece[s], rows)]
            at = (s * blocks + b) * 8
            scale = 1.0 / jnp.maximum(rows[2][:, VALID : VALID + 1], 1.0)
            for k in range(3):
                left[at : at + 8, k * LANE : (k + 1) * LANE] = rows[k] * scale
    series_ref[...] = jnp.dot(left[...].astype(BF16), basis_ref[...], preferred_element_type=F32)


def lags_kernel(per, seg, grps, tiles, names, basis_ref, keep_ref, spread_ref, series_ref, *refs):
    out_ref, result, sems = refs[-3:]
    left = []
    for ref in refs[:-3]:
        left += [over_count(rows) for rows in stacked(per, per * seg, spread_ref, ref)]
    left = jnp.concatenate(left, axis=0)
    places = [place_of(name, grps, tiles) for name in names]
    blocks = 3 * grps // 2
    copies = []
    for i, lo in enumerate(range(0, LAGS, LAG_STEP)):
        hi = min(lo + LAG_STEP, LAGS)
        late = jnp.dot(left, basis_ref[:, lo:hi], preferred_element_type=F32)
        half = iota((8, hi - lo), 0) >> 2
        for s in range(per):
            rows = []
            for b in range(blocks):
                at = (s * blocks + b) * 8
                row = series_ref[at : at + 8, lo:hi]
                for p, (place, there) in enumerate(places):
                    fit = (half + 2 * b) == place
                    fit = fit if there is None else fit & there
                    row = jnp.where(fit, late[(p * per + s) * 8 : (p * per + s) * 8 + 8], row)
                rows.append(row * keep_ref[at : at + 8, :1])
            result[s, :, lo:hi] = jnp.concatenate(rows, axis=0).astype(BF16)
        here = (slice(None), slice(None), slice(lo, hi))
        copies.append(pltpu.make_async_copy(result.at[here], out_ref.at[here], sems.at[i]))
        copies[-1].start()
    for copy in copies:
        copy.wait()


def solution(mesh):
    tiles, grps = mesh.shape["tile"], mesh.shape["grp"]
    axes = ("tile", "grp")
    vmem = pl.BlockSpec(memory_space=pltpu.VMEM)
    hbm = pl.BlockSpec(memory_space=pltpu.HBM)
    placed = pltpu.with_memory_space_constraint

    def exchange(array, way, by):
        pairs = []
        for t in range(tiles):
            to = (t, t ^ 1, ((t + 1) ^ 1) - 1)[way]
            for g in range(grps):
                if 0 <= to < tiles:
                    goal = to * grps + (g + by) % grps
                else:
                    goal = t * grps + (g + max(by, 1)) % grps
                pairs.append((t * grps + g, goal))
        return lax.ppermute(array, axes, pairs)

    def on_device(traces, validity, boundary_rows, boundary_count, pair_mask):
        per, seg, samples = traces.shape
        lines = per * seg
        columns = pair_mask.shape[1]
        table, factors = map(jnp.asarray, fourier_tables(samples))
        lag_basis = jnp.asarray(lag_table(samples))
        payload = pltpu.VMEM((lines, WIDE), BF16)
        names = [(2, d) for d in reversed(range(grps))]
        names += [(1, d) for d in range(1, grps)] + [(0, d) for d in range(1, grps)] + [(1, 0)]
        soon = [name for name in names if name not in LAST]
        late = [name for name in names if name in LAST]
        inputs = [boundary_rows, boundary_count, validity, traces.reshape(lines, samples), table, factors]
        mine, *rest = pl.pallas_call(
            lambda *refs: spectra_kernel(per, seg, samples, [way for way, _ in names], *refs),
            out_shape=(payload,) * (1 + len(names)),
            in_specs=[hbm] * len(inputs),
            out_specs=(vmem,) * (1 + len(names)),
            scratch_shapes=[
                pltpu.SMEM(boundary_rows.shape, jnp.int32),
                pltpu.SMEM(boundary_count.shape, jnp.int32),
                pltpu.VMEM(validity.shape, jnp.int32),
                pltpu.VMEM((lines, samples), F32),
                pltpu.VMEM(table.shape, BF16),
                pltpu.VMEM(factors.shape, F32),
                pltpu.SemaphoreType.DMA((6,)),
            ],
            compiler_params=pltpu.CompilerParams(vmem_limit_bytes=32 << 20),
            name="spectra",
        )(*[placed(x, pltpu.HBM) for x in inputs])
        came = {name: exchange(array, *name) for name, array in zip(names, rest)}
        rows = per * columns
        basis, keep, spread, first = pl.pallas_call(
            lambda *refs: ready_kernel(per, seg, *refs),
            out_shape=(
                pltpu.VMEM(lag_basis.shape, BF16),
                pltpu.VMEM((rows, LANE), F32),
                pltpu.VMEM((per * lines, WIDE), F32),
                pltpu.VMEM((per * 8, WIDE), F32),
            ),
            in_specs=[hbm, hbm, vmem],
            out_specs=(vmem,) * 4,
            scratch_shapes=[pltpu.VMEM(pair_mask.shape, jnp.int32), pltpu.SemaphoreType.DMA((2,))],
            compiler_params=pltpu.CompilerParams(vmem_limit_bytes=32 << 20),
            name="ready",
        )(placed(pair_mask, pltpu.HBM), placed(lag_basis, pltpu.HBM), placed(mine, pltpu.VMEM))
        inputs = [placed(x, pltpu.VMEM) for x in (basis, spread, first, *(came[name] for name in soon))]
        series = pl.pallas_call(
            lambda *refs: early_kernel(per, seg, grps, tiles, soon, *refs),
            out_shape=pltpu.VMEM((rows, LAGS), F32),
            in_specs=[vmem] * len(inputs),
            out_specs=vmem,
            scratch_shapes=[pltpu.VMEM((rows, WIDE), F32)],
            compiler_params=pltpu.CompilerParams(vmem_limit_bytes=32 << 20),
            name="early",
        )(*inputs)
        inputs = [placed(x, pltpu.VMEM) for x in (basis, keep, spread, series, *(came[name] for name in late))]
        return pl.pallas_call(
            lambda *refs: lags_kernel(per, seg, grps, tiles, late, *refs),
            out_shape=jax.ShapeDtypeStruct((per, columns, LAGS), BF16),
            in_specs=[vmem] * len(inputs),
            out_specs=hbm,
            scratch_shapes=[
                pltpu.VMEM((per, columns, LAGS), BF16),
                pltpu.SemaphoreType.DMA((pl.cdiv(LAGS, LAG_STEP),)),
            ],
            compiler_params=pltpu.CompilerParams(vmem_limit_bytes=32 << 20),
            name="lags",
        )(*inputs)

    return jax.shard_map(
        on_device,
        mesh=mesh,
        in_specs=(P(axes, None, None), P(axes, None), P(axes, None, None), P(axes, None), P(axes, None)),
        out_specs=P(axes, None, None),
        check_vma=False,
    )
```

```python
import numpy as np
import ml_dtypes

import jax
import jax.numpy as jnp
from jax import lax
from jax.experimental import pallas as pl
from jax.experimental.pallas import tpu as pltpu
from jax.sharding import PartitionSpec as P

NBIN = 144
MAXLAG = 1000
LAGS = 2001
LANE = 128
TAIL = NBIN - LANE
HALF = 64
LAST = ((0, 1), (1, 0))
VALID = 16
WIDE = 3 * LANE
LAG_STEP = 4 * LANE
STEP = 2 * LANE
FINE = 16
F32 = jnp.float32
BF16 = jnp.bfloat16


def split(table):
    high = table.astype(ml_dtypes.bfloat16)
    low = (table - high.astype(np.float64)).astype(ml_dtypes.bfloat16)
    return high, low


def in_lanes(real, imag):
    out = np.zeros((real.shape[0], WIDE))
    out[:, :LANE] = real[:, :LANE]
    out[:, LANE : 2 * LANE] = imag[:, :LANE]
    out[:, 2 * LANE : 2 * LANE + TAIL] = real[:, LANE:]
    out[:, 2 * LANE + HALF : 2 * LANE + HALF + TAIL] = imag[:, LANE:]
    return out


def fourier_tables(samples):
    bins = np.arange(1, NBIN + 1)
    turn = np.pi / samples
    stretches = -(-samples // STEP)

    def angles(number):
        return np.mod(number[:, None] * bins[None, :], 2 * samples) * turn

    whole = angles(np.arange(stretches) * STEP)
    coarse = angles(np.arange(STEP // FINE) * FINE)
    fine = angles(np.arange(FINE))
    number = np.arange(stretches * STEP)
    taper = np.where(number < samples, 0.5 - 0.5 * np.cos(number * (2.0 * np.pi / samples)), 0.0)
    parts = [
        in_lanes(np.cos(whole), np.cos(whole)),
        in_lanes(np.sin(whole), -np.sin(whole)),
        np.pad(taper.reshape(stretches, STEP), ((0, 0), (0, WIDE - STEP))),
        in_lanes(np.cos(coarse), -np.sin(coarse)),
        in_lanes(-np.sin(coarse), -np.cos(coarse)),
        in_lanes(np.cos(fine), np.cos(fine)),
        in_lanes(np.sin(fine), np.sin(fine)),
    ]
    starts, rows = [], 0
    for i, part in enumerate(parts):
        parts[i] = np.pad(part, ((0, -len(part) % 8), (0, 0)))
        starts.append(rows)
        rows += len(parts[i])
    return np.concatenate(parts).astype(np.float32), starts, stretches


def lag_table(samples):
    lags = np.arange(LAGS) - MAXLAG
    bins = np.arange(1, NBIN + 1)
    angle = np.mod(lags[:, None] * bins[None, :], 2 * samples) * (np.pi / samples)
    scale = 1.0 / np.sqrt(NBIN)
    high, low = split(in_lanes(scale * np.cos(angle), -scale * np.sin(angle)).T)
    lane = np.arange(LANE)
    tail = np.where(holds_tail(lane)[:, None], high[2 * LANE :], low[LANE : 2 * LANE])
    return np.concatenate([high[: 2 * LANE], tail])


def holds_tail(lane):
    return ((lane & (HALF - 1)) < TAIL) | (lane == VALID)


def packed(real, imag, tail):
    return jnp.concatenate([real, imag, jnp.where(holds_tail(iota(tail.shape, 1)), tail, imag)], axis=1)


def iota(shape, dim):
    return lax.broadcasted_iota(jnp.int32, shape, dim)


def divided(value, by):
    if by & (by - 1) == 0:
        return value >> (by.bit_length() - 1), value & (by - 1)
    return lax.div(value, by), lax.rem(value, by)


def column_of(rows):
    n, m = rows.shape
    diagonal = iota((m, m), 0) == iota((m, m), 1)
    return [
        jnp.sum(jnp.where(diagonal, jnp.broadcast_to(rows[i : i + 1], (m, m)), 0.0), axis=1, keepdims=True)
        for i in range(n)
    ]


def spectra_kernel(
    per, seg, samples, ways, starts, stretches, rows_hbm, count_hbm, valid_hbm, traces_hbm, factors_hbm,
    *refs,
):
    mine_ref, *outs, rows_ref, count_ref, valid_ref, traces, factors, white_ref, order_ref, sems = refs
    lines = per * seg
    pairs = [
        (factors_hbm, factors), (traces_hbm, traces),
        (rows_hbm, rows_ref), (count_hbm, count_ref), (valid_hbm, valid_ref),
    ]
    copies = [pltpu.make_async_copy(src, dst, sems.at[i]) for i, (src, dst) in enumerate(pairs)]
    for copy in copies:
        copy.start()

    odd = lax.rem(lax.axis_index("tile"), 2)
    col = iota((STEP, STEP), 0)
    row = iota((STEP, STEP), 1)

    def bin_of(lane):
        tail = lane & (HALF - 1)
        known = (lane < LANE) | (tail < TAIL)
        return known, jnp.where(lane < LANE, lane, LANE + tail)

    known_in, bin_in = bin_of(col)
    known_out, bin_out = bin_of(row)
    near_bins = jnp.abs(bin_in - bin_out) <= 4
    window = jnp.where(known_in & known_out, jnp.where(near_bins, 17.0, 1.0), 0.0).astype(BF16)

    for copy in copies[2:]:
        copy.wait()
    usable = jnp.concatenate(column_of(valid_ref[...].astype(F32)), axis=0)

    copies[0].wait()
    turn_at, swap_at, taper_at, coarse_at, cross_at, fine_at, other_at = starts
    fine, other = factors[fine_at : fine_at + FINE, :], factors[other_at : other_at + FINE, :]
    high, low = [], []
    for i in range(STEP // FINE):
        rows = factors[coarse_at + i : coarse_at + i + 1, :] * fine
        rows = rows + factors[cross_at + i : cross_at + i + 1, :] * other
        high.append(rows.astype(BF16))
        low.append((rows - high[-1].astype(F32)).astype(BF16))
    table = jnp.concatenate([*high, *high, *low], axis=0)

    copies[1].wait()
    left = []
    for j in range(stretches):
        at = j * STEP
        x = traces[:, at : min(at + STEP, samples)]
        if at + STEP > samples:
            x = jnp.concatenate([x, jnp.zeros((lines, at + STEP - samples), F32)], axis=1)
        x = x * factors[taper_at + j : taper_at + j + 1, :STEP]
        x_high = x.astype(BF16)
        x_low = (x - x_high.astype(F32)).astype(BF16)
        left.append(jnp.concatenate([x_high, x_low, x_high], axis=1))
    parts = jnp.dot(jnp.concatenate(left, axis=0), table, preferred_element_type=F32)
    real, imag, tail = (parts[:lines, k * LANE : (k + 1) * LANE] for k in range(3))
    for j in range(1, stretches):
        p_re, p_im, p_tail = (parts[j * lines : (j + 1) * lines, k * LANE : (k + 1) * LANE] for k in range(3))
        turn = factors[turn_at + j : turn_at + j + 1, :]
        swap = factors[swap_at + j : swap_at + j + 1, :]
        real = real + p_re * turn[:, :LANE] + p_im * swap[:, :LANE]
        imag = imag + p_im * turn[:, LANE : 2 * LANE] + p_re * swap[:, LANE : 2 * LANE]
        tail = tail + p_tail * turn[:, 2 * LANE :] + pltpu.roll(p_tail, HALF, 1) * swap[:, 2 * LANE :]

    power = jnp.concatenate([real * real + imag * imag, tail * tail], axis=1)
    p_high = power.astype(BF16)
    p_low = (power - p_high.astype(F32)).astype(BF16)
    level = jnp.dot(p_high, window, preferred_element_type=F32)
    level = level + jnp.dot(p_low, window, preferred_element_type=F32)
    factor = usable / jnp.sqrt(level * (1.0 / (2 * NBIN)) + 1e-06)
    tail = tail * factor[:, LANE:]
    tail = jnp.where(iota((lines, LANE), 1) == VALID, usable, tail)
    white = jnp.concatenate([real * factor[:, :LANE], imag * factor[:, :LANE], tail], axis=1)
    white_ref[...] = white.reshape(per, seg, WIDE)

    def ordered(direction):
        for j in range(per):
            if direction is None:
                rows = white_ref[j]
            else:
                rows = white_ref[rows_ref[0, direction, j]]
                rows = jnp.where(j < count_ref[0, direction], rows, 0.0)
            for k in range(3):
                order_ref[k, pl.ds(j, seg, stride=per), :] = rows[:, k * LANE : (k + 1) * LANE]
        return jnp.concatenate([order_ref[k] for k in range(3)], axis=1).astype(BF16)

    own, near, far = ordered(None), ordered(odd), ordered(1 - odd)
    mine_ref[...] = own
    for ref, way in zip(outs, ways):
        ref[...] = (own, near, far)[way]


def stacked(per, lines, spread, ref):
    sums = [[None] * 4 for _ in range(per)]

    def add(s, i, value):
        sums[s][i] = value if sums[s][i] is None else sums[s][i] + value

    for at in range(0, lines, 16):
        both = ref[at : at + 16, :].astype(F32)
        for half in range(2):
            one = both[8 * half : 8 * half + 8]
            c_re, c_im, c_tail = one[:, :LANE], one[:, LANE : 2 * LANE], one[:, 2 * LANE :]
            c_turn = pltpu.roll(c_tail, HALF, 1)
            for s in range(per):
                here = s * lines + at + 8 * half
                left = spread[here : here + 8, :]
                l_re, l_im, l_tail = left[:, :LANE], left[:, LANE : 2 * LANE], left[:, 2 * LANE :]
                add(s, 0, l_re * c_re + l_im * c_im)
                add(s, 1, l_im * c_re - l_re * c_im)
                add(s, 2, l_tail * c_tail)
                add(s, 3, l_tail * c_turn)
    low_lanes = iota((8, LANE), 1) < HALF
    out = []
    for s in range(per):
        straight, turned = sums[s][2], sums[s][3]
        straight = straight + pltpu.roll(straight, HALF, 1)
        turned = turned - pltpu.roll(turned, HALF, 1)
        all_lanes = [sums[s][0], sums[s][1], jnp.where(low_lanes, straight, turned)]
        out.append([v + pltpu.roll(v, 4, 0) for v in all_lanes])
    return out


def store_sums(per, ref, i, pieces):
    for s, sums in enumerate(pieces):
        at = (i * per + s) * 8
        for k in range(3):
            ref[at : at + 8, k * LANE : (k + 1) * LANE] = sums[k]


def load_sums(per, ref, i):
    rows = [ref[(i * per + s) * 8 : (i * per + s) * 8 + 8, :] for s in range(per)]
    return [[row[:, k * LANE : (k + 1) * LANE] for k in range(3)] for row in rows]


def ready_kernel(per, seg, mask_hbm, basis_hbm, mine_ref, basis_ref, keep_ref, spread_ref, sums_ref, mask_ref, sems):
    copies = [
        pltpu.make_async_copy(mask_hbm, mask_ref, sems.at[0]),
        pltpu.make_async_copy(basis_hbm, basis_ref, sems.at[1]),
    ]
    for copy in copies:
        copy.start()
    lines = per * seg
    part, _ = divided(iota((lines, lines), 0), per)
    source = iota((lines, lines), 1)
    pick = [jnp.where(source == part * per + s, 1.0, 0.0).astype(BF16) for s in range(per)]
    spread_ref[...] = jnp.dot(jnp.concatenate(pick, axis=0), mine_ref[...], preferred_element_type=F32)
    store_sums(per, sums_ref, 0, stacked(per, lines, spread_ref, mine_ref))
    copies[0].wait()
    keep = jnp.concatenate(column_of(mask_ref[...].astype(F32)), axis=0)
    keep_ref[...] = jnp.broadcast_to(keep, keep_ref.shape)
    copies[1].wait()


def place_of(name, grps, tiles):
    way, by = name
    tile = lax.axis_index("tile")
    odd = lax.rem(tile, 2)
    source = lax.rem(lax.axis_index("grp") + (grps - by), grps)
    kind = (0, 2 - odd, 1 + odd)[way]
    there = jnp.where(odd == 1, tile < tiles - 1, tile > 0) if way == 2 else None
    return 3 * source + kind, there


def over_count(rows):
    scale = 1.0 / jnp.maximum(rows[2][:, VALID : VALID + 1], 1.0)
    return packed(*(row * scale for row in rows)).astype(BF16)


def early_kernel(per, seg, grps, tiles, names, basis_ref, spread_ref, mine_ref, *refs):
    series_ref = refs[-1]
    sums = [load_sums(per, mine_ref, 0)]
    sums += [stacked(per, per * seg, spread_ref, ref) for ref in refs[:-1]]
    places = [place_of(name, grps, tiles) for name in ((0, 0), *names)]
    half = iota((8, LANE), 0) >> 2
    blocks = 3 * grps // 2
    left = [None] * (per * blocks)
    for b in range(blocks):
        fits = []
        for place, there in places:
            fit = (half + 2 * b) == place
            fits.append(fit if there is None else fit & there)
        for s in range(per):
            rows = [jnp.zeros((8, LANE), F32)] * 3
            for fit, piece in zip(fits, sums):
                rows = [jnp.where(fit, new, row) for new, row in zip(piece[s], rows)]
            at = (s * blocks + b) * 8
            left[at // 8] = over_count(rows)
    series_ref[...] = jnp.dot(jnp.concatenate(left, axis=0), basis_ref[...], preferred_element_type=F32)


def lags_kernel(per, seg, grps, tiles, names, basis_ref, keep_ref, spread_ref, series_ref, *refs):
    out_ref, result, sems = refs[-3:]
    left = []
    for ref in refs[:-3]:
        left += [over_count(rows) for rows in stacked(per, per * seg, spread_ref, ref)]
    left = jnp.concatenate(left, axis=0)
    places = [place_of(name, grps, tiles) for name in names]
    blocks = 3 * grps // 2
    copies = []
    for i, lo in enumerate(range(0, LAGS, LAG_STEP)):
        hi = min(lo + LAG_STEP, LAGS)
        late = jnp.dot(left, basis_ref[:, lo:hi], preferred_element_type=F32)
        half = iota((8, hi - lo), 0) >> 2
        for s in range(per):
            rows = []
            for b in range(blocks):
                at = (s * blocks + b) * 8
                row = series_ref[at : at + 8, lo:hi]
                for p, (place, there) in enumerate(places):
                    fit = (half + 2 * b) == place
                    fit = fit if there is None else fit & there
                    row = jnp.where(fit, late[(p * per + s) * 8 : (p * per + s) * 8 + 8], row)
                rows.append(row * keep_ref[at : at + 8, :1])
            result[s, :, lo:hi] = jnp.concatenate(rows, axis=0).astype(BF16)
        here = (slice(None), slice(None), slice(lo, hi))
        copies.append(pltpu.make_async_copy(result.at[here], out_ref.at[here], sems.at[i]))
        copies[-1].start()
    for copy in copies:
        copy.wait()


def solution(mesh):
    tiles, grps = mesh.shape["tile"], mesh.shape["grp"]
    axes = ("tile", "grp")
    vmem = pl.BlockSpec(memory_space=pltpu.VMEM)
    hbm = pl.BlockSpec(memory_space=pltpu.HBM)
    placed = pltpu.with_memory_space_constraint

    def exchange(array, way, by):
        pairs = []
        for t in range(tiles):
            to = (t, t ^ 1, ((t + 1) ^ 1) - 1)[way]
            for g in range(grps):
                if 0 <= to < tiles:
                    goal = to * grps + (g + by) % grps
                else:
                    goal = t * grps + (g + max(by, 1)) % grps
                pairs.append((t * grps + g, goal))
        return lax.ppermute(array, axes, pairs)

    def on_device(traces, validity, boundary_rows, boundary_count, pair_mask):
        per, seg, samples = traces.shape
        lines = per * seg
        columns = pair_mask.shape[1]
        factors, starts, stretches = fourier_tables(samples)
        lag_basis = jnp.asarray(lag_table(samples))
        payload = pltpu.VMEM((lines, WIDE), BF16)
        names = [(2, d) for d in reversed(range(grps))]
        names += [(1, d) for d in range(1, grps)] + [(0, d) for d in range(1, grps)] + [(1, 0)]
        soon = [name for name in names if name not in LAST]
        late = [name for name in names if name in LAST]
        inputs = [boundary_rows, boundary_count, validity, traces.reshape(lines, samples), jnp.asarray(factors)]
        mine, *rest = pl.pallas_call(
            lambda *refs: spectra_kernel(
                per, seg, samples, [way for way, _ in names], starts, stretches, *refs
            ),
            out_shape=(payload,) * (1 + len(names)),
            in_specs=[hbm] * len(inputs),
            out_specs=(vmem,) * (1 + len(names)),
            scratch_shapes=[
                pltpu.SMEM(boundary_rows.shape, jnp.int32),
                pltpu.SMEM(boundary_count.shape, jnp.int32),
                pltpu.VMEM(validity.shape, jnp.int32),
                pltpu.VMEM((lines, samples), F32),
                pltpu.VMEM(factors.shape, F32),
                pltpu.VMEM((per, seg, WIDE), F32),
                pltpu.VMEM((3, lines, LANE), F32),
                pltpu.SemaphoreType.DMA((5,)),
            ],
            compiler_params=pltpu.CompilerParams(vmem_limit_bytes=32 << 20),
            name="spectra",
        )(*[placed(x, pltpu.HBM) for x in inputs])
        came = {name: exchange(array, *name) for name, array in zip(names, rest)}
        rows = per * columns
        basis, keep, spread, first = pl.pallas_call(
            lambda *refs: ready_kernel(per, seg, *refs),
            out_shape=(
                pltpu.VMEM(lag_basis.shape, BF16),
                pltpu.VMEM((rows, LANE), F32),
                pltpu.VMEM((per * lines, WIDE), F32),
                pltpu.VMEM((per * 8, WIDE), F32),
            ),
            in_specs=[hbm, hbm, vmem],
            out_specs=(vmem,) * 4,
            scratch_shapes=[pltpu.VMEM(pair_mask.shape, jnp.int32), pltpu.SemaphoreType.DMA((2,))],
            compiler_params=pltpu.CompilerParams(vmem_limit_bytes=32 << 20),
            name="ready",
        )(placed(pair_mask, pltpu.HBM), placed(lag_basis, pltpu.HBM), placed(mine, pltpu.VMEM))
        inputs = [placed(x, pltpu.VMEM) for x in (basis, spread, first, *(came[name] for name in soon))]
        series = pl.pallas_call(
            lambda *refs: early_kernel(per, seg, grps, tiles, soon, *refs),
            out_shape=pltpu.VMEM((rows, LAGS), F32),
            in_specs=[vmem] * len(inputs),
            out_specs=vmem,
            compiler_params=pltpu.CompilerParams(vmem_limit_bytes=32 << 20),
            name="early",
        )(*inputs)
        inputs = [placed(x, pltpu.VMEM) for x in (basis, keep, spread, series, *(came[name] for name in late))]
        return pl.pallas_call(
            lambda *refs: lags_kernel(per, seg, grps, tiles, late, *refs),
            out_shape=jax.ShapeDtypeStruct((per, columns, LAGS), BF16),
            in_specs=[vmem] * len(inputs),
            out_specs=hbm,
            scratch_shapes=[
                pltpu.VMEM((per, columns, LAGS), BF16),
                pltpu.SemaphoreType.DMA((pl.cdiv(LAGS, LAG_STEP),)),
            ],
            compiler_params=pltpu.CompilerParams(vmem_limit_bytes=32 << 20),
            name="lags",
        )(*inputs)

    return jax.shard_map(
        on_device,
        mesh=mesh,
        in_specs=(P(axes, None, None), P(axes, None), P(axes, None, None), P(axes, None), P(axes, None)),
        out_specs=P(axes, None, None),
        check_vma=False,
    )
```

```python
import numpy as np
import ml_dtypes

import jax
import jax.numpy as jnp
from jax import lax
from jax.experimental import pallas as pl
from jax.experimental.pallas import tpu as pltpu
from jax.sharding import PartitionSpec as P

NBIN = 144
MAXLAG = 1000
LAGS = 2001
LANE = 128
TAIL = NBIN - LANE
HALF = 64
LAST = ((0, 1), (1, 0))
VALID = 16
WIDE = 3 * LANE
LAG_STEP = 4 * LANE
STEP = 2 * LANE
FINE = 16
F32 = jnp.float32
BF16 = jnp.bfloat16


def split(table):
    high = table.astype(ml_dtypes.bfloat16)
    low = (table - high.astype(np.float64)).astype(ml_dtypes.bfloat16)
    return high, low


def in_lanes(real, imag):
    out = np.zeros((real.shape[0], WIDE))
    out[:, :LANE] = real[:, :LANE]
    out[:, LANE : 2 * LANE] = imag[:, :LANE]
    out[:, 2 * LANE : 2 * LANE + TAIL] = real[:, LANE:]
    out[:, 2 * LANE + HALF : 2 * LANE + HALF + TAIL] = imag[:, LANE:]
    return out


def fourier_tables(samples):
    bins = np.arange(1, NBIN + 1)
    turn = np.pi / samples
    stretches = -(-samples // STEP)

    def angles(number):
        return np.mod(number[:, None] * bins[None, :], 2 * samples) * turn

    whole = angles(np.arange(stretches) * STEP)
    coarse = angles(np.arange(STEP // FINE) * FINE)
    fine = angles(np.arange(FINE))
    number = np.arange(stretches * STEP)
    taper = np.where(number < samples, 0.5 - 0.5 * np.cos(number * (2.0 * np.pi / samples)), 0.0)
    parts = [
        in_lanes(np.cos(whole), np.cos(whole)),
        in_lanes(np.sin(whole), -np.sin(whole)),
        np.pad(taper.reshape(stretches, STEP), ((0, 0), (0, WIDE - STEP))),
        in_lanes(np.cos(coarse), -np.sin(coarse)),
        in_lanes(-np.sin(coarse), -np.cos(coarse)),
        in_lanes(np.cos(fine), np.cos(fine)),
        in_lanes(np.sin(fine), np.sin(fine)),
    ]
    starts, rows = [], 0
    for i, part in enumerate(parts):
        parts[i] = np.pad(part, ((0, -len(part) % 8), (0, 0)))
        starts.append(rows)
        rows += len(parts[i])
    return np.concatenate(parts).astype(np.float32), starts, stretches


def lag_table(samples):
    lags = np.arange(LAGS) - MAXLAG
    bins = np.arange(1, NBIN + 1)
    angle = np.mod(lags[:, None] * bins[None, :], 2 * samples) * (np.pi / samples)
    scale = 1.0 / np.sqrt(NBIN)
    high, low = split(in_lanes(scale * np.cos(angle), -scale * np.sin(angle)).T)
    lane = np.arange(LANE)
    tail = np.where(holds_tail(lane)[:, None], high[2 * LANE :], low[LANE : 2 * LANE])
    return np.concatenate([high[: 2 * LANE], tail])


def holds_tail(lane):
    return ((lane & (HALF - 1)) < TAIL) | (lane == VALID)


def packed(real, imag, tail):
    return jnp.concatenate([real, imag, jnp.where(holds_tail(iota(tail.shape, 1)), tail, imag)], axis=1)


def iota(shape, dim):
    return lax.broadcasted_iota(jnp.int32, shape, dim)


def divided(value, by):
    if by & (by - 1) == 0:
        return value >> (by.bit_length() - 1), value & (by - 1)
    return lax.div(value, by), lax.rem(value, by)


def column_of(rows):
    n, m = rows.shape
    diagonal = iota((m, m), 0) == iota((m, m), 1)
    return [
        jnp.sum(jnp.where(diagonal, jnp.broadcast_to(rows[i : i + 1], (m, m)), 0.0), axis=1, keepdims=True)
        for i in range(n)
    ]


def spectra_kernel(
    per, seg, samples, ways, starts, stretches, rows_hbm, count_hbm, valid_hbm, traces_hbm, factors_hbm,
    *refs,
):
    mine_ref, *outs, rows_ref, count_ref, valid_ref, traces, factors, white_ref, order_ref, sems = refs
    lines = per * seg
    pairs = [
        (factors_hbm, factors), (traces_hbm, traces),
        (rows_hbm, rows_ref), (count_hbm, count_ref), (valid_hbm, valid_ref),
    ]
    copies = [pltpu.make_async_copy(src, dst, sems.at[i]) for i, (src, dst) in enumerate(pairs)]
    for copy in copies:
        copy.start()

    odd = lax.rem(lax.axis_index("tile"), 2)
    col = iota((STEP, STEP), 0)
    row = iota((STEP, STEP), 1)

    def bin_of(lane):
        tail = lane & (HALF - 1)
        known = (lane < LANE) | (tail < TAIL)
        return known, jnp.where(lane < LANE, lane, LANE + tail)

    known_in, bin_in = bin_of(col)
    known_out, bin_out = bin_of(row)
    near_bins = jnp.abs(bin_in - bin_out) <= 4
    window = jnp.where(known_in & known_out, jnp.where(near_bins, 17.0, 1.0), 0.0).astype(BF16)

    for copy in copies[2:]:
        copy.wait()
    usable = jnp.concatenate(column_of(valid_ref[...].astype(F32)), axis=0)

    copies[0].wait()
    turn_at, swap_at, taper_at, coarse_at, cross_at, fine_at, other_at = starts
    fine, other = factors[fine_at : fine_at + FINE, :], factors[other_at : other_at + FINE, :]
    high, low = [], []
    for i in range(STEP // FINE):
        rows = factors[coarse_at + i : coarse_at + i + 1, :] * fine
        rows = rows + factors[cross_at + i : cross_at + i + 1, :] * other
        high.append(rows.astype(BF16))
        low.append((rows - high[-1].astype(F32)).astype(BF16))
    table = jnp.concatenate([*high, *high, *low], axis=0)

    copies[1].wait()
    left = []
    for j in range(stretches):
        at = j * STEP
        x = traces[:, at : min(at + STEP, samples)]
        if at + STEP > samples:
            x = jnp.concatenate([x, jnp.zeros((lines, at + STEP - samples), F32)], axis=1)
        x = x * factors[taper_at + j : taper_at + j + 1, :STEP]
        x_high = x.astype(BF16)
        x_low = (x - x_high.astype(F32)).astype(BF16)
        left.append(jnp.concatenate([x_high, x_low, x_high], axis=1))
    parts = jnp.dot(jnp.concatenate(left, axis=0), table, preferred_element_type=F32)
    real, imag, tail = (parts[:lines, k * LANE : (k + 1) * LANE] for k in range(3))
    for j in range(1, stretches):
        p_re, p_im, p_tail = (parts[j * lines : (j + 1) * lines, k * LANE : (k + 1) * LANE] for k in range(3))
        turn = factors[turn_at + j : turn_at + j + 1, :]
        swap = factors[swap_at + j : swap_at + j + 1, :]
        real = real + p_re * turn[:, :LANE] + p_im * swap[:, :LANE]
        imag = imag + p_im * turn[:, LANE : 2 * LANE] + p_re * swap[:, LANE : 2 * LANE]
        tail = tail + p_tail * turn[:, 2 * LANE :] + pltpu.roll(p_tail, HALF, 1) * swap[:, 2 * LANE :]

    power = jnp.concatenate([real * real + imag * imag, tail * tail], axis=1)
    p_high = power.astype(BF16)
    p_low = (power - p_high.astype(F32)).astype(BF16)
    level = jnp.dot(p_high, window, preferred_element_type=F32)
    level = level + jnp.dot(p_low, window, preferred_element_type=F32)
    factor = usable / jnp.sqrt(level * (1.0 / (2 * NBIN)) + 1e-06)
    tail = tail * factor[:, LANE:]
    tail = jnp.where(iota((lines, LANE), 1) == VALID, usable, tail)
    white = jnp.concatenate([real * factor[:, :LANE], imag * factor[:, :LANE], tail], axis=1)
    white_ref[...] = white.reshape(per, seg, WIDE)

    def ordered(direction):
        for j in range(per):
            if direction is None:
                rows = white_ref[j]
            else:
                rows = white_ref[rows_ref[0, direction, j]]
                rows = jnp.where(j < count_ref[0, direction], rows, 0.0)
            for k in range(3):
                order_ref[k, pl.ds(j, seg, stride=per), :] = rows[:, k * LANE : (k + 1) * LANE]
        return jnp.concatenate([order_ref[k] for k in range(3)], axis=1).astype(BF16)

    own, near, far = ordered(None), ordered(odd), ordered(1 - odd)
    mine_ref[...] = own
    for ref, way in zip(outs, ways):
        ref[...] = (own, near, far, jnp.concatenate([own, near], axis=0))[way]


def stacked(per, lines, spread, ref):
    sums = [[None] * 4 for _ in range(per)]

    def add(s, i, value):
        sums[s][i] = value if sums[s][i] is None else sums[s][i] + value

    for at in range(0, lines, 16):
        both = ref[at : at + 16, :].astype(F32)
        for half in range(2):
            one = both[8 * half : 8 * half + 8]
            c_re, c_im, c_tail = one[:, :LANE], one[:, LANE : 2 * LANE], one[:, 2 * LANE :]
            c_turn = pltpu.roll(c_tail, HALF, 1)
            for s in range(per):
                here = s * lines + at + 8 * half
                left = spread[here : here + 8, :]
                l_re, l_im, l_tail = left[:, :LANE], left[:, LANE : 2 * LANE], left[:, 2 * LANE :]
                add(s, 0, l_re * c_re + l_im * c_im)
                add(s, 1, l_im * c_re - l_re * c_im)
                add(s, 2, l_tail * c_tail)
                add(s, 3, l_tail * c_turn)
    low_lanes = iota((8, LANE), 1) < HALF
    out = []
    for s in range(per):
        straight, turned = sums[s][2], sums[s][3]
        straight = straight + pltpu.roll(straight, HALF, 1)
        turned = turned - pltpu.roll(turned, HALF, 1)
        all_lanes = [sums[s][0], sums[s][1], jnp.where(low_lanes, straight, turned)]
        out.append([v + pltpu.roll(v, 4, 0) for v in all_lanes])
    return out


def store_sums(per, ref, i, pieces):
    for s, sums in enumerate(pieces):
        at = (i * per + s) * 8
        for k in range(3):
            ref[at : at + 8, k * LANE : (k + 1) * LANE] = sums[k]


def load_sums(per, ref, i):
    rows = [ref[(i * per + s) * 8 : (i * per + s) * 8 + 8, :] for s in range(per)]
    return [[row[:, k * LANE : (k + 1) * LANE] for k in range(3)] for row in rows]


def ready_kernel(per, seg, mask_hbm, basis_hbm, mine_ref, basis_ref, keep_ref, spread_ref, sums_ref, mask_ref, sems):
    copies = [
        pltpu.make_async_copy(mask_hbm, mask_ref, sems.at[0]),
        pltpu.make_async_copy(basis_hbm, basis_ref, sems.at[1]),
    ]
    for copy in copies:
        copy.start()
    lines = per * seg
    part, _ = divided(iota((lines, lines), 0), per)
    source = iota((lines, lines), 1)
    pick = [jnp.where(source == part * per + s, 1.0, 0.0).astype(BF16) for s in range(per)]
    spread_ref[...] = jnp.dot(jnp.concatenate(pick, axis=0), mine_ref[...], preferred_element_type=F32)
    store_sums(per, sums_ref, 0, stacked(per, lines, spread_ref, mine_ref))
    copies[0].wait()
    keep = jnp.concatenate(column_of(mask_ref[...].astype(F32)), axis=0)
    keep_ref[...] = jnp.broadcast_to(keep, keep_ref.shape)
    copies[1].wait()


def pass_kernel(lines, *refs):
    half = len(refs) // 2
    for src, dst in zip(refs[:half], refs[half:]):
        dst[...] = src[lines:, :]


def place_of(name, grps, tiles):
    way, by = name
    tile = lax.axis_index("tile")
    odd = lax.rem(tile, 2)
    source = lax.rem(lax.axis_index("grp") + (grps - by), grps)
    kind = (0, 2 - odd, 1 + odd)[way]
    there = jnp.where(odd == 1, tile < tiles - 1, tile > 0) if way == 2 else None
    return 3 * source + kind, there


def over_count(rows):
    scale = 1.0 / jnp.maximum(rows[2][:, VALID : VALID + 1], 1.0)
    return packed(*(row * scale for row in rows)).astype(BF16)


def early_kernel(per, seg, grps, tiles, names, basis_ref, spread_ref, mine_ref, *refs):
    series_ref = refs[-1]
    sums = [load_sums(per, mine_ref, 0)]
    sums += [stacked(per, per * seg, spread_ref, ref) for ref in refs[:-1]]
    places = [place_of(name, grps, tiles) for name in ((0, 0), *names)]
    half = iota((8, LANE), 0) >> 2
    blocks = 3 * grps // 2
    left = [None] * (per * blocks)
    for b in range(blocks):
        fits = []
        for place, there in places:
            fit = (half + 2 * b) == place
            fits.append(fit if there is None else fit & there)
        for s in range(per):
            rows = [jnp.zeros((8, LANE), F32)] * 3
            for fit, piece in zip(fits, sums):
                rows = [jnp.where(fit, new, row) for new, row in zip(piece[s], rows)]
            at = (s * blocks + b) * 8
            left[at // 8] = over_count(rows)
    series_ref[...] = jnp.dot(jnp.concatenate(left, axis=0), basis_ref[...], preferred_element_type=F32)


def lags_kernel(per, seg, grps, tiles, names, basis_ref, keep_ref, spread_ref, series_ref, *refs):
    out_ref, result, sems = refs[-3:]
    left = []
    for ref in refs[:-3]:
        left += [over_count(rows) for rows in stacked(per, per * seg, spread_ref, ref)]
    left = jnp.concatenate(left, axis=0)
    places = [place_of(name, grps, tiles) for name in names]
    blocks = 3 * grps // 2
    copies = []
    for i, lo in enumerate(range(0, LAGS, LAG_STEP)):
        hi = min(lo + LAG_STEP, LAGS)
        late = jnp.dot(left, basis_ref[:, lo:hi], preferred_element_type=F32)
        half = iota((8, hi - lo), 0) >> 2
        for s in range(per):
            rows = []
            for b in range(blocks):
                at = (s * blocks + b) * 8
                row = series_ref[at : at + 8, lo:hi]
                for p, (place, there) in enumerate(places):
                    fit = (half + 2 * b) == place
                    fit = fit if there is None else fit & there
                    row = jnp.where(fit, late[(p * per + s) * 8 : (p * per + s) * 8 + 8], row)
                rows.append(row * keep_ref[at : at + 8, :1])
            result[s, :, lo:hi] = jnp.concatenate(rows, axis=0).astype(BF16)
        here = (slice(None), slice(None), slice(lo, hi))
        copies.append(pltpu.make_async_copy(result.at[here], out_ref.at[here], sems.at[i]))
        copies[-1].start()
    for copy in copies:
        copy.wait()


def solution(mesh):
    tiles, grps = mesh.shape["tile"], mesh.shape["grp"]
    axes = ("tile", "grp")
    vmem = pl.BlockSpec(memory_space=pltpu.VMEM)
    hbm = pl.BlockSpec(memory_space=pltpu.HBM)
    placed = pltpu.with_memory_space_constraint

    def exchange(array, way, by):
        pairs = []
        for t in range(tiles):
            to = (t, t ^ 1, ((t + 1) ^ 1) - 1)[way]
            for g in range(grps):
                if 0 <= to < tiles:
                    goal = to * grps + (g + by) % grps
                else:
                    goal = t * grps + (g + max(by, 1)) % grps
                pairs.append((t * grps + g, goal))
        return lax.ppermute(array, axes, pairs)

    def on_device(traces, validity, boundary_rows, boundary_count, pair_mask):
        per, seg, samples = traces.shape
        lines = per * seg
        columns = pair_mask.shape[1]
        factors, starts, stretches = fourier_tables(samples)
        lag_basis = jnp.asarray(lag_table(samples))
        payload = pltpu.VMEM((lines, WIDE), BF16)
        sent = [(3, d) for d in range(1, grps)] + [(1, 0)] + [(2, d) for d in reversed(range(grps))]
        soon = [(0, d) for d in range(1, grps)] + [(1, 0)] + [(2, d) for d in range(1, grps)]
        late = [(2, 0)] + [(1, d) for d in range(1, grps)]
        inputs = [boundary_rows, boundary_count, validity, traces.reshape(lines, samples), jnp.asarray(factors)]
        mine, *rest = pl.pallas_call(
            lambda *refs: spectra_kernel(
                per, seg, samples, [way for way, _ in sent], starts, stretches, *refs
            ),
            out_shape=(payload,) + tuple(
                pltpu.VMEM(((1 + way // 3) * lines, WIDE), BF16) for way, _ in sent
            ),
            in_specs=[hbm] * len(inputs),
            out_specs=(vmem,) * (1 + len(sent)),
            scratch_shapes=[
                pltpu.SMEM(boundary_rows.shape, jnp.int32),
                pltpu.SMEM(boundary_count.shape, jnp.int32),
                pltpu.VMEM(validity.shape, jnp.int32),
                pltpu.VMEM((lines, samples), F32),
                pltpu.VMEM(factors.shape, F32),
                pltpu.VMEM((per, seg, WIDE), F32),
                pltpu.VMEM((3, lines, LANE), F32),
                pltpu.SemaphoreType.DMA((5,)),
            ],
            compiler_params=pltpu.CompilerParams(vmem_limit_bytes=32 << 20),
            name="spectra",
        )(*[placed(x, pltpu.HBM) for x in inputs])
        came = {(way, by): exchange(array, way % 3, by) for (way, by), array in zip(sent, rest)}
        rows = per * columns
        basis, keep, spread, first = pl.pallas_call(
            lambda *refs: ready_kernel(per, seg, *refs),
            out_shape=(
                pltpu.VMEM(lag_basis.shape, BF16),
                pltpu.VMEM((rows, LANE), F32),
                pltpu.VMEM((per * lines, WIDE), F32),
                pltpu.VMEM((per * 8, WIDE), F32),
            ),
            in_specs=[hbm, hbm, vmem],
            out_specs=(vmem,) * 4,
            scratch_shapes=[pltpu.VMEM(pair_mask.shape, jnp.int32), pltpu.SemaphoreType.DMA((2,))],
            compiler_params=pltpu.CompilerParams(vmem_limit_bytes=32 << 20),
            name="ready",
        )(placed(pair_mask, pltpu.HBM), placed(lag_basis, pltpu.HBM), placed(mine, pltpu.VMEM))
        both = [came[3, d] for d in range(1, grps)]
        for d in range(1, grps):
            came[0, d] = came[3, d]
        if both:
            passed = pl.pallas_call(
                lambda _, *refs: pass_kernel(lines, *refs),
                out_shape=(payload,) * len(both),
                in_specs=[vmem] * (1 + len(both)),
                out_specs=(vmem,) * len(both),
                name="pass",
            )(*[placed(x, pltpu.VMEM) for x in (first, *both)])
            for d, array in enumerate(passed):
                came[1, d + 1] = exchange(array, 1, 0)
        inputs = [placed(x, pltpu.VMEM) for x in (basis, spread, first, *(came[name] for name in soon))]
        series = pl.pallas_call(
            lambda *refs: early_kernel(per, seg, grps, tiles, soon, *refs),
            out_shape=pltpu.VMEM((rows, LAGS), F32),
            in_specs=[vmem] * len(inputs),
            out_specs=vmem,
            compiler_params=pltpu.CompilerParams(vmem_limit_bytes=32 << 20),
            name="early",
        )(*inputs)
        inputs = [placed(x, pltpu.VMEM) for x in (basis, keep, spread, series, *(came[name] for name in late))]
        return pl.pallas_call(
            lambda *refs: lags_kernel(per, seg, grps, tiles, late, *refs),
            out_shape=jax.ShapeDtypeStruct((per, columns, LAGS), BF16),
            in_specs=[vmem] * len(inputs),
            out_specs=hbm,
            scratch_shapes=[
                pltpu.VMEM((per, columns, LAGS), BF16),
                pltpu.SemaphoreType.DMA((pl.cdiv(LAGS, LAG_STEP),)),
            ],
            compiler_params=pltpu.CompilerParams(vmem_limit_bytes=32 << 20),
            name="lags",
        )(*inputs)

    return jax.shard_map(
        on_device,
        mesh=mesh,
        in_specs=(P(axes, None, None), P(axes, None), P(axes, None, None), P(axes, None), P(axes, None)),
        out_specs=P(axes, None, None),
        check_vma=False,
    )
```

```python
import numpy as np
import ml_dtypes

import jax
import jax.numpy as jnp
from jax import lax
from jax.experimental import pallas as pl
from jax.experimental.pallas import tpu as pltpu
from jax.sharding import PartitionSpec as P

NBIN = 144
MAXLAG = 1000
LAGS = 2001
LANE = 128
TAIL = NBIN - LANE
HALF = 64
LAST = ((0, 1), (1, 0))
VALID = 16
WIDE = 3 * LANE
LAG_STEP = 4 * LANE
STEP = 2 * LANE
FINE = 16
F32 = jnp.float32
BF16 = jnp.bfloat16


def split(table):
    high = table.astype(ml_dtypes.bfloat16)
    low = (table - high.astype(np.float64)).astype(ml_dtypes.bfloat16)
    return high, low


def in_lanes(real, imag):
    out = np.zeros((real.shape[0], WIDE))
    out[:, :LANE] = real[:, :LANE]
    out[:, LANE : 2 * LANE] = imag[:, :LANE]
    out[:, 2 * LANE : 2 * LANE + TAIL] = real[:, LANE:]
    out[:, 2 * LANE + HALF : 2 * LANE + HALF + TAIL] = imag[:, LANE:]
    return out


def fourier_tables(samples):
    bins = np.arange(1, NBIN + 1)
    turn = np.pi / samples
    stretches = -(-samples // STEP)

    def angles(number):
        return np.mod(number[:, None] * bins[None, :], 2 * samples) * turn

    whole = angles(np.arange(stretches) * STEP)
    coarse = angles(np.arange(STEP // FINE) * FINE)
    fine = angles(np.arange(FINE))
    number = np.arange(stretches * STEP)
    taper = np.where(number < samples, 0.5 - 0.5 * np.cos(number * (2.0 * np.pi / samples)), 0.0)
    parts = [
        in_lanes(np.cos(whole), np.cos(whole)),
        in_lanes(np.sin(whole), -np.sin(whole)),
        np.pad(taper.reshape(stretches, STEP), ((0, 0), (0, WIDE - STEP))),
        in_lanes(np.cos(coarse), -np.sin(coarse)),
        in_lanes(-np.sin(coarse), -np.cos(coarse)),
        in_lanes(np.cos(fine), np.cos(fine)),
        in_lanes(np.sin(fine), np.sin(fine)),
    ]
    starts, rows = [], 0
    for i, part in enumerate(parts):
        parts[i] = np.pad(part, ((0, -len(part) % 8), (0, 0)))
        starts.append(rows)
        rows += len(parts[i])
    return np.concatenate(parts).astype(np.float32), starts, stretches


def lag_table(samples):
    lags = np.arange(LAGS) - MAXLAG
    bins = np.arange(1, NBIN + 1)
    angle = np.mod(lags[:, None] * bins[None, :], 2 * samples) * (np.pi / samples)
    scale = 1.0 / np.sqrt(NBIN)
    high, low = split(in_lanes(scale * np.cos(angle), -scale * np.sin(angle)).T)
    lane = np.arange(LANE)
    tail = np.where(holds_tail(lane)[:, None], high[2 * LANE :], low[LANE : 2 * LANE])
    return np.concatenate([high[: 2 * LANE], tail])


def holds_tail(lane):
    return ((lane & (HALF - 1)) < TAIL) | (lane == VALID)


def packed(real, imag, tail):
    return jnp.concatenate([real, imag, jnp.where(holds_tail(iota(tail.shape, 1)), tail, imag)], axis=1)


def iota(shape, dim):
    return lax.broadcasted_iota(jnp.int32, shape, dim)


def divided(value, by):
    if by & (by - 1) == 0:
        return value >> (by.bit_length() - 1), value & (by - 1)
    return lax.div(value, by), lax.rem(value, by)


def column_of(rows):
    n, m = rows.shape
    diagonal = iota((m, m), 0) == iota((m, m), 1)
    return [
        jnp.sum(jnp.where(diagonal, jnp.broadcast_to(rows[i : i + 1], (m, m)), 0.0), axis=1, keepdims=True)
        for i in range(n)
    ]


def spectra_kernel(
    per, seg, samples, ways, starts, stretches, rows_hbm, count_hbm, valid_hbm, traces_hbm, factors_hbm, basis_hbm,
    *refs,
):
    mine_ref, *outs, basis_ref, rows_ref, count_ref, valid_ref, traces, factors, white_ref, order_ref, sems = refs
    lines = per * seg
    pairs = [
        (factors_hbm, factors), (traces_hbm, traces),
        (rows_hbm, rows_ref), (count_hbm, count_ref), (valid_hbm, valid_ref), (basis_hbm, basis_ref),
    ]
    copies = [pltpu.make_async_copy(src, dst, sems.at[i]) for i, (src, dst) in enumerate(pairs)]
    for copy in copies:
        copy.start()

    odd = lax.rem(lax.axis_index("tile"), 2)
    col = iota((STEP, STEP), 0)
    row = iota((STEP, STEP), 1)

    def bin_of(lane):
        tail = lane & (HALF - 1)
        known = (lane < LANE) | (tail < TAIL)
        return known, jnp.where(lane < LANE, lane, LANE + tail)

    known_in, bin_in = bin_of(col)
    known_out, bin_out = bin_of(row)
    near_bins = jnp.abs(bin_in - bin_out) <= 4
    window = jnp.where(known_in & known_out, jnp.where(near_bins, 17.0, 1.0), 0.0).astype(BF16)

    for copy in copies[2:5]:
        copy.wait()
    usable = jnp.concatenate(column_of(valid_ref[...].astype(F32)), axis=0)

    copies[0].wait()
    turn_at, swap_at, taper_at, coarse_at, cross_at, fine_at, other_at = starts
    fine, other = factors[fine_at : fine_at + FINE, :], factors[other_at : other_at + FINE, :]
    high, low = [], []
    for i in range(STEP // FINE):
        rows = factors[coarse_at + i : coarse_at + i + 1, :] * fine
        rows = rows + factors[cross_at + i : cross_at + i + 1, :] * other
        high.append(rows.astype(BF16))
        low.append((rows - high[-1].astype(F32)).astype(BF16))
    table = jnp.concatenate([*high, *high, *low], axis=0)

    copies[1].wait()
    left = []
    for j in range(stretches):
        at = j * STEP
        x = traces[:, at : min(at + STEP, samples)]
        if at + STEP > samples:
            x = jnp.concatenate([x, jnp.zeros((lines, at + STEP - samples), F32)], axis=1)
        x = x * factors[taper_at + j : taper_at + j + 1, :STEP]
        x_high = x.astype(BF16)
        x_low = (x - x_high.astype(F32)).astype(BF16)
        left.append(jnp.concatenate([x_high, x_low, x_high], axis=1))
    parts = jnp.dot(jnp.concatenate(left, axis=0), table, preferred_element_type=F32)
    real, imag, tail = (parts[:lines, k * LANE : (k + 1) * LANE] for k in range(3))
    for j in range(1, stretches):
        p_re, p_im, p_tail = (parts[j * lines : (j + 1) * lines, k * LANE : (k + 1) * LANE] for k in range(3))
        turn = factors[turn_at + j : turn_at + j + 1, :]
        swap = factors[swap_at + j : swap_at + j + 1, :]
        real = real + p_re * turn[:, :LANE] + p_im * swap[:, :LANE]
        imag = imag + p_im * turn[:, LANE : 2 * LANE] + p_re * swap[:, LANE : 2 * LANE]
        tail = tail + p_tail * turn[:, 2 * LANE :] + pltpu.roll(p_tail, HALF, 1) * swap[:, 2 * LANE :]

    power = jnp.concatenate([real * real + imag * imag, tail * tail], axis=1)
    p_high = power.astype(BF16)
    p_low = (power - p_high.astype(F32)).astype(BF16)
    level = jnp.dot(p_high, window, preferred_element_type=F32)
    level = level + jnp.dot(p_low, window, preferred_element_type=F32)
    factor = usable / jnp.sqrt(level * (1.0 / (2 * NBIN)) + 1e-06)
    tail = tail * factor[:, LANE:]
    tail = jnp.where(iota((lines, LANE), 1) == VALID, usable, tail)
    white = jnp.concatenate([real * factor[:, :LANE], imag * factor[:, :LANE], tail], axis=1)
    white_ref[...] = white.reshape(per, seg, WIDE)

    def ordered(direction):
        for j in range(per):
            if direction is None:
                rows = white_ref[j]
            else:
                rows = white_ref[rows_ref[0, direction, j]]
                rows = jnp.where(j < count_ref[0, direction], rows, 0.0)
            for k in range(3):
                order_ref[k, pl.ds(j, seg, stride=per), :] = rows[:, k * LANE : (k + 1) * LANE]
        return jnp.concatenate([order_ref[k] for k in range(3)], axis=1).astype(BF16)

    own, near, far = ordered(None), ordered(odd), ordered(1 - odd)
    mine_ref[...] = own
    for ref, way in zip(outs, ways):
        ref[...] = (own, near, far, jnp.concatenate([own, near], axis=0))[way]
    copies[5].wait()


def stacked(per, lines, spread, ref):
    sums = [[None] * 5 for _ in range(per)]

    def add(s, i, value):
        sums[s][i] = value if sums[s][i] is None else sums[s][i] + value

    for at in range(0, lines, 16):
        both = ref[at : at + 16, :].astype(F32)
        for half in range(2):
            one = both[8 * half : 8 * half + 8]
            c_re, c_im, c_tail = one[:, :LANE], one[:, LANE : 2 * LANE], one[:, 2 * LANE :]
            c_turn = pltpu.roll(c_tail, HALF, 1)
            c_valid = jnp.broadcast_to(c_tail[:, VALID : VALID + 1], c_tail.shape)
            for s in range(per):
                here = s * lines + at + 8 * half
                left = spread[here : here + 8, :]
                l_re, l_im, l_tail, l_valid = (left[:, k * LANE : (k + 1) * LANE] for k in range(4))
                add(s, 0, l_re * c_re + l_im * c_im)
                add(s, 1, l_im * c_re - l_re * c_im)
                add(s, 2, l_tail * c_tail)
                add(s, 3, l_tail * c_turn)
                add(s, 4, l_valid * c_valid)
    low_lanes = iota((8, LANE), 1) < HALF
    out = []
    for s in range(per):
        straight, turned = sums[s][2], sums[s][3]
        straight = straight + pltpu.roll(straight, HALF, 1)
        turned = turned - pltpu.roll(turned, HALF, 1)
        all_lanes = [sums[s][0], sums[s][1], jnp.where(low_lanes, straight, turned), sums[s][4]]
        out.append([v + pltpu.roll(v, 4, 0) for v in all_lanes])
    return out


def store_sums(per, ref, i, pieces):
    for s, sums in enumerate(pieces):
        at = (i * per + s) * 8
        for k in range(4):
            ref[at : at + 8, k * LANE : (k + 1) * LANE] = sums[k]


def load_sums(per, ref, i):
    rows = [ref[(i * per + s) * 8 : (i * per + s) * 8 + 8, :] for s in range(per)]
    return [[row[:, k * LANE : (k + 1) * LANE] for k in range(4)] for row in rows]


def ready_kernel(per, seg, mask_hbm, mine_ref, keep_ref, spread_ref, sums_ref, mask_ref, sems):
    copies = [
        pltpu.make_async_copy(mask_hbm, mask_ref, sems.at[0]),
    ]
    for copy in copies:
        copy.start()
    lines = per * seg
    part, _ = divided(iota((lines, lines), 0), per)
    source = iota((lines, lines), 1)
    pick = [jnp.where(source == part * per + s, 1.0, 0.0).astype(BF16) for s in range(per)]
    spread = jnp.dot(jnp.concatenate(pick, axis=0), mine_ref[...], preferred_element_type=F32)
    spread_ref[:, :WIDE] = spread
    valid = spread[:, 2 * LANE + VALID : 2 * LANE + VALID + 1]
    spread_ref[:, WIDE:] = jnp.broadcast_to(valid, (per * lines, LANE))
    store_sums(per, sums_ref, 0, stacked(per, lines, spread_ref, mine_ref))
    copies[0].wait()
    keep = jnp.concatenate(column_of(mask_ref[...].astype(F32)), axis=0)
    keep_ref[...] = jnp.broadcast_to(keep, keep_ref.shape)


def pass_kernel(lines, *refs):
    half = len(refs) // 2
    for src, dst in zip(refs[:half], refs[half:]):
        dst[...] = src[lines:, :]


def place_of(name, grps, tiles):
    way, by = name
    tile = lax.axis_index("tile")
    odd = lax.rem(tile, 2)
    source = lax.rem(lax.axis_index("grp") + (grps - by), grps)
    kind = (0, 2 - odd, 1 + odd)[way]
    there = jnp.where(odd == 1, tile < tiles - 1, tile > 0) if way == 2 else None
    return 3 * source + kind, there


def over_count(rows):
    scale = 1.0 / jnp.maximum(rows[3], 1.0)
    return packed(*(row * scale for row in rows[:3])).astype(BF16)


def early_kernel(per, seg, grps, tiles, names, basis_ref, spread_ref, mine_ref, *refs):
    series_ref = refs[-1]
    sums = [load_sums(per, mine_ref, 0)]
    sums += [stacked(per, per * seg, spread_ref, ref) for ref in refs[:-1]]
    places = [place_of(name, grps, tiles) for name in ((0, 0), *names)]
    half = iota((8, LANE), 0) >> 2
    blocks = 3 * grps // 2
    left = [None] * (per * blocks)
    for b in range(blocks):
        fits = []
        for place, there in places:
            fit = (half + 2 * b) == place
            fits.append(fit if there is None else fit & there)
        for s in range(per):
            rows = [jnp.zeros((8, LANE), F32)] * 4
            for fit, piece in zip(fits, sums):
                rows = [jnp.where(fit, new, row) for new, row in zip(piece[s], rows)]
            at = (s * blocks + b) * 8
            left[at // 8] = over_count(rows)
    series_ref[...] = jnp.dot(jnp.concatenate(left, axis=0), basis_ref[...], preferred_element_type=F32)


def lags_kernel(per, seg, grps, tiles, names, basis_ref, keep_ref, spread_ref, series_ref, *refs):
    out_ref, result, sems = refs[-3:]
    left = []
    for ref in refs[:-3]:
        left += [over_count(rows) for rows in stacked(per, per * seg, spread_ref, ref)]
    left = jnp.concatenate(left, axis=0)
    places = [place_of(name, grps, tiles) for name in names]
    blocks = 3 * grps // 2
    copies = []
    for i, lo in enumerate(range(0, LAGS, LAG_STEP)):
        hi = min(lo + LAG_STEP, LAGS)
        late = jnp.dot(left, basis_ref[:, lo:hi], preferred_element_type=F32)
        half = iota((8, hi - lo), 0) >> 2
        for s in range(per):
            rows = []
            for b in range(blocks):
                at = (s * blocks + b) * 8
                row = series_ref[at : at + 8, lo:hi]
                for p, (place, there) in enumerate(places):
                    fit = (half + 2 * b) == place
                    fit = fit if there is None else fit & there
                    row = jnp.where(fit, late[(p * per + s) * 8 : (p * per + s) * 8 + 8], row)
                rows.append(row * keep_ref[at : at + 8, :1])
            result[s, :, lo:hi] = jnp.concatenate(rows, axis=0).astype(BF16)
        here = (slice(None), slice(None), slice(lo, hi))
        copies.append(pltpu.make_async_copy(result.at[here], out_ref.at[here], sems.at[i]))
        copies[-1].start()
    for copy in copies:
        copy.wait()


def solution(mesh):
    tiles, grps = mesh.shape["tile"], mesh.shape["grp"]
    axes = ("tile", "grp")
    vmem = pl.BlockSpec(memory_space=pltpu.VMEM)
    hbm = pl.BlockSpec(memory_space=pltpu.HBM)
    placed = pltpu.with_memory_space_constraint

    def exchange(array, way, by):
        pairs = []
        for t in range(tiles):
            to = (t, t ^ 1, ((t + 1) ^ 1) - 1)[way]
            for g in range(grps):
                if 0 <= to < tiles:
                    goal = to * grps + (g + by) % grps
                else:
                    goal = t * grps + (g + max(by, 1)) % grps
                pairs.append((t * grps + g, goal))
        return lax.ppermute(array, axes, pairs)

    def on_device(traces, validity, boundary_rows, boundary_count, pair_mask):
        per, seg, samples = traces.shape
        lines = per * seg
        columns = pair_mask.shape[1]
        factors, starts, stretches = fourier_tables(samples)
        lag_basis = jnp.asarray(lag_table(samples))
        payload = pltpu.VMEM((lines, WIDE), BF16)
        sent = [(3, d) for d in range(1, grps)] + [(1, 0)] + [(2, d) for d in reversed(range(grps))]
        soon = [(0, d) for d in range(1, grps)] + [(1, 0)]
        late = [(2, d) for d in reversed(range(grps))] + [(1, d) for d in range(1, grps)]
        inputs = [boundary_rows, boundary_count, validity, traces.reshape(lines, samples), jnp.asarray(factors), lag_basis]
        mine, *rest, basis = pl.pallas_call(
            lambda *refs: spectra_kernel(
                per, seg, samples, [way for way, _ in sent], starts, stretches, *refs
            ),
            out_shape=(payload,) + tuple(
                pltpu.VMEM(((1 + way // 3) * lines, WIDE), BF16) for way, _ in sent
            ) + (pltpu.VMEM(lag_basis.shape, BF16),),
            in_specs=[hbm] * len(inputs),
            out_specs=(vmem,) * (2 + len(sent)),
            scratch_shapes=[
                pltpu.SMEM(boundary_rows.shape, jnp.int32),
                pltpu.SMEM(boundary_count.shape, jnp.int32),
                pltpu.VMEM(validity.shape, jnp.int32),
                pltpu.VMEM((lines, samples), F32),
                pltpu.VMEM(factors.shape, F32),
                pltpu.VMEM((per, seg, WIDE), F32),
                pltpu.VMEM((3, lines, LANE), F32),
                pltpu.SemaphoreType.DMA((6,)),
            ],
            compiler_params=pltpu.CompilerParams(vmem_limit_bytes=32 << 20),
            name="spectra",
        )(*[placed(x, pltpu.HBM) for x in inputs])
        came = {(way, by): exchange(array, way % 3, by) for (way, by), array in zip(sent, rest)}
        rows = per * columns
        keep, spread, first = pl.pallas_call(
            lambda *refs: ready_kernel(per, seg, *refs),
            out_shape=(
                pltpu.VMEM((rows, LANE), F32),
                pltpu.VMEM((per * lines, WIDE + LANE), F32),
                pltpu.VMEM((per * 8, WIDE + LANE), F32),
            ),
            in_specs=[hbm, vmem],
            out_specs=(vmem,) * 3,
            scratch_shapes=[pltpu.VMEM(pair_mask.shape, jnp.int32), pltpu.SemaphoreType.DMA((2,))],
            compiler_params=pltpu.CompilerParams(vmem_limit_bytes=32 << 20),
            name="ready",
        )(placed(pair_mask, pltpu.HBM), placed(mine, pltpu.VMEM))
        both = [came[3, d] for d in range(1, grps)]
        for d in range(1, grps):
            came[0, d] = came[3, d]
        if both:
            passed = pl.pallas_call(
                lambda _, *refs: pass_kernel(lines, *refs),
                out_shape=(payload,) * len(both),
                in_specs=[vmem] * (1 + len(both)),
                out_specs=(vmem,) * len(both),
                name="pass",
            )(*[placed(x, pltpu.VMEM) for x in (first, *both)])
            for d, array in enumerate(passed):
                came[1, d + 1] = exchange(array, 1, 0)
        inputs = [placed(x, pltpu.VMEM) for x in (basis, spread, first, *(came[name] for name in soon))]
        series = pl.pallas_call(
            lambda *refs: early_kernel(per, seg, grps, tiles, soon, *refs),
            out_shape=pltpu.VMEM((rows, LAGS), F32),
            in_specs=[vmem] * len(inputs),
            out_specs=vmem,
            compiler_params=pltpu.CompilerParams(vmem_limit_bytes=32 << 20),
            name="early",
        )(*inputs)
        inputs = [placed(x, pltpu.VMEM) for x in (basis, keep, spread, series, *(came[name] for name in late))]
        return pl.pallas_call(
            lambda *refs: lags_kernel(per, seg, grps, tiles, late, *refs),
            out_shape=jax.ShapeDtypeStruct((per, columns, LAGS), BF16),
            in_specs=[vmem] * len(inputs),
            out_specs=hbm,
            scratch_shapes=[
                pltpu.VMEM((per, columns, LAGS), BF16),
                pltpu.SemaphoreType.DMA((pl.cdiv(LAGS, LAG_STEP),)),
            ],
            compiler_params=pltpu.CompilerParams(vmem_limit_bytes=32 << 20),
            name="lags",
        )(*inputs)

    return jax.shard_map(
        on_device,
        mesh=mesh,
        in_specs=(P(axes, None, None), P(axes, None), P(axes, None, None), P(axes, None), P(axes, None)),
        out_specs=P(axes, None, None),
        check_vma=False,
    )
```

```python
import numpy as np
import ml_dtypes

import jax
import jax.numpy as jnp
from jax import lax
from jax.experimental import pallas as pl
from jax.experimental.pallas import tpu as pltpu
from jax.sharding import PartitionSpec as P

NBIN = 144
MAXLAG = 1000
LAGS = 2001
LANE = 128
TAIL = NBIN - LANE
HALF = 64
LAST = ((0, 1), (1, 0))
VALID = 16
SLOT = 24
WIDE = 3 * LANE
LAG_STEP = 4 * LANE
STEP = 2 * LANE
FINE = 16
F32 = jnp.float32
BF16 = jnp.bfloat16


def split(table):
    high = table.astype(ml_dtypes.bfloat16)
    low = (table - high.astype(np.float64)).astype(ml_dtypes.bfloat16)
    return high, low


def in_lanes(real, imag):
    out = np.zeros((real.shape[0], WIDE))
    out[:, :LANE] = real[:, :LANE]
    out[:, LANE : 2 * LANE] = imag[:, :LANE]
    out[:, 2 * LANE : 2 * LANE + TAIL] = real[:, LANE:]
    out[:, 2 * LANE + HALF : 2 * LANE + HALF + TAIL] = imag[:, LANE:]
    return out


def fourier_tables(samples):
    bins = np.arange(1, NBIN + 1)
    turn = np.pi / samples
    stretches = -(-samples // STEP)

    def angles(number):
        return np.mod(number[:, None] * bins[None, :], 2 * samples) * turn

    whole = angles(np.arange(stretches) * STEP)
    coarse = angles(np.arange(STEP // FINE) * FINE)
    fine = angles(np.arange(FINE))
    number = np.arange(stretches * STEP)
    taper = np.where(number < samples, 0.5 - 0.5 * np.cos(number * (2.0 * np.pi / samples)), 0.0)
    parts = [
        in_lanes(np.cos(whole), np.cos(whole)),
        in_lanes(np.sin(whole), -np.sin(whole)),
        np.pad(taper.reshape(stretches, STEP), ((0, 0), (0, WIDE - STEP))),
        in_lanes(np.cos(coarse), -np.sin(coarse)),
        in_lanes(-np.sin(coarse), -np.cos(coarse)),
        in_lanes(np.cos(fine), np.cos(fine)),
        in_lanes(np.sin(fine), np.sin(fine)),
    ]
    starts, rows = [], 0
    for i, part in enumerate(parts):
        parts[i] = np.pad(part, ((0, -len(part) % 8), (0, 0)))
        starts.append(rows)
        rows += len(parts[i])
    return np.concatenate(parts).astype(np.float32), starts, stretches


def lag_table(samples):
    lags = np.arange(LAGS) - MAXLAG
    bins = np.arange(1, NBIN + 1)
    angle = np.mod(lags[:, None] * bins[None, :], 2 * samples) * (np.pi / samples)
    scale = 1.0 / np.sqrt(NBIN)
    high, low = split(in_lanes(scale * np.cos(angle), -scale * np.sin(angle)).T)
    lane = np.arange(LANE)
    tail = np.where(holds_tail(lane)[:, None], high[2 * LANE :], low[LANE : 2 * LANE])
    return np.concatenate([high[: 2 * LANE], tail])


def holds_tail(lane):
    return ((lane & (HALF - 1)) < TAIL) | (lane == VALID)


def packed(real, imag, tail):
    return jnp.concatenate([real, imag, jnp.where(holds_tail(iota(tail.shape, 1)), tail, imag)], axis=1)


def iota(shape, dim):
    return lax.broadcasted_iota(jnp.int32, shape, dim)


def divided(value, by):
    if by & (by - 1) == 0:
        return value >> (by.bit_length() - 1), value & (by - 1)
    return lax.div(value, by), lax.rem(value, by)


def column_of(rows):
    n, m = rows.shape
    diagonal = iota((m, m), 0) == iota((m, m), 1)
    return [
        jnp.sum(jnp.where(diagonal, jnp.broadcast_to(rows[i : i + 1], (m, m)), 0.0), axis=1, keepdims=True)
        for i in range(n)
    ]


def spectra_kernel(
    per, seg, samples, ways, starts, stretches, rows_hbm, count_hbm, valid_hbm, traces_hbm, factors_hbm, basis_hbm, mask_hbm,
    *refs,
):
    mine_ref, *outs, basis_ref, mask_ref, rows_ref, count_ref, valid_ref, traces, factors, white_ref, order_ref, sems = refs
    lines = per * seg
    pairs = [
        (factors_hbm, factors), (traces_hbm, traces),
        (rows_hbm, rows_ref), (count_hbm, count_ref), (valid_hbm, valid_ref), (basis_hbm, basis_ref), (mask_hbm, mask_ref),
    ]
    copies = [pltpu.make_async_copy(src, dst, sems.at[i]) for i, (src, dst) in enumerate(pairs)]
    for copy in copies:
        copy.start()

    odd = lax.rem(lax.axis_index("tile"), 2)
    col = iota((STEP, STEP), 0)
    row = iota((STEP, STEP), 1)

    def bin_of(lane):
        tail = lane & (HALF - 1)
        known = (lane < LANE) | (tail < TAIL)
        return known, jnp.where(lane < LANE, lane, LANE + tail)

    known_in, bin_in = bin_of(col)
    known_out, bin_out = bin_of(row)
    near_bins = jnp.abs(bin_in - bin_out) <= 4
    window = jnp.where(known_in & known_out, jnp.where(near_bins, 17.0, 1.0), 0.0).astype(BF16)

    for copy in copies[2:5]:
        copy.wait()
    station, _ = divided(iota((lines, LANE), 0), seg)
    extra = jnp.zeros((lines, LANE), F32)
    for j in range(per):
        listed = (station == rows_ref[0, odd, j]) & (j < count_ref[0, odd])
        extra = jnp.where((iota((lines, LANE), 1) == SLOT + j) & listed, 1.0, extra)
    usable = jnp.concatenate(column_of(valid_ref[...].astype(F32)), axis=0)

    copies[0].wait()
    turn_at, swap_at, taper_at, coarse_at, cross_at, fine_at, other_at = starts
    fine, other = factors[fine_at : fine_at + FINE, :], factors[other_at : other_at + FINE, :]
    high, low = [], []
    for i in range(STEP // FINE):
        rows = factors[coarse_at + i : coarse_at + i + 1, :] * fine
        rows = rows + factors[cross_at + i : cross_at + i + 1, :] * other
        high.append(rows.astype(BF16))
        low.append((rows - high[-1].astype(F32)).astype(BF16))
    table = jnp.concatenate([*high, *high, *low], axis=0)

    copies[1].wait()
    left = []
    for j in range(stretches):
        at = j * STEP
        x = traces[:, at : min(at + STEP, samples)]
        if at + STEP > samples:
            x = jnp.concatenate([x, jnp.zeros((lines, at + STEP - samples), F32)], axis=1)
        x = x * factors[taper_at + j : taper_at + j + 1, :STEP]
        x_high = x.astype(BF16)
        x_low = (x - x_high.astype(F32)).astype(BF16)
        left.append(jnp.concatenate([x_high, x_low, x_high], axis=1))
    parts = jnp.dot(jnp.concatenate(left, axis=0), table, preferred_element_type=F32)
    real, imag, tail = (parts[:lines, k * LANE : (k + 1) * LANE] for k in range(3))
    for j in range(1, stretches):
        p_re, p_im, p_tail = (parts[j * lines : (j + 1) * lines, k * LANE : (k + 1) * LANE] for k in range(3))
        turn = factors[turn_at + j : turn_at + j + 1, :]
        swap = factors[swap_at + j : swap_at + j + 1, :]
        real = real + p_re * turn[:, :LANE] + p_im * swap[:, :LANE]
        imag = imag + p_im * turn[:, LANE : 2 * LANE] + p_re * swap[:, LANE : 2 * LANE]
        tail = tail + p_tail * turn[:, 2 * LANE :] + pltpu.roll(p_tail, HALF, 1) * swap[:, 2 * LANE :]

    power = jnp.concatenate([real * real + imag * imag, tail * tail], axis=1)
    p_high = power.astype(BF16)
    p_low = (power - p_high.astype(F32)).astype(BF16)
    level = jnp.dot(p_high, window, preferred_element_type=F32)
    level = level + jnp.dot(p_low, window, preferred_element_type=F32)
    factor = usable / jnp.sqrt(level * (1.0 / (2 * NBIN)) + 1e-06)
    tail = tail * factor[:, LANE:]
    tail = jnp.where(iota((lines, LANE), 1) == VALID, usable, tail) + extra
    white = jnp.concatenate([real * factor[:, :LANE], imag * factor[:, :LANE], tail], axis=1)
    white_ref[...] = white.reshape(per, seg, WIDE)

    def ordered(direction):
        for j in range(per):
            if direction is None:
                rows = white_ref[j]
            else:
                rows = white_ref[rows_ref[0, direction, j]]
                rows = jnp.where(j < count_ref[0, direction], rows, 0.0)
            for k in range(3):
                order_ref[k, pl.ds(j, seg, stride=per), :] = rows[:, k * LANE : (k + 1) * LANE]
        return jnp.concatenate([order_ref[k] for k in range(3)], axis=1).astype(BF16)

    own, near, far = ordered(None), ordered(odd), ordered(1 - odd)
    mine_ref[...] = own
    for ref, way in zip(outs, ways):
        ref[...] = (own, near, far, own)[way]
    for copy in copies[5:]:
        copy.wait()


def stacked(per, lines, spread, ref):
    sums = [[None] * 5 for _ in range(per)]

    def add(s, i, value):
        sums[s][i] = value if sums[s][i] is None else sums[s][i] + value

    for at in range(0, lines, 16):
        both = ref[at : at + 16, :].astype(F32)
        for half in range(2):
            one = both[8 * half : 8 * half + 8]
            c_re, c_im, c_tail = one[:, :LANE], one[:, LANE : 2 * LANE], one[:, 2 * LANE :]
            c_turn = pltpu.roll(c_tail, HALF, 1)
            c_valid = jnp.broadcast_to(c_tail[:, VALID : VALID + 1], c_tail.shape)
            for s in range(per):
                here = s * lines + at + 8 * half
                left = spread[here : here + 8, :]
                l_re, l_im, l_tail, l_valid = (left[:, k * LANE : (k + 1) * LANE] for k in range(4))
                add(s, 0, l_re * c_re + l_im * c_im)
                add(s, 1, l_im * c_re - l_re * c_im)
                add(s, 2, l_tail * c_tail)
                add(s, 3, l_tail * c_turn)
                add(s, 4, l_valid * c_valid)
    low_lanes = iota((8, LANE), 1) < HALF
    out = []
    for s in range(per):
        straight, turned = sums[s][2], sums[s][3]
        straight = straight + pltpu.roll(straight, HALF, 1)
        turned = turned - pltpu.roll(turned, HALF, 1)
        all_lanes = [sums[s][0], sums[s][1], jnp.where(low_lanes, straight, turned), sums[s][4]]
        out.append([v + pltpu.roll(v, 4, 0) for v in all_lanes])
    return out


def store_sums(per, ref, i, pieces):
    for s, sums in enumerate(pieces):
        at = (i * per + s) * 8
        for k in range(4):
            ref[at : at + 8, k * LANE : (k + 1) * LANE] = sums[k]


def load_sums(per, ref, i):
    rows = [ref[(i * per + s) * 8 : (i * per + s) * 8 + 8, :] for s in range(per)]
    return [[row[:, k * LANE : (k + 1) * LANE] for k in range(4)] for row in rows]


def ready_kernel(per, seg, mine_ref, spread_ref, sums_ref):
    lines = per * seg
    part, _ = divided(iota((lines, lines), 0), per)
    source = iota((lines, lines), 1)
    pick = [jnp.where(source == part * per + s, 1.0, 0.0).astype(BF16) for s in range(per)]
    spread = jnp.dot(jnp.concatenate(pick, axis=0), mine_ref[...], preferred_element_type=F32)
    spread_ref[:, : 2 * LANE] = spread[:, : 2 * LANE]
    tail = spread[:, 2 * LANE :]
    spread_ref[:, 2 * LANE : WIDE] = jnp.where(holds_tail(iota(tail.shape, 1)), tail, 0.0)
    valid = spread[:, 2 * LANE + VALID : 2 * LANE + VALID + 1]
    spread_ref[:, WIDE:] = jnp.broadcast_to(valid, (per * lines, LANE))
    store_sums(per, sums_ref, 0, stacked(per, lines, spread_ref, mine_ref))


def pass_kernel(_, near_ref, *refs):
    half = len(refs) // 2
    for src, dst in zip((near_ref, *refs[:half]), refs[half:]):
        dst[...] = src[...]


def place_of(name, grps, tiles):
    way, by = name
    tile = lax.axis_index("tile")
    odd = lax.rem(tile, 2)
    source = lax.rem(lax.axis_index("grp") + (grps - by), grps)
    kind = (0, 2 - odd, 1 + odd)[way]
    there = jnp.where(odd == 1, tile < tiles - 1, tile > 0) if way == 2 else None
    return 3 * source + kind, there


def over_count(rows):
    scale = 1.0 / jnp.maximum(rows[3], 1.0)
    return packed(*(row * scale for row in rows[:3])).astype(BF16)


def early_kernel(per, seg, grps, tiles, names, mask_ref, basis_ref, spread_ref, mine_ref, *refs):
    *came, series_ref, keep_ref, near_ref = refs
    keep = jnp.concatenate(column_of(mask_ref[...].astype(F32)), axis=0)
    keep_ref[...] = jnp.broadcast_to(keep, keep_ref.shape)
    lines = per * seg
    _, slot = divided(iota((LANE, lines), 1), per)
    to_slots = jnp.where(iota((LANE, lines), 0) == SLOT + slot, 1.0, 0.0).astype(BF16)
    same = divided(iota((lines, lines), 0), per)[0] == divided(iota((lines, lines), 1), per)[0]
    sums = [load_sums(per, mine_ref, 0)]
    for i, ref in enumerate(came):
        listed = jnp.dot(ref[:, 2 * LANE :], to_slots, preferred_element_type=F32)
        listed = jnp.where(same, listed, 0.0).astype(BF16)
        near_ref[i] = lax.dot_general(listed, ref[...], (((0,), (0,)), ((), ())), preferred_element_type=F32)
        sums.append(stacked(per, lines, spread_ref, near_ref.at[i]))
    places = [place_of(name, grps, tiles) for name in ((0, 0), *names)]
    half = iota((8, LANE), 0) >> 2
    blocks = 3 * grps // 2
    left = [None] * (per * blocks)
    for b in range(blocks):
        fits = []
        for place, there in places:
            fit = (half + 2 * b) == place
            fits.append(fit if there is None else fit & there)
        for s in range(per):
            rows = [jnp.zeros((8, LANE), F32)] * 4
            for fit, piece in zip(fits, sums):
                rows = [jnp.where(fit, new, row) for new, row in zip(piece[s], rows)]
            at = (s * blocks + b) * 8
            left[at // 8] = over_count(rows)
    series_ref[...] = jnp.dot(jnp.concatenate(left, axis=0), basis_ref[...], preferred_element_type=F32)


def lags_kernel(per, seg, grps, tiles, names, basis_ref, keep_ref, spread_ref, series_ref, *refs):
    *came, out_ref, result, sems = refs
    left = []
    for ref in came:
        left += [over_count(rows) for rows in stacked(per, per * seg, spread_ref, ref)]
    left = jnp.concatenate(left, axis=0)
    places = [place_of(name, grps, tiles) for name in names]
    blocks = 3 * grps // 2
    copies = []
    for i, lo in enumerate(range(0, LAGS, LAG_STEP)):
        hi = min(lo + LAG_STEP, LAGS)
        late = jnp.dot(left, basis_ref[:, lo:hi], preferred_element_type=F32)
        half = iota((8, hi - lo), 0) >> 2
        for s in range(per):
            rows = []
            for b in range(blocks):
                at = (s * blocks + b) * 8
                row = series_ref[at : at + 8, lo:hi]
                for p, (place, there) in enumerate(places):
                    fit = (half + 2 * b) == place
                    fit = fit if there is None else fit & there
                    row = jnp.where(fit, late[(p * per + s) * 8 : (p * per + s) * 8 + 8], row)
                rows.append(row * keep_ref[at : at + 8, :1])
            result[s, :, lo:hi] = jnp.concatenate(rows, axis=0).astype(BF16)
        here = (slice(None), slice(None), slice(lo, hi))
        copies.append(pltpu.make_async_copy(result.at[here], out_ref.at[here], sems.at[i]))
        copies[-1].start()
    for copy in copies:
        copy.wait()


def solution(mesh):
    tiles, grps = mesh.shape["tile"], mesh.shape["grp"]
    axes = ("tile", "grp")
    vmem = pl.BlockSpec(memory_space=pltpu.VMEM)
    hbm = pl.BlockSpec(memory_space=pltpu.HBM)
    placed = pltpu.with_memory_space_constraint

    def exchange(array, way, by):
        pairs = []
        for t in range(tiles):
            to = (t, t ^ 1, ((t + 1) ^ 1) - 1)[way]
            for g in range(grps):
                if 0 <= to < tiles:
                    goal = to * grps + (g + by) % grps
                else:
                    goal = t * grps + (g + max(by, 1)) % grps
                pairs.append((t * grps + g, goal))
        return lax.ppermute(array, axes, pairs)

    def call(kernel, name, inputs, **kw):
        return pl.pallas_call(
            kernel,
            in_specs=[vmem] * len(inputs),
            compiler_params=pltpu.CompilerParams(vmem_limit_bytes=32 << 20),
            name=name,
            **kw,
        )(*[placed(x, pltpu.VMEM) for x in inputs])

    def on_device(traces, validity, boundary_rows, boundary_count, pair_mask):
        per, seg, samples = traces.shape
        lines = per * seg
        columns = pair_mask.shape[1]
        factors, starts, stretches = fourier_tables(samples)
        lag_basis = jnp.asarray(lag_table(samples))
        payload = pltpu.VMEM((lines, WIDE), BF16)
        sent = [(3, d) for d in range(1, grps)] + [(2, d) for d in reversed(range(grps))]
        soon = [(1, d) for d in range(1, grps)]
        late = [(2, d) for d in reversed(range(grps))] + [(1, 0)] + [(0, d) for d in range(1, grps)]
        inputs = [boundary_rows, boundary_count, validity, traces.reshape(lines, samples), jnp.asarray(factors), lag_basis, pair_mask]
        mine, near, *rest, basis, mask = pl.pallas_call(
            lambda *refs: spectra_kernel(
                per, seg, samples, [1] + [way for way, _ in sent], starts, stretches, *refs
            ),
            out_shape=(payload,) * (2 + len(sent))
            + (pltpu.VMEM(lag_basis.shape, BF16), pltpu.VMEM(pair_mask.shape, jnp.int32)),
            in_specs=[hbm] * len(inputs),
            out_specs=(vmem,) * (4 + len(sent)),
            scratch_shapes=[
                pltpu.SMEM(boundary_rows.shape, jnp.int32),
                pltpu.SMEM(boundary_count.shape, jnp.int32),
                pltpu.VMEM(validity.shape, jnp.int32),
                pltpu.VMEM((lines, samples), F32),
                pltpu.VMEM(factors.shape, F32),
                pltpu.VMEM((per, seg, WIDE), F32),
                pltpu.VMEM((3, lines, LANE), F32),
                pltpu.SemaphoreType.DMA((7,)),
            ],
            compiler_params=pltpu.CompilerParams(vmem_limit_bytes=32 << 20),
            name="spectra",
        )(*[placed(x, pltpu.HBM) for x in inputs])
        came = [exchange(array, min(way, 4 - way), by) for (way, by), array in zip(sent, rest)]
        aside, far = came[: grps - 1], came[grps - 1 :]
        rows = per * columns
        spread, first = call(
            lambda *refs: ready_kernel(per, seg, *refs),
            "ready",
            [mine],
            out_shape=(
                pltpu.VMEM((per * lines, WIDE + LANE), F32),
                pltpu.VMEM((per * 8, WIDE + LANE), F32),
            ),
            out_specs=(vmem,) * 2,
        )
        passed = call(
            pass_kernel,
            "pass",
            [first, near, *aside],
            out_shape=(payload,) * grps,
            out_specs=(vmem,) * grps,
        )
        passed = [exchange(array, 1, 0) for array in passed]
        series, keep = call(
            lambda *refs: early_kernel(per, seg, grps, tiles, soon, *refs),
            "early",
            [mask, basis, spread, first, *aside],
            out_shape=(pltpu.VMEM((rows, LAGS), F32), pltpu.VMEM((rows, LANE), F32)),
            out_specs=(vmem,) * 2,
            scratch_shapes=[pltpu.VMEM((max(len(soon), 1), lines, WIDE), F32)],
        )
        return call(
            lambda *refs: lags_kernel(per, seg, grps, tiles, late, *refs),
            "lags",
            [basis, keep, spread, series, *far, *passed],
            out_shape=jax.ShapeDtypeStruct((per, columns, LAGS), BF16),
            out_specs=hbm,
            scratch_shapes=[
                pltpu.VMEM((per, columns, LAGS), BF16),
                pltpu.SemaphoreType.DMA((pl.cdiv(LAGS, LAG_STEP),)),
            ],
        )

    return jax.shard_map(
        on_device,
        mesh=mesh,
        in_specs=(P(axes, None, None), P(axes, None), P(axes, None, None), P(axes, None), P(axes, None)),
        out_specs=P(axes, None, None),
        check_vma=False,
    )
```

```python
import numpy as np
import ml_dtypes

import jax
import jax.numpy as jnp
from jax import lax
from jax.experimental import pallas as pl
from jax.experimental.pallas import tpu as pltpu
from jax.sharding import PartitionSpec as P

NBIN = 144
MAXLAG = 1000
LAGS = 2001
LANE = 128
TAIL = NBIN - LANE
HALF = 64
LAST = ((0, 1), (1, 0))
TOGETHER = 2
VALID = 16
SLOT = 24
WIDE = 3 * LANE
LAG_STEP = 4 * LANE
STEP = 2 * LANE
FINE = 16
F32 = jnp.float32
BF16 = jnp.bfloat16


def split(table):
    high = table.astype(ml_dtypes.bfloat16)
    low = (table - high.astype(np.float64)).astype(ml_dtypes.bfloat16)
    return high, low


def in_lanes(real, imag):
    out = np.zeros((real.shape[0], WIDE))
    out[:, :LANE] = real[:, :LANE]
    out[:, LANE : 2 * LANE] = imag[:, :LANE]
    out[:, 2 * LANE : 2 * LANE + TAIL] = real[:, LANE:]
    out[:, 2 * LANE + HALF : 2 * LANE + HALF + TAIL] = imag[:, LANE:]
    return out


def fourier_tables(samples):
    bins = np.arange(1, NBIN + 1)
    turn = np.pi / samples
    stretches = -(-samples // STEP)

    def angles(number):
        return np.mod(number[:, None] * bins[None, :], 2 * samples) * turn

    whole = angles(np.arange(stretches) * STEP)
    coarse = angles(np.arange(STEP // FINE) * FINE)
    fine = angles(np.arange(FINE))
    number = np.arange(stretches * STEP)
    taper = np.where(number < samples, 0.5 - 0.5 * np.cos(number * (2.0 * np.pi / samples)), 0.0)
    parts = [
        in_lanes(np.cos(whole), np.cos(whole)),
        in_lanes(np.sin(whole), -np.sin(whole)),
        np.pad(taper.reshape(stretches, STEP), ((0, 0), (0, WIDE - STEP))),
        in_lanes(np.cos(coarse), -np.sin(coarse)),
        in_lanes(-np.sin(coarse), -np.cos(coarse)),
        in_lanes(np.cos(fine), np.cos(fine)),
        in_lanes(np.sin(fine), np.sin(fine)),
    ]
    starts, rows = [], 0
    for i, part in enumerate(parts):
        parts[i] = np.pad(part, ((0, -len(part) % 8), (0, 0)))
        starts.append(rows)
        rows += len(parts[i])
    return np.concatenate(parts).astype(np.float32), starts, stretches


def lag_table(samples):
    lags = np.arange(LAGS) - MAXLAG
    bins = np.arange(1, NBIN + 1)
    angle = np.mod(lags[:, None] * bins[None, :], 2 * samples) * (np.pi / samples)
    scale = 1.0 / np.sqrt(NBIN)
    high, low = split(in_lanes(scale * np.cos(angle), -scale * np.sin(angle)).T)
    lane = np.arange(LANE)
    tail = np.where(holds_tail(lane)[:, None], high[2 * LANE :], low[LANE : 2 * LANE])
    return np.concatenate([high[: 2 * LANE], tail])


def holds_tail(lane):
    return ((lane & (HALF - 1)) < TAIL) | (lane == VALID)


def packed(real, imag, tail):
    return jnp.concatenate([real, imag, jnp.where(holds_tail(iota(tail.shape, 1)), tail, imag)], axis=1)


def iota(shape, dim):
    return lax.broadcasted_iota(jnp.int32, shape, dim)


def divided(value, by):
    if by & (by - 1) == 0:
        return value >> (by.bit_length() - 1), value & (by - 1)
    return lax.div(value, by), lax.rem(value, by)


def column_of(rows):
    n, m = rows.shape
    diagonal = iota((m, m), 0) == iota((m, m), 1)
    return [
        jnp.sum(jnp.where(diagonal, jnp.broadcast_to(rows[i : i + 1], (m, m)), 0.0), axis=1, keepdims=True)
        for i in range(n)
    ]


def spectra_kernel(
    per, seg, samples, ways, starts, stretches, rows_hbm, count_hbm, valid_hbm, traces_hbm, factors_hbm, basis_hbm, mask_hbm,
    *refs,
):
    mine_ref, *outs, basis_ref, mask_ref, rows_ref, count_ref, valid_ref, traces, factors, white_ref, order_ref, sems = refs
    lines = per * seg
    pairs = [
        (factors_hbm, factors), (traces_hbm, traces),
        (rows_hbm, rows_ref), (count_hbm, count_ref), (valid_hbm, valid_ref), (basis_hbm, basis_ref), (mask_hbm, mask_ref),
    ]
    copies = [pltpu.make_async_copy(src, dst, sems.at[i]) for i, (src, dst) in enumerate(pairs)]
    for copy in copies:
        copy.start()

    odd = lax.rem(lax.axis_index("tile"), 2)
    col = iota((STEP, STEP), 0)
    row = iota((STEP, STEP), 1)

    def bin_of(lane):
        tail = lane & (HALF - 1)
        known = (lane < LANE) | (tail < TAIL)
        return known, jnp.where(lane < LANE, lane, LANE + tail)

    known_in, bin_in = bin_of(col)
    known_out, bin_out = bin_of(row)
    near_bins = jnp.abs(bin_in - bin_out) <= 4
    window = jnp.where(known_in & known_out, jnp.where(near_bins, 17.0, 1.0), 0.0).astype(BF16)

    for copy in copies[2:5]:
        copy.wait()
    station, _ = divided(iota((lines, LANE), 0), seg)
    extra = jnp.zeros((lines, LANE), F32)
    for j in range(per):
        listed = (station == rows_ref[0, odd, j]) & (j < count_ref[0, odd])
        extra = jnp.where((iota((lines, LANE), 1) == SLOT + j) & listed, 1.0, extra)
    usable = jnp.concatenate(column_of(valid_ref[...].astype(F32)), axis=0)

    copies[0].wait()
    turn_at, swap_at, taper_at, coarse_at, cross_at, fine_at, other_at = starts
    fine, other = factors[fine_at : fine_at + FINE, :], factors[other_at : other_at + FINE, :]
    high, low = [], []
    for i in range(STEP // FINE):
        rows = factors[coarse_at + i : coarse_at + i + 1, :] * fine
        rows = rows + factors[cross_at + i : cross_at + i + 1, :] * other
        high.append(rows.astype(BF16))
        low.append((rows - high[-1].astype(F32)).astype(BF16))
    table = jnp.concatenate([*high, *high, *low], axis=0)

    copies[1].wait()
    left = []
    for j in range(stretches):
        at = j * STEP
        x = traces[:, at : min(at + STEP, samples)]
        if at + STEP > samples:
            x = jnp.concatenate([x, jnp.zeros((lines, at + STEP - samples), F32)], axis=1)
        x = x * factors[taper_at + j : taper_at + j + 1, :STEP]
        x_high = x.astype(BF16)
        x_low = (x - x_high.astype(F32)).astype(BF16)
        left.append(jnp.concatenate([x_high, x_low, x_high], axis=1))
    parts = jnp.dot(jnp.concatenate(left, axis=0), table, preferred_element_type=F32)
    real, imag, tail = (parts[:lines, k * LANE : (k + 1) * LANE] for k in range(3))
    for j in range(1, stretches):
        p_re, p_im, p_tail = (parts[j * lines : (j + 1) * lines, k * LANE : (k + 1) * LANE] for k in range(3))
        turn = factors[turn_at + j : turn_at + j + 1, :]
        swap = factors[swap_at + j : swap_at + j + 1, :]
        real = real + p_re * turn[:, :LANE] + p_im * swap[:, :LANE]
        imag = imag + p_im * turn[:, LANE : 2 * LANE] + p_re * swap[:, LANE : 2 * LANE]
        tail = tail + p_tail * turn[:, 2 * LANE :] + pltpu.roll(p_tail, HALF, 1) * swap[:, 2 * LANE :]

    power = jnp.concatenate([real * real + imag * imag, tail * tail], axis=1)
    p_high = power.astype(BF16)
    p_low = (power - p_high.astype(F32)).astype(BF16)
    level = jnp.dot(p_high, window, preferred_element_type=F32)
    level = level + jnp.dot(p_low, window, preferred_element_type=F32)
    factor = usable / jnp.sqrt(level * (1.0 / (2 * NBIN)) + 1e-06)
    tail = tail * factor[:, LANE:]
    tail = jnp.where(iota((lines, LANE), 1) == VALID, usable, tail) + extra
    white = jnp.concatenate([real * factor[:, :LANE], imag * factor[:, :LANE], tail], axis=1)
    white_ref[...] = white.reshape(per, seg, WIDE)

    def ordered(direction):
        for j in range(per):
            if direction is None:
                rows = white_ref[j]
            else:
                rows = white_ref[rows_ref[0, direction, j]]
                rows = jnp.where(j < count_ref[0, direction], rows, 0.0)
            for k in range(3):
                order_ref[k, pl.ds(j, seg, stride=per), :] = rows[:, k * LANE : (k + 1) * LANE]
        return jnp.concatenate([order_ref[k] for k in range(3)], axis=1).astype(BF16)

    own, near, far = ordered(None), ordered(odd), ordered(1 - odd)
    mine_ref[...] = own
    for ref, way in zip(outs, ways):
        ref[...] = (own, near, far, own)[way]
    for copy in copies[5:]:
        copy.wait()


def stacked(per, lines, spread, refs):
    sums = [[[None] * 5 for _ in range(per)] for _ in refs]

    def add(total, i, value):
        total[i] = value if total[i] is None else total[i] + value

    for at in range(0, lines, 16):
        both = [ref[at : at + 16, :].astype(F32) for ref in refs]
        for half in range(2):
            columns = []
            for x in both:
                one = x[8 * half : 8 * half + 8]
                c_re, c_im, c_tail = one[:, :LANE], one[:, LANE : 2 * LANE], one[:, 2 * LANE :]
                c_valid = jnp.broadcast_to(c_tail[:, VALID : VALID + 1], c_tail.shape)
                columns.append((c_re, c_im, c_tail, pltpu.roll(c_tail, HALF, 1), c_valid))
            for s in range(per):
                here = s * lines + at + 8 * half
                left = spread[here : here + 8, :]
                l_re, l_im, l_tail, l_valid = (left[:, k * LANE : (k + 1) * LANE] for k in range(4))
                for total, (c_re, c_im, c_tail, c_turn, c_valid) in zip(sums, columns):
                    add(total[s], 0, l_re * c_re + l_im * c_im)
                    add(total[s], 1, l_im * c_re - l_re * c_im)
                    add(total[s], 2, l_tail * c_tail)
                    add(total[s], 3, l_tail * c_turn)
                    add(total[s], 4, l_valid * c_valid)
    low_lanes = iota((8, LANE), 1) < HALF
    out = []
    for total in sums:
        piece = []
        for re, im, straight, turned, count in total:
            straight = straight + pltpu.roll(straight, HALF, 1)
            turned = turned - pltpu.roll(turned, HALF, 1)
            all_lanes = [re, im, jnp.where(low_lanes, straight, turned), count]
            piece.append([v + pltpu.roll(v, 4, 0) for v in all_lanes])
        out.append(piece)
    return out


def store_sums(per, ref, i, pieces):
    for s, sums in enumerate(pieces):
        at = (i * per + s) * 8
        for k in range(4):
            ref[at : at + 8, k * LANE : (k + 1) * LANE] = sums[k]


def load_sums(per, ref, i):
    rows = [ref[(i * per + s) * 8 : (i * per + s) * 8 + 8, :] for s in range(per)]
    return [[row[:, k * LANE : (k + 1) * LANE] for k in range(4)] for row in rows]


def ready_kernel(per, seg, mine_ref, spread_ref, sums_ref):
    lines = per * seg
    part, _ = divided(iota((lines, lines), 0), per)
    source = iota((lines, lines), 1)
    pick = [jnp.where(source == part * per + s, 1.0, 0.0).astype(BF16) for s in range(per)]
    spread = jnp.dot(jnp.concatenate(pick, axis=0), mine_ref[...], preferred_element_type=F32)
    spread_ref[:, : 2 * LANE] = spread[:, : 2 * LANE]
    tail = spread[:, 2 * LANE :]
    spread_ref[:, 2 * LANE : WIDE] = jnp.where(holds_tail(iota(tail.shape, 1)), tail, 0.0)
    valid = spread[:, 2 * LANE + VALID : 2 * LANE + VALID + 1]
    spread_ref[:, WIDE:] = jnp.broadcast_to(valid, (per * lines, LANE))
    store_sums(per, sums_ref, 0, stacked(per, lines, spread_ref, [mine_ref])[0])


def pass_kernel(_, near_ref, *refs):
    half = len(refs) // 2
    for src, dst in zip((near_ref, *refs[:half]), refs[half:]):
        dst[...] = src[...]


def place_of(name, grps, tiles):
    way, by = name
    tile = lax.axis_index("tile")
    odd = lax.rem(tile, 2)
    source = lax.rem(lax.axis_index("grp") + (grps - by), grps)
    kind = (0, 2 - odd, 1 + odd)[way]
    there = jnp.where(odd == 1, tile < tiles - 1, tile > 0) if way == 2 else None
    return 3 * source + kind, there


def over_count(rows):
    scale = 1.0 / jnp.maximum(rows[3], 1.0)
    return packed(*(row * scale for row in rows[:3]))


def put(names, grps, tiles, per, pieces, rows):
    places = [place_of(name, grps, tiles) for name in names]
    half = iota((8, WIDE), 0) >> 2
    blocks = 3 * grps // 2
    for b in range(blocks):
        for (place, there), piece in zip(places, pieces):
            fit = (half + 2 * b) == place
            fit = fit if there is None else fit & there
            for s in range(per):
                at = s * blocks + b
                rows[at] = jnp.where(fit, piece[s], rows[at])
    return rows


def early_kernel(per, seg, grps, tiles, names, mask_ref, spread_ref, mine_ref, *refs):
    *came, rows_ref, keep_ref, near_ref = refs
    keep = jnp.concatenate(column_of(mask_ref[...].astype(F32)), axis=0)
    keep_ref[...] = jnp.broadcast_to(keep, keep_ref.shape)
    lines = per * seg
    _, slot = divided(iota((LANE, lines), 1), per)
    to_slots = jnp.where(iota((LANE, lines), 0) == SLOT + slot, 1.0, 0.0).astype(BF16)
    same = divided(iota((lines, lines), 0), per)[0] == divided(iota((lines, lines), 1), per)[0]
    sums = [load_sums(per, mine_ref, 0)]
    for i, ref in enumerate(came):
        listed = jnp.dot(ref[:, 2 * LANE :], to_slots, preferred_element_type=F32)
        listed = jnp.where(same, listed, 0.0).astype(BF16)
        near_ref[i] = lax.dot_general(listed, ref[...], (((0,), (0,)), ((), ())), preferred_element_type=F32)
        sums += stacked(per, lines, spread_ref, [near_ref.at[i]])
    pieces = [[over_count(rows) for rows in piece] for piece in sums]
    rows = [jnp.zeros((8, WIDE), F32)] * (rows_ref.shape[0] // 8)
    rows_ref[...] = jnp.concatenate(put(((0, 0), *names), grps, tiles, per, pieces, rows), axis=0)


def middle_kernel(per, seg, grps, tiles, names, spread_ref, early_ref, *refs):
    *came, rows_ref = refs
    pieces = []
    for i in range(0, len(came), TOGETHER):
        for piece in stacked(per, per * seg, spread_ref, came[i : i + TOGETHER]):
            pieces.append([over_count(rows) for rows in piece])
    rows = [early_ref[at : at + 8, :] for at in range(0, early_ref.shape[0], 8)]
    rows_ref[...] = jnp.concatenate(put(names, grps, tiles, per, pieces, rows), axis=0)


def lags_kernel(per, seg, grps, tiles, names, basis_ref, keep_ref, spread_ref, rows_ref, *refs):
    *came, out_ref, result, sems = refs
    pieces = []
    for i in range(0, len(came), TOGETHER):
        for piece in stacked(per, per * seg, spread_ref, came[i : i + TOGETHER]):
            pieces.append([over_count(rows) for rows in piece])
    total = rows_ref.shape[0]
    rows = [rows_ref[at : at + 8, :] for at in range(0, total, 8)]
    rows = put(names, grps, tiles, per, pieces, rows)
    keep = [keep_ref[at : at + 8, :] for at in range(0, total, 8)]
    left = [row * jnp.concatenate([k, k, k], axis=1) for row, k in zip(rows, keep)]
    left = jnp.concatenate(left, axis=0).astype(BF16)
    columns = total // per
    copies = []
    for i, lo in enumerate(range(0, LAGS, LAG_STEP)):
        hi = min(lo + LAG_STEP, LAGS)
        series = jnp.dot(left, basis_ref[:, lo:hi], preferred_element_type=F32).astype(BF16)
        for s in range(per):
            result[s, :, lo:hi] = series[s * columns : (s + 1) * columns]
        here = (slice(None), slice(None), slice(lo, hi))
        copies.append(pltpu.make_async_copy(result.at[here], out_ref.at[here], sems.at[i]))
        copies[-1].start()
    for copy in copies:
        copy.wait()


def solution(mesh):
    tiles, grps = mesh.shape["tile"], mesh.shape["grp"]
    axes = ("tile", "grp")
    vmem = pl.BlockSpec(memory_space=pltpu.VMEM)
    hbm = pl.BlockSpec(memory_space=pltpu.HBM)
    placed = pltpu.with_memory_space_constraint

    def exchange(array, way, by):
        pairs = []
        for t in range(tiles):
            to = (t, t ^ 1, ((t + 1) ^ 1) - 1)[way]
            for g in range(grps):
                if 0 <= to < tiles:
                    goal = to * grps + (g + by) % grps
                else:
                    goal = t * grps + (g + max(by, 1)) % grps
                pairs.append((t * grps + g, goal))
        return lax.ppermute(array, axes, pairs)

    def call(kernel, name, inputs, **kw):
        return pl.pallas_call(
            kernel,
            in_specs=[vmem] * len(inputs),
            compiler_params=pltpu.CompilerParams(vmem_limit_bytes=32 << 20),
            name=name,
            **kw,
        )(*[placed(x, pltpu.VMEM) for x in inputs])

    def on_device(traces, validity, boundary_rows, boundary_count, pair_mask):
        per, seg, samples = traces.shape
        lines = per * seg
        columns = pair_mask.shape[1]
        factors, starts, stretches = fourier_tables(samples)
        lag_basis = jnp.asarray(lag_table(samples))
        payload = pltpu.VMEM((lines, WIDE), BF16)
        sent = [(3, d) for d in range(1, grps)] + [(2, d) for d in reversed(range(grps))]
        soon = [(1, d) for d in range(1, grps)]
        late = [(2, d) for d in reversed(range(grps))] + [(1, 0)] + [(0, d) for d in range(1, grps)]
        inputs = [boundary_rows, boundary_count, validity, traces.reshape(lines, samples), jnp.asarray(factors), lag_basis, pair_mask]
        mine, near, *rest, basis, mask = pl.pallas_call(
            lambda *refs: spectra_kernel(
                per, seg, samples, [1] + [way for way, _ in sent], starts, stretches, *refs
            ),
            out_shape=(payload,) * (2 + len(sent))
            + (pltpu.VMEM(lag_basis.shape, BF16), pltpu.VMEM(pair_mask.shape, jnp.int32)),
            in_specs=[hbm] * len(inputs),
            out_specs=(vmem,) * (4 + len(sent)),
            scratch_shapes=[
                pltpu.SMEM(boundary_rows.shape, jnp.int32),
                pltpu.SMEM(boundary_count.shape, jnp.int32),
                pltpu.VMEM(validity.shape, jnp.int32),
                pltpu.VMEM((lines, samples), F32),
                pltpu.VMEM(factors.shape, F32),
                pltpu.VMEM((per, seg, WIDE), F32),
                pltpu.VMEM((3, lines, LANE), F32),
                pltpu.SemaphoreType.DMA((7,)),
            ],
            compiler_params=pltpu.CompilerParams(vmem_limit_bytes=32 << 20),
            name="spectra",
        )(*[placed(x, pltpu.HBM) for x in inputs])
        came = [exchange(array, min(way, 4 - way), by) for (way, by), array in zip(sent, rest)]
        aside, far = came[: grps - 1], came[grps - 1 :]
        rows = per * columns
        spread, first = call(
            lambda *refs: ready_kernel(per, seg, *refs),
            "ready",
            [mine],
            out_shape=(
                pltpu.VMEM((per * lines, WIDE + LANE), F32),
                pltpu.VMEM((per * 8, WIDE + LANE), F32),
            ),
            out_specs=(vmem,) * 2,
        )
        passed = call(
            pass_kernel,
            "pass",
            [first, near, *aside],
            out_shape=(payload,) * grps,
            out_specs=(vmem,) * grps,
        )
        passed = [exchange(array, 1, 0) for array in passed]
        early, keep = call(
            lambda *refs: early_kernel(per, seg, grps, tiles, soon, *refs),
            "early",
            [mask, spread, first, *aside],
            out_shape=(pltpu.VMEM((rows, WIDE), F32), pltpu.VMEM((rows, LANE), F32)),
            out_specs=(vmem,) * 2,
            scratch_shapes=[pltpu.VMEM((max(len(soon), 1), lines, WIDE), F32)],
            cost_estimate=pl.CostEstimate(flops=100000000000, transcendentals=0, bytes_accessed=1000000000),
        )
        early = call(
            lambda *refs: middle_kernel(per, seg, grps, tiles, late[grps:], *refs),
            "middle",
            [spread, early, *passed],
            out_shape=pltpu.VMEM((rows, WIDE), F32),
            out_specs=vmem,
        )
        return call(
            lambda *refs: lags_kernel(per, seg, grps, tiles, late[:grps], *refs),
            "lags",
            [basis, keep, spread, early, *far],
            out_shape=jax.ShapeDtypeStruct((per, columns, LAGS), BF16),
            out_specs=hbm,
            scratch_shapes=[
                pltpu.VMEM((per, columns, LAGS), BF16),
                pltpu.SemaphoreType.DMA((pl.cdiv(LAGS, LAG_STEP),)),
            ],
        )

    return jax.shard_map(
        on_device,
        mesh=mesh,
        in_specs=(P(axes, None, None), P(axes, None), P(axes, None, None), P(axes, None), P(axes, None)),
        out_specs=P(axes, None, None),
        check_vma=False,
    )
```

```python
import numpy as np
import ml_dtypes

import jax
import jax.numpy as jnp
from jax import lax
from jax.experimental import pallas as pl
from jax.experimental.pallas import tpu as pltpu
from jax.sharding import PartitionSpec as P

NBIN = 144
MAXLAG = 1000
LAGS = 2001
LANE = 128
TAIL = NBIN - LANE
HALF = 64
LAST = ((0, 1), (1, 0))
TOGETHER = 2
VALID = 16
SLOT = 24
WIDE = 3 * LANE
LAG_STEP = 4 * LANE
STEP = 2 * LANE
FINE = 16
F32 = jnp.float32
BF16 = jnp.bfloat16


def split(table):
    high = table.astype(ml_dtypes.bfloat16)
    low = (table - high.astype(np.float64)).astype(ml_dtypes.bfloat16)
    return high, low


def in_lanes(real, imag):
    out = np.zeros((real.shape[0], WIDE))
    out[:, :LANE] = real[:, :LANE]
    out[:, LANE : 2 * LANE] = imag[:, :LANE]
    out[:, 2 * LANE : 2 * LANE + TAIL] = real[:, LANE:]
    out[:, 2 * LANE + HALF : 2 * LANE + HALF + TAIL] = imag[:, LANE:]
    return out


def fourier_tables(samples):
    bins = np.arange(1, NBIN + 1)
    turn = np.pi / samples
    stretches = -(-samples // STEP)

    def angles(number):
        return np.mod(number[:, None] * bins[None, :], 2 * samples) * turn

    whole = angles(np.arange(stretches) * STEP)
    coarse = angles(np.arange(STEP // FINE) * FINE)
    fine = angles(np.arange(FINE))
    number = np.arange(stretches * STEP)
    taper = np.where(number < samples, 0.5 - 0.5 * np.cos(number * (2.0 * np.pi / samples)), 0.0)
    parts = [
        in_lanes(np.cos(whole), np.cos(whole)),
        in_lanes(np.sin(whole), -np.sin(whole)),
        np.pad(taper.reshape(stretches, STEP), ((0, 0), (0, WIDE - STEP))),
        in_lanes(np.cos(coarse), -np.sin(coarse)),
        in_lanes(-np.sin(coarse), -np.cos(coarse)),
        in_lanes(np.cos(fine), np.cos(fine)),
        in_lanes(np.sin(fine), np.sin(fine)),
    ]
    starts, rows = [], 0
    for i, part in enumerate(parts):
        parts[i] = np.pad(part, ((0, -len(part) % 8), (0, 0)))
        starts.append(rows)
        rows += len(parts[i])
    return np.concatenate(parts).astype(np.float32), starts, stretches


def lag_table(samples):
    lags = np.arange(LAGS) - MAXLAG
    bins = np.arange(1, NBIN + 1)
    angle = np.mod(lags[:, None] * bins[None, :], 2 * samples) * (np.pi / samples)
    scale = 1.0 / np.sqrt(NBIN)
    high, low = split(in_lanes(scale * np.cos(angle), -scale * np.sin(angle)).T)
    lane = np.arange(LANE)
    tail = np.where(holds_tail(lane)[:, None], high[2 * LANE :], low[LANE : 2 * LANE])
    return np.concatenate([high[: 2 * LANE], tail])


def holds_tail(lane):
    return ((lane & (HALF - 1)) < TAIL) | (lane == VALID)


def packed(real, imag, tail):
    return jnp.concatenate([real, imag, jnp.where(holds_tail(iota(tail.shape, 1)), tail, imag)], axis=1)


def iota(shape, dim):
    return lax.broadcasted_iota(jnp.int32, shape, dim)


def divided(value, by):
    if by & (by - 1) == 0:
        return value >> (by.bit_length() - 1), value & (by - 1)
    return lax.div(value, by), lax.rem(value, by)


def column_of(rows):
    n, m = rows.shape
    diagonal = iota((m, m), 0) == iota((m, m), 1)
    return [
        jnp.sum(jnp.where(diagonal, jnp.broadcast_to(rows[i : i + 1], (m, m)), 0.0), axis=1, keepdims=True)
        for i in range(n)
    ]


def spectra_kernel(
    per, seg, samples, ways, starts, stretches, rows_hbm, count_hbm, valid_hbm, traces_hbm, factors_hbm, basis_hbm, mask_hbm,
    *refs,
):
    mine_ref, *outs, basis_ref, mask_ref, rows_ref, count_ref, valid_ref, traces, factors, white_ref, order_ref, sems = refs
    lines = per * seg
    pairs = [
        (factors_hbm, factors), (traces_hbm, traces),
        (rows_hbm, rows_ref), (count_hbm, count_ref), (valid_hbm, valid_ref), (basis_hbm, basis_ref), (mask_hbm, mask_ref),
    ]
    copies = [pltpu.make_async_copy(src, dst, sems.at[i]) for i, (src, dst) in enumerate(pairs)]
    for copy in copies:
        copy.start()

    odd = lax.rem(lax.axis_index("tile"), 2)
    col = iota((STEP, STEP), 0)
    row = iota((STEP, STEP), 1)

    def bin_of(lane):
        tail = lane & (HALF - 1)
        known = (lane < LANE) | (tail < TAIL)
        return known, jnp.where(lane < LANE, lane, LANE + tail)

    known_in, bin_in = bin_of(col)
    known_out, bin_out = bin_of(row)
    near_bins = jnp.abs(bin_in - bin_out) <= 4
    window = jnp.where(known_in & known_out, jnp.where(near_bins, 17.0, 1.0), 0.0).astype(BF16)

    for copy in copies[2:5]:
        copy.wait()
    station, _ = divided(iota((lines, LANE), 0), seg)
    extra = jnp.zeros((lines, LANE), F32)
    for j in range(per):
        listed = (station == rows_ref[0, odd, j]) & (j < count_ref[0, odd])
        extra = jnp.where((iota((lines, LANE), 1) == SLOT + j) & listed, 1.0, extra)
    usable = jnp.concatenate(column_of(valid_ref[...].astype(F32)), axis=0)

    copies[0].wait()
    turn_at, swap_at, taper_at, coarse_at, cross_at, fine_at, other_at = starts
    fine, other = factors[fine_at : fine_at + FINE, :], factors[other_at : other_at + FINE, :]
    high, low = [], []
    for i in range(STEP // FINE):
        rows = factors[coarse_at + i : coarse_at + i + 1, :] * fine
        rows = rows + factors[cross_at + i : cross_at + i + 1, :] * other
        high.append(rows.astype(BF16))
        low.append((rows - high[-1].astype(F32)).astype(BF16))
    table = jnp.concatenate([*high, *high, *low], axis=0)

    copies[1].wait()
    left = []
    for j in range(stretches):
        at = j * STEP
        x = traces[:, at : min(at + STEP, samples)]
        if at + STEP > samples:
            x = jnp.concatenate([x, jnp.zeros((lines, at + STEP - samples), F32)], axis=1)
        x = x * factors[taper_at + j : taper_at + j + 1, :STEP]
        x_high = x.astype(BF16)
        x_low = (x - x_high.astype(F32)).astype(BF16)
        left.append(jnp.concatenate([x_high, x_low, x_high], axis=1))
    parts = jnp.dot(jnp.concatenate(left, axis=0), table, preferred_element_type=F32)
    real, imag, tail = (parts[:lines, k * LANE : (k + 1) * LANE] for k in range(3))
    for j in range(1, stretches):
        p_re, p_im, p_tail = (parts[j * lines : (j + 1) * lines, k * LANE : (k + 1) * LANE] for k in range(3))
        turn = factors[turn_at + j : turn_at + j + 1, :]
        swap = factors[swap_at + j : swap_at + j + 1, :]
        real = real + p_re * turn[:, :LANE] + p_im * swap[:, :LANE]
        imag = imag + p_im * turn[:, LANE : 2 * LANE] + p_re * swap[:, LANE : 2 * LANE]
        tail = tail + p_tail * turn[:, 2 * LANE :] + pltpu.roll(p_tail, HALF, 1) * swap[:, 2 * LANE :]

    power = jnp.concatenate([real * real + imag * imag, tail * tail], axis=1)
    p_high = power.astype(BF16)
    p_low = (power - p_high.astype(F32)).astype(BF16)
    level = jnp.dot(p_high, window, preferred_element_type=F32)
    level = level + jnp.dot(p_low, window, preferred_element_type=F32)
    factor = usable / jnp.sqrt(level * (1.0 / (2 * NBIN)) + 1e-06)
    tail = tail * factor[:, LANE:]
    tail = jnp.where(iota((lines, LANE), 1) == VALID, usable, tail) + extra
    white = jnp.concatenate([real * factor[:, :LANE], imag * factor[:, :LANE], tail], axis=1)
    white_ref[...] = white.reshape(per, seg, WIDE)

    def ordered(direction):
        for j in range(per):
            if direction is None:
                rows = white_ref[j]
            else:
                rows = white_ref[rows_ref[0, direction, j]]
                rows = jnp.where(j < count_ref[0, direction], rows, 0.0)
            for k in range(3):
                order_ref[k, pl.ds(j, seg, stride=per), :] = rows[:, k * LANE : (k + 1) * LANE]
        return jnp.concatenate([order_ref[k] for k in range(3)], axis=1).astype(BF16)

    own, near, far = ordered(None), ordered(odd), ordered(1 - odd)
    mine_ref[...] = own
    for ref, way in zip(outs, ways):
        ref[...] = (own, near, far, own)[way]
    for copy in copies[5:]:
        copy.wait()


def stacked(per, lines, spread, refs):
    sums = [[[None] * 5 for _ in range(per)] for _ in refs]

    def add(total, i, value):
        total[i] = value if total[i] is None else total[i] + value

    for at in range(0, lines, 16):
        both = [ref[at : at + 16, :].astype(F32) for ref in refs]
        for half in range(2):
            columns = []
            for x in both:
                one = x[8 * half : 8 * half + 8]
                c_re, c_im, c_tail = one[:, :LANE], one[:, LANE : 2 * LANE], one[:, 2 * LANE :]
                c_valid = jnp.broadcast_to(c_tail[:, VALID : VALID + 1], c_tail.shape)
                columns.append((c_re, c_im, c_tail, pltpu.roll(c_tail, HALF, 1), c_valid))
            for s in range(per):
                here = s * lines + at + 8 * half
                left = spread[here : here + 8, :]
                l_re, l_im, l_tail, l_valid = (left[:, k * LANE : (k + 1) * LANE] for k in range(4))
                for total, (c_re, c_im, c_tail, c_turn, c_valid) in zip(sums, columns):
                    add(total[s], 0, l_re * c_re + l_im * c_im)
                    add(total[s], 1, l_im * c_re - l_re * c_im)
                    add(total[s], 2, l_tail * c_tail)
                    add(total[s], 3, l_tail * c_turn)
                    add(total[s], 4, l_valid * c_valid)
    low_lanes = iota((8, LANE), 1) < HALF
    out = []
    for total in sums:
        piece = []
        for re, im, straight, turned, count in total:
            straight = straight + pltpu.roll(straight, HALF, 1)
            turned = turned - pltpu.roll(turned, HALF, 1)
            all_lanes = [re, im, jnp.where(low_lanes, straight, turned), count]
            piece.append([v + pltpu.roll(v, 4, 0) for v in all_lanes])
        out.append(piece)
    return out


def store_sums(per, ref, i, pieces):
    for s, sums in enumerate(pieces):
        at = (i * per + s) * 8
        for k in range(4):
            ref[at : at + 8, k * LANE : (k + 1) * LANE] = sums[k]


def load_sums(per, ref, i):
    rows = [ref[(i * per + s) * 8 : (i * per + s) * 8 + 8, :] for s in range(per)]
    return [[row[:, k * LANE : (k + 1) * LANE] for k in range(4)] for row in rows]


def ready_kernel(per, seg, mine_ref, spread_ref, sums_ref):
    lines = per * seg
    part, _ = divided(iota((lines, lines), 0), per)
    source = iota((lines, lines), 1)
    pick = [jnp.where(source == part * per + s, 1.0, 0.0).astype(BF16) for s in range(per)]
    spread = jnp.dot(jnp.concatenate(pick, axis=0), mine_ref[...], preferred_element_type=F32)
    spread_ref[:, : 2 * LANE] = spread[:, : 2 * LANE]
    tail = spread[:, 2 * LANE :]
    spread_ref[:, 2 * LANE : WIDE] = jnp.where(holds_tail(iota(tail.shape, 1)), tail, 0.0)
    valid = spread[:, 2 * LANE + VALID : 2 * LANE + VALID + 1]
    spread_ref[:, WIDE:] = jnp.broadcast_to(valid, (per * lines, LANE))
    store_sums(per, sums_ref, 0, stacked(per, lines, spread_ref, [mine_ref])[0])


def pass_kernel(_, near_ref, *refs):
    half = len(refs) // 2
    for src, dst in zip((near_ref, *refs[:half]), refs[half:]):
        dst[...] = src[...]


def place_of(name, grps, tiles):
    way, by = name
    tile = lax.axis_index("tile")
    odd = lax.rem(tile, 2)
    source = lax.rem(lax.axis_index("grp") + (grps - by), grps)
    kind = (0, 2 - odd, 1 + odd)[way]
    there = jnp.where(odd == 1, tile < tiles - 1, tile > 0) if way == 2 else None
    return 3 * source + kind, there


def over_count(rows):
    scale = 1.0 / jnp.maximum(rows[3], 1.0)
    return packed(*(row * scale for row in rows[:3]))


def put(names, grps, tiles, per, pieces, rows):
    places = [place_of(name, grps, tiles) for name in names]
    half = iota((8, WIDE), 0) >> 2
    blocks = 3 * grps // 2
    for b in range(blocks):
        for (place, there), piece in zip(places, pieces):
            fit = (half + 2 * b) == place
            fit = fit if there is None else fit & there
            for s in range(per):
                at = s * blocks + b
                rows[at] = jnp.where(fit, piece[s], rows[at])
    return rows


def early_kernel(per, seg, grps, tiles, names, mask_ref, spread_ref, mine_ref, *refs):
    *came, rows_ref, keep_ref, near_ref = refs
    keep = jnp.concatenate(column_of(mask_ref[...].astype(F32)), axis=0)
    keep_ref[...] = jnp.broadcast_to(keep, keep_ref.shape)
    lines = per * seg
    _, slot = divided(iota((LANE, lines), 1), per)
    to_slots = jnp.where(iota((LANE, lines), 0) == SLOT + slot, 1.0, 0.0).astype(BF16)
    same = divided(iota((lines, lines), 0), per)[0] == divided(iota((lines, lines), 1), per)[0]
    sums = [load_sums(per, mine_ref, 0)]
    for i, ref in enumerate(came):
        listed = jnp.dot(ref[:, 2 * LANE :], to_slots, preferred_element_type=F32)
        listed = jnp.where(same, listed, 0.0).astype(BF16)
        near_ref[i] = lax.dot_general(listed, ref[...], (((0,), (0,)), ((), ())), preferred_element_type=F32)
        sums += stacked(per, lines, spread_ref, [near_ref.at[i]])
    pieces = [[over_count(rows) for rows in piece] for piece in sums]
    rows = [jnp.zeros((8, WIDE), F32)] * (rows_ref.shape[0] // 8)
    rows_ref[...] = jnp.concatenate(put(((0, 0), *names), grps, tiles, per, pieces, rows), axis=0)


def middle_kernel(per, seg, grps, tiles, names, basis_ref, keep_ref, spread_ref, early_ref, *refs):
    *came, series_ref = refs
    pieces = [[over_count(rows) for rows in piece] for piece in stacked(per, per * seg, spread_ref, came)]
    rows = [early_ref[at : at + 8, :] for at in range(0, early_ref.shape[0], 8)]
    rows = put(names, grps, tiles, per, pieces, rows)
    left = [masked(row, keep_ref[8 * i : 8 * i + 8, :]) for i, row in enumerate(rows)]
    left = jnp.concatenate(left, axis=0).astype(BF16)
    series_ref[...] = jnp.dot(left, basis_ref[...], preferred_element_type=F32)


def masked(row, keep):
    return row * jnp.concatenate([keep] * (WIDE // LANE), axis=1)


def lags_kernel(per, seg, grps, tiles, names, basis_ref, keep_ref, spread_ref, series_ref, *refs):
    *came, out_ref, result, sems = refs
    blocks = 3 * grps // 2
    half = iota((8, WIDE), 0) >> 2
    left, places = [], []
    for i in range(0, grps, 2):
        one, two = stacked(per, per * seg, spread_ref, came[i : i + 2])
        (first, there), (second, _) = (place_of(name, grps, tiles) for name in names[i : i + 2])
        places.append((first, second, there))
        for s in range(per):
            row = jnp.where(half == (first & 1), over_count(one[s]), over_count(two[s]))
            keep = jnp.zeros((8, LANE), F32)
            for b in range(blocks):
                at = (s * blocks + b) * 8
                here = (half[:, :LANE] + 2 * b == first) | (half[:, :LANE] + 2 * b == second)
                keep = jnp.where(here, keep_ref[at : at + 8, :], keep)
            left.append(masked(row, keep))
    left = jnp.concatenate(left, axis=0).astype(BF16)
    copies = []
    for i, lo in enumerate(range(0, LAGS, LAG_STEP)):
        hi = min(lo + LAG_STEP, LAGS)
        late = jnp.dot(left, basis_ref[:, lo:hi], preferred_element_type=F32)
        half = iota((8, hi - lo), 0) >> 2
        for s in range(per):
            rows = []
            for b in range(blocks):
                at = (s * blocks + b) * 8
                row = series_ref[at : at + 8, lo:hi]
                for p, (first, second, there) in enumerate(places):
                    here = ((half + 2 * b == first) | (half + 2 * b == second)) & there
                    row = jnp.where(here, late[(p * per + s) * 8 : (p * per + s) * 8 + 8], row)
                rows.append(row)
            result[s, :, lo:hi] = jnp.concatenate(rows, axis=0).astype(BF16)
        here = (slice(None), slice(None), slice(lo, hi))
        copies.append(pltpu.make_async_copy(result.at[here], out_ref.at[here], sems.at[i]))
        copies[-1].start()
    for copy in copies:
        copy.wait()


def solution(mesh):
    tiles, grps = mesh.shape["tile"], mesh.shape["grp"]
    axes = ("tile", "grp")
    vmem = pl.BlockSpec(memory_space=pltpu.VMEM)
    hbm = pl.BlockSpec(memory_space=pltpu.HBM)
    placed = pltpu.with_memory_space_constraint

    def exchange(array, way, by):
        pairs = []
        for t in range(tiles):
            to = (t, t ^ 1, ((t + 1) ^ 1) - 1)[way]
            for g in range(grps):
                if 0 <= to < tiles:
                    goal = to * grps + (g + by) % grps
                else:
                    goal = t * grps + (g + max(by, 1)) % grps
                pairs.append((t * grps + g, goal))
        return lax.ppermute(array, axes, pairs)

    def call(kernel, name, inputs, **kw):
        return pl.pallas_call(
            kernel,
            in_specs=[vmem] * len(inputs),
            compiler_params=pltpu.CompilerParams(vmem_limit_bytes=32 << 20),
            name=name,
            **kw,
        )(*[placed(x, pltpu.VMEM) for x in inputs])

    def on_device(traces, validity, boundary_rows, boundary_count, pair_mask):
        per, seg, samples = traces.shape
        lines = per * seg
        columns = pair_mask.shape[1]
        factors, starts, stretches = fourier_tables(samples)
        lag_basis = jnp.asarray(lag_table(samples))
        payload = pltpu.VMEM((lines, WIDE), BF16)
        sent = [(3, d) for d in range(1, grps)] + [(2, d) for d in reversed(range(grps))]
        soon = [(1, d) for d in range(1, grps)]
        late = [(2, d) for d in reversed(range(grps))] + [(1, 0)] + [(0, d) for d in range(1, grps)]
        inputs = [boundary_rows, boundary_count, validity, traces.reshape(lines, samples), jnp.asarray(factors), lag_basis, pair_mask]
        mine, near, *rest, basis, mask = pl.pallas_call(
            lambda *refs: spectra_kernel(
                per, seg, samples, [1] + [way for way, _ in sent], starts, stretches, *refs
            ),
            out_shape=(payload,) * (2 + len(sent))
            + (pltpu.VMEM(lag_basis.shape, BF16), pltpu.VMEM(pair_mask.shape, jnp.int32)),
            in_specs=[hbm] * len(inputs),
            out_specs=(vmem,) * (4 + len(sent)),
            scratch_shapes=[
                pltpu.SMEM(boundary_rows.shape, jnp.int32),
                pltpu.SMEM(boundary_count.shape, jnp.int32),
                pltpu.VMEM(validity.shape, jnp.int32),
                pltpu.VMEM((lines, samples), F32),
                pltpu.VMEM(factors.shape, F32),
                pltpu.VMEM((per, seg, WIDE), F32),
                pltpu.VMEM((3, lines, LANE), F32),
                pltpu.SemaphoreType.DMA((7,)),
            ],
            compiler_params=pltpu.CompilerParams(vmem_limit_bytes=32 << 20),
            name="spectra",
        )(*[placed(x, pltpu.HBM) for x in inputs])
        came = [exchange(array, min(way, 4 - way), by) for (way, by), array in zip(sent, rest)]
        aside, far = came[: grps - 1], came[grps - 1 :]
        rows = per * columns
        spread, first = call(
            lambda *refs: ready_kernel(per, seg, *refs),
            "ready",
            [mine],
            out_shape=(
                pltpu.VMEM((per * lines, WIDE + LANE), F32),
                pltpu.VMEM((per * 8, WIDE + LANE), F32),
            ),
            out_specs=(vmem,) * 2,
        )
        passed = call(
            pass_kernel,
            "pass",
            [first, near, *aside],
            out_shape=(payload,) * grps,
            out_specs=(vmem,) * grps,
        )
        passed = [exchange(array, 1, 0) for array in passed]
        early, keep = call(
            lambda *refs: early_kernel(per, seg, grps, tiles, soon, *refs),
            "early",
            [mask, spread, first, *aside],
            out_shape=(pltpu.VMEM((rows, WIDE), F32), pltpu.VMEM((rows, LANE), F32)),
            out_specs=(vmem,) * 2,
            scratch_shapes=[pltpu.VMEM((max(len(soon), 1), lines, WIDE), F32)],
            cost_estimate=pl.CostEstimate(flops=100000000000, transcendentals=0, bytes_accessed=1000000000),
        )
        series = call(
            lambda *refs: middle_kernel(per, seg, grps, tiles, late[grps:], *refs),
            "middle",
            [basis, keep, spread, early, *passed],
            out_shape=pltpu.VMEM((rows, LAGS), F32),
            out_specs=vmem,
        )
        return call(
            lambda *refs: lags_kernel(per, seg, grps, tiles, late[:grps], *refs),
            "lags",
            [basis, keep, spread, series, *far],
            out_shape=jax.ShapeDtypeStruct((per, columns, LAGS), BF16),
            out_specs=hbm,
            scratch_shapes=[
                pltpu.VMEM((per, columns, LAGS), BF16),
                pltpu.SemaphoreType.DMA((pl.cdiv(LAGS, LAG_STEP),)),
            ],
        )

    return jax.shard_map(
        on_device,
        mesh=mesh,
        in_specs=(P(axes, None, None), P(axes, None), P(axes, None, None), P(axes, None), P(axes, None)),
        out_specs=P(axes, None, None),
        check_vma=False,
    )
```

```python
import numpy as np
import ml_dtypes

import jax
import jax.numpy as jnp
from jax import lax
from jax.experimental import pallas as pl
from jax.experimental.pallas import tpu as pltpu
from jax.sharding import PartitionSpec as P

NBIN = 144
MAXLAG = 1000
LAGS = 2001
LANE = 128
TAIL = NBIN - LANE
HALF = 64
LAST = ((0, 1), (1, 0))
TOGETHER = 2
VALID = 16
SLOT = 24
WIDE = 3 * LANE
LAG_STEP = 4 * LANE
STEP = 2 * LANE
FINE = 16
F32 = jnp.float32
BF16 = jnp.bfloat16


def split(table):
    high = table.astype(ml_dtypes.bfloat16)
    low = (table - high.astype(np.float64)).astype(ml_dtypes.bfloat16)
    return high, low


def in_lanes(real, imag):
    out = np.zeros((real.shape[0], WIDE))
    out[:, :LANE] = real[:, :LANE]
    out[:, LANE : 2 * LANE] = imag[:, :LANE]
    out[:, 2 * LANE : 2 * LANE + TAIL] = real[:, LANE:]
    out[:, 2 * LANE + HALF : 2 * LANE + HALF + TAIL] = imag[:, LANE:]
    return out


def round_to(rows):
    return -(-rows // 8) * 8


def fourier_rows(samples):
    stretches = -(-samples // STEP)
    sizes = [round_to(stretches)] * 3 + [STEP // FINE] * 2 + [FINE] * 2
    return [sum(sizes[:i]) for i in range(len(sizes) + 1)], stretches


def cos_sin(number, points):
    number = number - points * jnp.floor((number + 0.5) * (1.0 / points))
    turn = jnp.floor(number * (4.0 / points) + 0.5)
    angle = (number - turn * (points / 4)) * (2.0 * np.pi / points)
    square = angle * angle
    sine = 1.0 / 120 + square * (-1.0 / 5040 + square * (1.0 / 362880))
    sine = angle + angle * square * (-1.0 / 6 + square * sine)
    cosine = 1.0 / 24 + square * (-1.0 / 720 + square * (1.0 / 40320))
    cosine = 1.0 + square * (-0.5 + square * cosine)
    odd = (turn == 1) | (turn == 3)
    cosine, sine = jnp.where(odd, sine, cosine), jnp.where(odd, cosine, sine)
    cosine = jnp.where((turn == 1) | (turn == 2), -cosine, cosine)
    return cosine, jnp.where((turn == 2) | (turn == 3), -sine, sine)


def fill_factors(factors, starts, samples):
    points = 2 * samples

    def of(rows, step):
        lane = iota((rows, WIDE), 1)
        tail = lane & (HALF - 1)
        known = (lane < 2 * LANE) | (tail < TAIL)
        imag = ((lane >= LANE) & (lane < 2 * LANE)) | (lane >= 2 * LANE + HALF)
        bins = jnp.where(lane < 2 * LANE, lane & (LANE - 1), LANE + tail) + 1
        cosine, sine = cos_sin((iota((rows, WIDE), 0) * step * bins).astype(F32), points)
        return cosine, sine, imag, known

    def put_rows(i, rows):
        factors[starts[i] : starts[i + 1], :] = rows

    cosine, sine, imag, _ = of(starts[1] - starts[0], STEP)
    put_rows(0, cosine)
    put_rows(1, jnp.where(imag, -sine, sine))
    rows = starts[3] - starts[2]
    number = iota((rows, WIDE), 0) * STEP + iota((rows, WIDE), 1)
    put_rows(2, 0.5 - 0.5 * cos_sin((2 * number).astype(F32), points)[0])
    cosine, sine, imag, known = of(STEP // FINE, FINE)
    put_rows(3, jnp.where(known, jnp.where(imag, -sine, cosine), 0.0))
    put_rows(4, jnp.where(known, jnp.where(imag, -cosine, -sine), 0.0))
    cosine, sine, _, _ = of(FINE, 1)
    put_rows(5, cosine)
    put_rows(6, sine)


def lag_table(samples):
    lags = np.arange(LAGS) - MAXLAG
    bins = np.arange(1, NBIN + 1)
    angle = np.mod(lags[:, None] * bins[None, :], 2 * samples) * (np.pi / samples)
    scale = 1.0 / np.sqrt(NBIN)
    high, low = split(in_lanes(scale * np.cos(angle), -scale * np.sin(angle)).T)
    lane = np.arange(LANE)
    tail = np.where(holds_tail(lane)[:, None], high[2 * LANE :], low[LANE : 2 * LANE])
    return np.concatenate([high[: 2 * LANE], tail])


def holds_tail(lane):
    return ((lane & (HALF - 1)) < TAIL) | (lane == VALID)


def packed(real, imag, tail):
    return jnp.concatenate([real, imag, jnp.where(holds_tail(iota(tail.shape, 1)), tail, imag)], axis=1)


def iota(shape, dim):
    return lax.broadcasted_iota(jnp.int32, shape, dim)


def divided(value, by):
    if by & (by - 1) == 0:
        return value >> (by.bit_length() - 1), value & (by - 1)
    return lax.div(value, by), lax.rem(value, by)


def column_of(rows):
    n, m = rows.shape
    diagonal = iota((m, m), 0) == iota((m, m), 1)
    return [
        jnp.sum(jnp.where(diagonal, jnp.broadcast_to(rows[i : i + 1], (m, m)), 0.0), axis=1, keepdims=True)
        for i in range(n)
    ]


def spectra_kernel(
    per, seg, samples, ways, starts, stretches, rows_hbm, count_hbm, valid_hbm, traces_hbm, basis_hbm, mask_hbm,
    *refs,
):
    mine_ref, *outs, basis_ref, mask_ref, rows_ref, count_ref, valid_ref, traces, factors, table, window, white_ref, order_ref, sems = refs
    lines = per * seg
    pairs = [
        (traces_hbm, traces),
        (rows_hbm, rows_ref), (count_hbm, count_ref), (valid_hbm, valid_ref), (basis_hbm, basis_ref), (mask_hbm, mask_ref),
    ]
    copies = [pltpu.make_async_copy(src, dst, sems.at[i]) for i, (src, dst) in enumerate(pairs)]
    for copy in copies:
        copy.start()

    odd = lax.rem(lax.axis_index("tile"), 2)
    col = iota((STEP, STEP), 0)
    row = iota((STEP, STEP), 1)

    def bin_of(lane):
        tail = lane & (HALF - 1)
        known = (lane < LANE) | (tail < TAIL)
        return known, jnp.where(lane < LANE, lane, LANE + tail)

    known_in, bin_in = bin_of(col)
    known_out, bin_out = bin_of(row)
    near_bins = jnp.abs(bin_in - bin_out) <= 4
    window[...] = jnp.where(known_in & known_out, jnp.where(near_bins, 17.0, 1.0), 0.0).astype(BF16)

    fill_factors(factors, starts, samples)
    turn_at, swap_at, taper_at, coarse_at, cross_at, fine_at, other_at = starts[:-1]
    fine, other = factors[fine_at : fine_at + FINE, :], factors[other_at : other_at + FINE, :]
    for i in range(STEP // FINE):
        rows = factors[coarse_at + i : coarse_at + i + 1, :] * fine
        rows = rows + factors[cross_at + i : cross_at + i + 1, :] * other
        high = rows.astype(BF16)
        low = (rows - high.astype(F32)).astype(BF16)
        for k, part in enumerate((high, high, low)):
            table[k * STEP + i * FINE : k * STEP + (i + 1) * FINE, :] = part

    for copy in copies[1:4]:
        copy.wait()
    station, _ = divided(iota((lines, LANE), 0), seg)
    extra = jnp.zeros((lines, LANE), F32)
    for j in range(per):
        listed = (station == rows_ref[0, odd, j]) & (j < count_ref[0, odd])
        extra = jnp.where((iota((lines, LANE), 1) == SLOT + j) & listed, 1.0, extra)
    usable = jnp.concatenate(column_of(valid_ref[...].astype(F32)), axis=0)

    copies[0].wait()
    left = []
    for j in range(stretches):
        at = j * STEP
        x = traces[:, at : min(at + STEP, samples)]
        if at + STEP > samples:
            x = jnp.concatenate([x, jnp.zeros((lines, at + STEP - samples), F32)], axis=1)
        x = x * factors[taper_at + j : taper_at + j + 1, :STEP]
        x_high = x.astype(BF16)
        x_low = (x - x_high.astype(F32)).astype(BF16)
        left.append(jnp.concatenate([x_high, x_low, x_high], axis=1))
    parts = jnp.dot(jnp.concatenate(left, axis=0), table[...], preferred_element_type=F32)
    real, imag, tail = (parts[:lines, k * LANE : (k + 1) * LANE] for k in range(3))
    for j in range(1, stretches):
        p_re, p_im, p_tail = (parts[j * lines : (j + 1) * lines, k * LANE : (k + 1) * LANE] for k in range(3))
        turn = factors[turn_at + j : turn_at + j + 1, :]
        swap = factors[swap_at + j : swap_at + j + 1, :]
        real = real + p_re * turn[:, :LANE] + p_im * swap[:, :LANE]
        imag = imag + p_im * turn[:, LANE : 2 * LANE] + p_re * swap[:, LANE : 2 * LANE]
        tail = tail + p_tail * turn[:, 2 * LANE :] + pltpu.roll(p_tail, HALF, 1) * swap[:, 2 * LANE :]

    power = jnp.concatenate([real * real + imag * imag, tail * tail], axis=1)
    p_high = power.astype(BF16)
    p_low = (power - p_high.astype(F32)).astype(BF16)
    level = jnp.dot(p_high, window[...], preferred_element_type=F32)
    level = level + jnp.dot(p_low, window[...], preferred_element_type=F32)
    factor = usable / jnp.sqrt(level * (1.0 / (2 * NBIN)) + 1e-06)
    tail = tail * factor[:, LANE:]
    tail = jnp.where(iota((lines, LANE), 1) == VALID, usable, tail) + extra
    white = jnp.concatenate([real * factor[:, :LANE], imag * factor[:, :LANE], tail], axis=1)
    white_ref[...] = white.reshape(per, seg, WIDE)

    def ordered(direction):
        for j in range(per):
            if direction is None:
                rows = white_ref[j]
            else:
                rows = white_ref[rows_ref[0, direction, j]]
                rows = jnp.where(j < count_ref[0, direction], rows, 0.0)
            for k in range(3):
                order_ref[k, pl.ds(j, seg, stride=per), :] = rows[:, k * LANE : (k + 1) * LANE]
        return jnp.concatenate([order_ref[k] for k in range(3)], axis=1).astype(BF16)

    own, near, far = ordered(None), ordered(odd), ordered(1 - odd)
    mine_ref[...] = own
    for ref, way in zip(outs, ways):
        ref[...] = (own, near, far, own)[way]
    for copy in copies[4:]:
        copy.wait()


def stacked(per, lines, spread, refs):
    sums = [[[None] * 5 for _ in range(per)] for _ in refs]

    def add(total, i, value):
        total[i] = value if total[i] is None else total[i] + value

    for at in range(0, lines, 16):
        both = [ref[at : at + 16, :].astype(F32) for ref in refs]
        for half in range(2):
            columns = []
            for x in both:
                one = x[8 * half : 8 * half + 8]
                c_re, c_im, c_tail = one[:, :LANE], one[:, LANE : 2 * LANE], one[:, 2 * LANE :]
                c_valid = jnp.broadcast_to(c_tail[:, VALID : VALID + 1], c_tail.shape)
                columns.append((c_re, c_im, c_tail, pltpu.roll(c_tail, HALF, 1), c_valid))
            for s in range(per):
                here = s * lines + at + 8 * half
                left = spread[here : here + 8, :]
                l_re, l_im, l_tail, l_valid = (left[:, k * LANE : (k + 1) * LANE] for k in range(4))
                for total, (c_re, c_im, c_tail, c_turn, c_valid) in zip(sums, columns):
                    add(total[s], 0, l_re * c_re + l_im * c_im)
                    add(total[s], 1, l_im * c_re - l_re * c_im)
                    add(total[s], 2, l_tail * c_tail)
                    add(total[s], 3, l_tail * c_turn)
                    add(total[s], 4, l_valid * c_valid)
    low_lanes = iota((8, LANE), 1) < HALF
    out = []
    for total in sums:
        piece = []
        for re, im, straight, turned, count in total:
            straight = straight + pltpu.roll(straight, HALF, 1)
            turned = turned - pltpu.roll(turned, HALF, 1)
            all_lanes = [re, im, jnp.where(low_lanes, straight, turned), count]
            piece.append([v + pltpu.roll(v, 4, 0) for v in all_lanes])
        out.append(piece)
    return out


def store_sums(per, ref, i, pieces):
    for s, sums in enumerate(pieces):
        at = (i * per + s) * 8
        for k in range(4):
            ref[at : at + 8, k * LANE : (k + 1) * LANE] = sums[k]


def load_sums(per, ref, i):
    rows = [ref[(i * per + s) * 8 : (i * per + s) * 8 + 8, :] for s in range(per)]
    return [[row[:, k * LANE : (k + 1) * LANE] for k in range(4)] for row in rows]


def ready_kernel(per, seg, mine_ref, spread_ref, sums_ref):
    lines = per * seg
    part, _ = divided(iota((lines, lines), 0), per)
    source = iota((lines, lines), 1)
    pick = [jnp.where(source == part * per + s, 1.0, 0.0).astype(BF16) for s in range(per)]
    spread = jnp.dot(jnp.concatenate(pick, axis=0), mine_ref[...], preferred_element_type=F32)
    spread_ref[:, : 2 * LANE] = spread[:, : 2 * LANE]
    tail = spread[:, 2 * LANE :]
    spread_ref[:, 2 * LANE : WIDE] = jnp.where(holds_tail(iota(tail.shape, 1)), tail, 0.0)
    valid = spread[:, 2 * LANE + VALID : 2 * LANE + VALID + 1]
    spread_ref[:, WIDE:] = jnp.broadcast_to(valid, (per * lines, LANE))
    store_sums(per, sums_ref, 0, stacked(per, lines, spread_ref, [mine_ref])[0])


def pass_kernel(_, near_ref, *refs):
    half = len(refs) // 2
    for src, dst in zip((near_ref, *refs[:half]), refs[half:]):
        dst[...] = src[...]


def place_of(name, grps, tiles):
    way, by = name
    tile = lax.axis_index("tile")
    odd = lax.rem(tile, 2)
    source = lax.rem(lax.axis_index("grp") + (grps - by), grps)
    kind = (0, 2 - odd, 1 + odd)[way]
    there = jnp.where(odd == 1, tile < tiles - 1, tile > 0) if way == 2 else None
    return 3 * source + kind, there


def over_count(rows):
    scale = 1.0 / jnp.maximum(rows[3], 1.0)
    return packed(*(row * scale for row in rows[:3]))


def put(names, grps, tiles, per, pieces, rows):
    places = [place_of(name, grps, tiles) for name in names]
    half = iota((8, WIDE), 0) >> 2
    blocks = 3 * grps // 2
    for b in range(blocks):
        for (place, there), piece in zip(places, pieces):
            fit = (half + 2 * b) == place
            fit = fit if there is None else fit & there
            for s in range(per):
                at = s * blocks + b
                rows[at] = jnp.where(fit, piece[s], rows[at])
    return rows


def early_kernel(per, seg, grps, tiles, names, mask_ref, spread_ref, mine_ref, *refs):
    *came, rows_ref, keep_ref, near_ref = refs
    keep = jnp.concatenate(column_of(mask_ref[...].astype(F32)), axis=0)
    keep_ref[...] = jnp.broadcast_to(keep, keep_ref.shape)
    lines = per * seg
    _, slot = divided(iota((LANE, lines), 1), per)
    to_slots = jnp.where(iota((LANE, lines), 0) == SLOT + slot, 1.0, 0.0).astype(BF16)
    same = divided(iota((lines, lines), 0), per)[0] == divided(iota((lines, lines), 1), per)[0]
    sums = [load_sums(per, mine_ref, 0)]
    for i, ref in enumerate(came):
        listed = jnp.dot(ref[:, 2 * LANE :], to_slots, preferred_element_type=F32)
        listed = jnp.where(same, listed, 0.0).astype(BF16)
        near_ref[i] = lax.dot_general(listed, ref[...], (((0,), (0,)), ((), ())), preferred_element_type=F32)
        sums += stacked(per, lines, spread_ref, [near_ref.at[i]])
    pieces = [[over_count(rows) for rows in piece] for piece in sums]
    rows = [jnp.zeros((8, WIDE), F32)] * (rows_ref.shape[0] // 8)
    rows_ref[...] = jnp.concatenate(put(((0, 0), *names), grps, tiles, per, pieces, rows), axis=0)


def middle_kernel(per, seg, grps, tiles, names, basis_ref, keep_ref, spread_ref, early_ref, *refs):
    *came, series_ref = refs
    pieces = [[over_count(rows) for rows in piece] for piece in stacked(per, per * seg, spread_ref, came)]
    rows = [early_ref[at : at + 8, :] for at in range(0, early_ref.shape[0], 8)]
    rows = put(names, grps, tiles, per, pieces, rows)
    left = [masked(row, keep_ref[8 * i : 8 * i + 8, :]) for i, row in enumerate(rows)]
    left = jnp.concatenate(left, axis=0).astype(BF16)
    series_ref[...] = jnp.dot(left, basis_ref[...], preferred_element_type=F32)


def masked(row, keep):
    return row * jnp.concatenate([keep] * (WIDE // LANE), axis=1)


def lags_kernel(per, seg, grps, tiles, names, basis_ref, keep_ref, spread_ref, series_ref, *refs):
    *came, out_ref, result, sems = refs
    blocks = 3 * grps // 2
    half = iota((8, WIDE), 0) >> 2
    left, places = [], []
    for i in range(0, grps, 2):
        one, two = stacked(per, per * seg, spread_ref, came[i : i + 2])
        (first, there), (second, _) = (place_of(name, grps, tiles) for name in names[i : i + 2])
        places.append((first, second, there))
        for s in range(per):
            row = jnp.where(half == (first & 1), over_count(one[s]), over_count(two[s]))
            keep = jnp.zeros((8, LANE), F32)
            for b in range(blocks):
                at = (s * blocks + b) * 8
                here = (half[:, :LANE] + 2 * b == first) | (half[:, :LANE] + 2 * b == second)
                keep = jnp.where(here, keep_ref[at : at + 8, :], keep)
            left.append(masked(row, keep))
    left = jnp.concatenate(left, axis=0).astype(BF16)
    copies = []
    for i, lo in enumerate(range(0, LAGS, LAG_STEP)):
        hi = min(lo + LAG_STEP, LAGS)
        late = jnp.dot(left, basis_ref[:, lo:hi], preferred_element_type=F32)
        half = iota((8, hi - lo), 0) >> 2
        for s in range(per):
            rows = []
            for b in range(blocks):
                at = (s * blocks + b) * 8
                row = series_ref[at : at + 8, lo:hi]
                for p, (first, second, there) in enumerate(places):
                    here = ((half + 2 * b == first) | (half + 2 * b == second)) & there
                    row = jnp.where(here, late[(p * per + s) * 8 : (p * per + s) * 8 + 8], row)
                rows.append(row)
            result[s, :, lo:hi] = jnp.concatenate(rows, axis=0).astype(BF16)
        here = (slice(None), slice(None), slice(lo, hi))
        copies.append(pltpu.make_async_copy(result.at[here], out_ref.at[here], sems.at[i]))
        copies[-1].start()
    for copy in copies:
        copy.wait()


def solution(mesh):
    tiles, grps = mesh.shape["tile"], mesh.shape["grp"]
    axes = ("tile", "grp")
    vmem = pl.BlockSpec(memory_space=pltpu.VMEM)
    hbm = pl.BlockSpec(memory_space=pltpu.HBM)
    placed = pltpu.with_memory_space_constraint

    def exchange(array, way, by):
        pairs = []
        for t in range(tiles):
            to = (t, t ^ 1, ((t + 1) ^ 1) - 1)[way]
            for g in range(grps):
                if 0 <= to < tiles:
                    goal = to * grps + (g + by) % grps
                else:
                    goal = t * grps + (g + max(by, 1)) % grps
                pairs.append((t * grps + g, goal))
        return lax.ppermute(array, axes, pairs)

    def call(kernel, name, inputs, **kw):
        return pl.pallas_call(
            kernel,
            in_specs=[vmem] * len(inputs),
            compiler_params=pltpu.CompilerParams(vmem_limit_bytes=32 << 20),
            name=name,
            **kw,
        )(*[placed(x, pltpu.VMEM) for x in inputs])

    def on_device(traces, validity, boundary_rows, boundary_count, pair_mask):
        per, seg, samples = traces.shape
        lines = per * seg
        columns = pair_mask.shape[1]
        starts, stretches = fourier_rows(samples)
        lag_basis = jnp.asarray(lag_table(samples))
        payload = pltpu.VMEM((lines, WIDE), BF16)
        sent = [(3, d) for d in range(1, grps)] + [(2, d) for d in reversed(range(grps))]
        soon = [(1, d) for d in range(1, grps)]
        late = [(2, d) for d in reversed(range(grps))] + [(1, 0)] + [(0, d) for d in range(1, grps)]
        inputs = [boundary_rows, boundary_count, validity, traces.reshape(lines, samples), lag_basis, pair_mask]
        mine, near, *rest, basis, mask = pl.pallas_call(
            lambda *refs: spectra_kernel(
                per, seg, samples, [1] + [way for way, _ in sent], starts, stretches, *refs
            ),
            out_shape=(payload,) * (2 + len(sent))
            + (pltpu.VMEM(lag_basis.shape, BF16), pltpu.VMEM(pair_mask.shape, jnp.int32)),
            in_specs=[hbm] * len(inputs),
            out_specs=(vmem,) * (4 + len(sent)),
            scratch_shapes=[
                pltpu.SMEM(boundary_rows.shape, jnp.int32),
                pltpu.SMEM(boundary_count.shape, jnp.int32),
                pltpu.VMEM(validity.shape, jnp.int32),
                pltpu.VMEM((lines, samples), F32),
                pltpu.VMEM((starts[-1], WIDE), F32),
                pltpu.VMEM((3 * STEP, WIDE), BF16),
                pltpu.VMEM((2 * LANE, 2 * LANE), BF16),
                pltpu.VMEM((per, seg, WIDE), F32),
                pltpu.VMEM((3, lines, LANE), F32),
                pltpu.SemaphoreType.DMA((6,)),
            ],
            compiler_params=pltpu.CompilerParams(vmem_limit_bytes=32 << 20),
            name="spectra",
        )(*[placed(x, pltpu.HBM) for x in inputs])
        came = [exchange(array, min(way, 4 - way), by) for (way, by), array in zip(sent, rest)]
        aside, far = came[: grps - 1], came[grps - 1 :]
        rows = per * columns
        spread, first = call(
            lambda *refs: ready_kernel(per, seg, *refs),
            "ready",
            [mine],
            out_shape=(
                pltpu.VMEM((per * lines, WIDE + LANE), F32),
                pltpu.VMEM((per * 8, WIDE + LANE), F32),
            ),
            out_specs=(vmem,) * 2,
        )
        passed = call(
            pass_kernel,
            "pass",
            [first, near, *aside],
            out_shape=(payload,) * grps,
            out_specs=(vmem,) * grps,
        )
        passed = [exchange(array, 1, 0) for array in passed]
        early, keep = call(
            lambda *refs: early_kernel(per, seg, grps, tiles, soon, *refs),
            "early",
            [mask, spread, first, *aside],
            out_shape=(pltpu.VMEM((rows, WIDE), F32), pltpu.VMEM((rows, LANE), F32)),
            out_specs=(vmem,) * 2,
            scratch_shapes=[pltpu.VMEM((max(len(soon), 1), lines, WIDE), F32)],
            cost_estimate=pl.CostEstimate(flops=100000000000, transcendentals=0, bytes_accessed=1000000000),
        )
        series = call(
            lambda *refs: middle_kernel(per, seg, grps, tiles, late[grps:], *refs),
            "middle",
            [basis, keep, spread, early, *passed],
            out_shape=pltpu.VMEM((rows, LAGS), F32),
            out_specs=vmem,
        )
        return call(
            lambda *refs: lags_kernel(per, seg, grps, tiles, late[:grps], *refs),
            "lags",
            [basis, keep, spread, series, *far],
            out_shape=jax.ShapeDtypeStruct((per, columns, LAGS), BF16),
            out_specs=hbm,
            scratch_shapes=[
                pltpu.VMEM((per, columns, LAGS), BF16),
                pltpu.SemaphoreType.DMA((pl.cdiv(LAGS, LAG_STEP),)),
            ],
        )

    return jax.shard_map(
        on_device,
        mesh=mesh,
        in_specs=(P(axes, None, None), P(axes, None), P(axes, None, None), P(axes, None), P(axes, None)),
        out_specs=P(axes, None, None),
        check_vma=False,
    )
```

```python
import numpy as np
import ml_dtypes

import jax
import jax.numpy as jnp
from jax import lax
from jax.experimental import pallas as pl
from jax.experimental.pallas import tpu as pltpu
from jax.sharding import PartitionSpec as P

NBIN = 144
MAXLAG = 1000
LAGS = 2001
LANE = 128
TAIL = NBIN - LANE
HALF = 64
LAST = ((0, 1), (1, 0))
TOGETHER = 2
VALID = 16
SLOT = 24
WIDE = 3 * LANE
LAG_STEP = 6 * LANE
STEP = 4 * LANE
FINE = 16
F32 = jnp.float32
BF16 = jnp.bfloat16


def split(table):
    high = table.astype(ml_dtypes.bfloat16)
    low = (table - high.astype(np.float64)).astype(ml_dtypes.bfloat16)
    return high, low


def in_lanes(real, imag):
    out = np.zeros((real.shape[0], WIDE))
    out[:, :LANE] = real[:, :LANE]
    out[:, LANE : 2 * LANE] = imag[:, :LANE]
    out[:, 2 * LANE : 2 * LANE + TAIL] = real[:, LANE:]
    out[:, 2 * LANE + HALF : 2 * LANE + HALF + TAIL] = imag[:, LANE:]
    return out


def round_to(rows):
    return -(-rows // 8) * 8


def fourier_rows(samples):
    stretches = -(-samples // STEP)
    sizes = [round_to(stretches)] * 2 + [round_to(stretches * STEP // LANE)] + [STEP // FINE] * 2 + [FINE] * 2
    return [sum(sizes[:i]) for i in range(len(sizes) + 1)], stretches


def cos_sin(number, points):
    number = number - points * jnp.floor((number + 0.5) * (1.0 / points))
    turn = jnp.floor(number * (4.0 / points) + 0.5)
    angle = (number - turn * (points / 4)) * (2.0 * np.pi / points)
    square = angle * angle
    sine = 1.0 / 120 + square * (-1.0 / 5040 + square * (1.0 / 362880))
    sine = angle + angle * square * (-1.0 / 6 + square * sine)
    cosine = 1.0 / 24 + square * (-1.0 / 720 + square * (1.0 / 40320))
    cosine = 1.0 + square * (-0.5 + square * cosine)
    odd = (turn == 1) | (turn == 3)
    cosine, sine = jnp.where(odd, sine, cosine), jnp.where(odd, cosine, sine)
    cosine = jnp.where((turn == 1) | (turn == 2), -cosine, cosine)
    return cosine, jnp.where((turn == 2) | (turn == 3), -sine, sine)


def fill_factors(factors, starts, samples):
    points = 2 * samples

    def of(rows, step):
        lane = iota((rows, WIDE), 1)
        tail = lane & (HALF - 1)
        known = (lane < 2 * LANE) | (tail < TAIL)
        imag = ((lane >= LANE) & (lane < 2 * LANE)) | (lane >= 2 * LANE + HALF)
        bins = jnp.where(lane < 2 * LANE, lane & (LANE - 1), LANE + tail) + 1
        cosine, sine = cos_sin((iota((rows, WIDE), 0) * step * bins).astype(F32), points)
        return cosine, sine, imag, known

    def put_rows(i, rows):
        factors[starts[i] : starts[i + 1], :] = rows

    cosine, sine, imag, _ = of(starts[1] - starts[0], STEP)
    put_rows(0, cosine)
    put_rows(1, jnp.where(imag, -sine, sine))
    rows = starts[3] - starts[2]
    number = iota((rows, WIDE), 0) * LANE + iota((rows, WIDE), 1)
    put_rows(2, 0.5 - 0.5 * cos_sin((2 * number).astype(F32), points)[0])
    cosine, sine, imag, known = of(STEP // FINE, FINE)
    put_rows(3, jnp.where(known, jnp.where(imag, -sine, cosine), 0.0))
    put_rows(4, jnp.where(known, jnp.where(imag, -cosine, -sine), 0.0))
    cosine, sine, _, _ = of(FINE, 1)
    put_rows(5, cosine)
    put_rows(6, sine)


def lag_table(samples):
    lags = np.arange(LAGS) - MAXLAG
    bins = np.arange(1, NBIN + 1)
    angle = np.mod(lags[:, None] * bins[None, :], 2 * samples) * (np.pi / samples)
    scale = 1.0 / np.sqrt(NBIN)
    high, low = split(in_lanes(scale * np.cos(angle), -scale * np.sin(angle)).T)
    lane = np.arange(LANE)
    tail = np.where(holds_tail(lane)[:, None], high[2 * LANE :], low[LANE : 2 * LANE])
    return np.concatenate([high[: 2 * LANE], tail])


def holds_tail(lane):
    return ((lane & (HALF - 1)) < TAIL) | (lane == VALID)


def packed(real, imag, tail):
    return jnp.concatenate([real, imag, jnp.where(holds_tail(iota(tail.shape, 1)), tail, imag)], axis=1)


def iota(shape, dim):
    return lax.broadcasted_iota(jnp.int32, shape, dim)


def divided(value, by):
    if by & (by - 1) == 0:
        return value >> (by.bit_length() - 1), value & (by - 1)
    return lax.div(value, by), lax.rem(value, by)


def column_of(rows):
    n, m = rows.shape
    diagonal = iota((m, m), 0) == iota((m, m), 1)
    return [
        jnp.sum(jnp.where(diagonal, jnp.broadcast_to(rows[i : i + 1], (m, m)), 0.0), axis=1, keepdims=True)
        for i in range(n)
    ]


def spectra_kernel(
    per, seg, samples, ways, starts, stretches, rows_hbm, count_hbm, valid_hbm, traces_hbm, basis_hbm, mask_hbm,
    *refs,
):
    mine_ref, *outs, basis_ref, mask_ref, rows_ref, count_ref, valid_ref, traces, factors, table, window, white_ref, order_ref, sems = refs
    lines = per * seg
    pairs = [
        (traces_hbm, traces),
        (rows_hbm, rows_ref), (count_hbm, count_ref), (valid_hbm, valid_ref), (basis_hbm, basis_ref), (mask_hbm, mask_ref),
    ]
    copies = [pltpu.make_async_copy(src, dst, sems.at[i]) for i, (src, dst) in enumerate(pairs)]
    for copy in copies:
        copy.start()

    odd = lax.rem(lax.axis_index("tile"), 2)
    col = iota((2 * LANE, 2 * LANE), 0)
    row = iota((2 * LANE, 2 * LANE), 1)

    def bin_of(lane):
        tail = lane & (HALF - 1)
        known = (lane < LANE) | (tail < TAIL)
        return known, jnp.where(lane < LANE, lane, LANE + tail)

    known_in, bin_in = bin_of(col)
    known_out, bin_out = bin_of(row)
    near_bins = jnp.abs(bin_in - bin_out) <= 4
    window[...] = jnp.where(known_in & known_out, jnp.where(near_bins, 17.0, 1.0), 0.0).astype(BF16)

    fill_factors(factors, starts, samples)
    turn_at, swap_at, taper_at, coarse_at, cross_at, fine_at, other_at = starts[:-1]
    fine, other = factors[fine_at : fine_at + FINE, :], factors[other_at : other_at + FINE, :]
    for i in range(STEP // FINE):
        rows = factors[coarse_at + i : coarse_at + i + 1, :] * fine
        rows = rows + factors[cross_at + i : cross_at + i + 1, :] * other
        high = rows.astype(BF16)
        low = (rows - high.astype(F32)).astype(BF16)
        for k, part in enumerate((high, high, low)):
            table[k * STEP + i * FINE : k * STEP + (i + 1) * FINE, :] = part

    for copy in copies[1:4]:
        copy.wait()
    station, _ = divided(iota((lines, LANE), 0), seg)
    extra = jnp.zeros((lines, LANE), F32)
    for j in range(per):
        listed = (station == rows_ref[0, odd, j]) & (j < count_ref[0, odd])
        extra = jnp.where((iota((lines, LANE), 1) == SLOT + j) & listed, 1.0, extra)
    usable = jnp.concatenate(column_of(valid_ref[...].astype(F32)), axis=0)

    copies[0].wait()
    left = []
    for j in range(stretches):
        at = j * STEP
        x = traces[:, at : min(at + STEP, samples)]
        if at + STEP > samples:
            x = jnp.concatenate([x, jnp.zeros((lines, at + STEP - samples), F32)], axis=1)
        first = taper_at + at // LANE
        taper = [factors[first + i : first + i + 1, :LANE] for i in range(STEP // LANE)]
        x = x * jnp.concatenate(taper, axis=1)
        x_high = x.astype(BF16)
        x_low = (x - x_high.astype(F32)).astype(BF16)
        left.append(jnp.concatenate([x_high, x_low, x_high], axis=1))
    parts = jnp.dot(jnp.concatenate(left, axis=0), table[...], preferred_element_type=F32)
    real, imag, tail = (parts[:lines, k * LANE : (k + 1) * LANE] for k in range(3))
    for j in range(1, stretches):
        p_re, p_im, p_tail = (parts[j * lines : (j + 1) * lines, k * LANE : (k + 1) * LANE] for k in range(3))
        turn = factors[turn_at + j : turn_at + j + 1, :]
        swap = factors[swap_at + j : swap_at + j + 1, :]
        real = real + p_re * turn[:, :LANE] + p_im * swap[:, :LANE]
        imag = imag + p_im * turn[:, LANE : 2 * LANE] + p_re * swap[:, LANE : 2 * LANE]
        tail = tail + p_tail * turn[:, 2 * LANE :] + pltpu.roll(p_tail, HALF, 1) * swap[:, 2 * LANE :]

    power = jnp.concatenate([real * real + imag * imag, tail * tail], axis=1)
    p_high = power.astype(BF16)
    p_low = (power - p_high.astype(F32)).astype(BF16)
    level = jnp.dot(p_high, window[...], preferred_element_type=F32)
    level = level + jnp.dot(p_low, window[...], preferred_element_type=F32)
    factor = usable / jnp.sqrt(level * (1.0 / (2 * NBIN)) + 1e-06)
    tail = tail * factor[:, LANE:]
    tail = jnp.where(iota((lines, LANE), 1) == VALID, usable, tail) + extra
    white = jnp.concatenate([real * factor[:, :LANE], imag * factor[:, :LANE], tail], axis=1)
    white_ref[...] = white.reshape(per, seg, WIDE)

    def ordered(direction):
        for j in range(per):
            if direction is None:
                rows = white_ref[j]
            else:
                rows = white_ref[rows_ref[0, direction, j]]
                rows = jnp.where(j < count_ref[0, direction], rows, 0.0)
            for k in range(3):
                order_ref[k, pl.ds(j, seg, stride=per), :] = rows[:, k * LANE : (k + 1) * LANE]
        return jnp.concatenate([order_ref[k] for k in range(3)], axis=1).astype(BF16)

    own, near, far = ordered(None), ordered(odd), ordered(1 - odd)
    mine_ref[...] = own
    for ref, way in zip(outs, ways):
        ref[...] = (own, near, far, own)[way]
    for copy in copies[4:]:
        copy.wait()


def stacked(per, lines, spread, refs):
    sums = [[[None] * 5 for _ in range(per)] for _ in refs]

    def add(total, i, value):
        total[i] = value if total[i] is None else total[i] + value

    for at in range(0, lines, 16):
        both = [ref[at : at + 16, :].astype(F32) for ref in refs]
        for half in range(2):
            columns = []
            for x in both:
                one = x[8 * half : 8 * half + 8]
                c_re, c_im, c_tail = one[:, :LANE], one[:, LANE : 2 * LANE], one[:, 2 * LANE :]
                c_valid = jnp.broadcast_to(c_tail[:, VALID : VALID + 1], c_tail.shape)
                columns.append((c_re, c_im, c_tail, pltpu.roll(c_tail, HALF, 1), c_valid))
            for s in range(per):
                here = s * lines + at + 8 * half
                left = spread[here : here + 8, :]
                l_re, l_im, l_tail, l_valid = (left[:, k * LANE : (k + 1) * LANE] for k in range(4))
                for total, (c_re, c_im, c_tail, c_turn, c_valid) in zip(sums, columns):
                    add(total[s], 0, l_re * c_re + l_im * c_im)
                    add(total[s], 1, l_im * c_re - l_re * c_im)
                    add(total[s], 2, l_tail * c_tail)
                    add(total[s], 3, l_tail * c_turn)
                    add(total[s], 4, l_valid * c_valid)
    low_lanes = iota((8, LANE), 1) < HALF
    out = []
    for total in sums:
        piece = []
        for re, im, straight, turned, count in total:
            straight = straight + pltpu.roll(straight, HALF, 1)
            turned = turned - pltpu.roll(turned, HALF, 1)
            all_lanes = [re, im, jnp.where(low_lanes, straight, turned), count]
            piece.append([v + pltpu.roll(v, 4, 0) for v in all_lanes])
        out.append(piece)
    return out


def store_sums(per, ref, i, pieces):
    for s, sums in enumerate(pieces):
        at = (i * per + s) * 8
        for k in range(4):
            ref[at : at + 8, k * LANE : (k + 1) * LANE] = sums[k]


def load_sums(per, ref, i):
    rows = [ref[(i * per + s) * 8 : (i * per + s) * 8 + 8, :] for s in range(per)]
    return [[row[:, k * LANE : (k + 1) * LANE] for k in range(4)] for row in rows]


def ready_kernel(per, seg, mine_ref, spread_ref, sums_ref):
    lines = per * seg
    part, _ = divided(iota((lines, lines), 0), per)
    source = iota((lines, lines), 1)
    pick = [jnp.where(source == part * per + s, 1.0, 0.0).astype(BF16) for s in range(per)]
    spread = jnp.dot(jnp.concatenate(pick, axis=0), mine_ref[...], preferred_element_type=F32)
    spread_ref[:, : 2 * LANE] = spread[:, : 2 * LANE]
    tail = spread[:, 2 * LANE :]
    spread_ref[:, 2 * LANE : WIDE] = jnp.where(holds_tail(iota(tail.shape, 1)), tail, 0.0)
    valid = spread[:, 2 * LANE + VALID : 2 * LANE + VALID + 1]
    spread_ref[:, WIDE:] = jnp.broadcast_to(valid, (per * lines, LANE))
    store_sums(per, sums_ref, 0, stacked(per, lines, spread_ref, [mine_ref])[0])


def pass_kernel(_, near_ref, *refs):
    half = len(refs) // 2
    for src, dst in zip((near_ref, *refs[:half]), refs[half:]):
        dst[...] = src[...]


def place_of(name, grps, tiles):
    way, by = name
    tile = lax.axis_index("tile")
    odd = lax.rem(tile, 2)
    source = lax.rem(lax.axis_index("grp") + (grps - by), grps)
    kind = (0, 2 - odd, 1 + odd)[way]
    there = jnp.where(odd == 1, tile < tiles - 1, tile > 0) if way == 2 else None
    return 3 * source + kind, there


def over_count(rows):
    scale = 1.0 / jnp.maximum(rows[3], 1.0)
    return packed(*(row * scale for row in rows[:3]))


def put(names, grps, tiles, per, pieces, rows):
    places = [place_of(name, grps, tiles) for name in names]
    half = iota((8, WIDE), 0) >> 2
    blocks = 3 * grps // 2
    for b in range(blocks):
        for (place, there), piece in zip(places, pieces):
            fit = (half + 2 * b) == place
            fit = fit if there is None else fit & there
            for s in range(per):
                at = s * blocks + b
                rows[at] = jnp.where(fit, piece[s], rows[at])
    return rows


def early_kernel(per, seg, grps, tiles, names, mask_ref, spread_ref, mine_ref, *refs):
    *came, rows_ref, keep_ref, near_ref = refs
    keep = jnp.concatenate(column_of(mask_ref[...].astype(F32)), axis=0)
    keep_ref[...] = jnp.broadcast_to(keep, keep_ref.shape)
    lines = per * seg
    _, slot = divided(iota((LANE, lines), 1), per)
    to_slots = jnp.where(iota((LANE, lines), 0) == SLOT + slot, 1.0, 0.0).astype(BF16)
    same = divided(iota((lines, lines), 0), per)[0] == divided(iota((lines, lines), 1), per)[0]
    sums = [load_sums(per, mine_ref, 0)]
    for i, ref in enumerate(came):
        listed = jnp.dot(ref[:, 2 * LANE :], to_slots, preferred_element_type=F32)
        listed = jnp.where(same, listed, 0.0).astype(BF16)
        near_ref[i] = lax.dot_general(listed, ref[...], (((0,), (0,)), ((), ())), preferred_element_type=F32)
        sums += stacked(per, lines, spread_ref, [near_ref.at[i]])
    pieces = [[over_count(rows) for rows in piece] for piece in sums]
    rows = [jnp.zeros((8, WIDE), F32)] * (rows_ref.shape[0] // 8)
    rows_ref[...] = jnp.concatenate(put(((0, 0), *names), grps, tiles, per, pieces, rows), axis=0)


def middle_kernel(per, seg, grps, tiles, names, basis_ref, keep_ref, spread_ref, early_ref, *refs):
    *came, series_ref = refs
    pieces = [[over_count(rows) for rows in piece] for piece in stacked(per, per * seg, spread_ref, came)]
    rows = [early_ref[at : at + 8, :] for at in range(0, early_ref.shape[0], 8)]
    rows = put(names, grps, tiles, per, pieces, rows)
    left = [masked(row, keep_ref[8 * i : 8 * i + 8, :]) for i, row in enumerate(rows)]
    left = jnp.concatenate(left, axis=0).astype(BF16)
    series_ref[...] = jnp.dot(left, basis_ref[...], preferred_element_type=F32)


def masked(row, keep):
    return row * jnp.concatenate([keep] * (WIDE // LANE), axis=1)


def lags_kernel(per, seg, grps, tiles, names, basis_ref, keep_ref, spread_ref, series_ref, *refs):
    *came, out_ref, result, sems = refs
    blocks = 3 * grps // 2
    half = iota((8, WIDE), 0) >> 2
    left, places = [], []
    for i in range(0, grps, 2):
        one, two = stacked(per, per * seg, spread_ref, came[i : i + 2])
        (first, there), (second, _) = (place_of(name, grps, tiles) for name in names[i : i + 2])
        places.append((first, second, there))
        for s in range(per):
            row = jnp.where(half == (first & 1), over_count(one[s]), over_count(two[s]))
            keep = jnp.zeros((8, LANE), F32)
            for b in range(blocks):
                at = (s * blocks + b) * 8
                here = (half[:, :LANE] + 2 * b == first) | (half[:, :LANE] + 2 * b == second)
                keep = jnp.where(here, keep_ref[at : at + 8, :], keep)
            left.append(masked(row, keep))
    left = jnp.concatenate(left, axis=0).astype(BF16)
    copies = []
    for i, lo in enumerate(range(0, LAGS, LAG_STEP)):
        hi = min(lo + LAG_STEP, LAGS)
        late = jnp.dot(left, basis_ref[:, lo:hi], preferred_element_type=F32)
        half = iota((8, hi - lo), 0) >> 2
        for s in range(per):
            rows = []
            for b in range(blocks):
                at = (s * blocks + b) * 8
                row = series_ref[at : at + 8, lo:hi]
                for p, (first, second, there) in enumerate(places):
                    here = ((half + 2 * b == first) | (half + 2 * b == second)) & there
                    row = jnp.where(here, late[(p * per + s) * 8 : (p * per + s) * 8 + 8], row)
                rows.append(row)
            result[s, :, lo:hi] = jnp.concatenate(rows, axis=0).astype(BF16)
        here = (slice(None), slice(None), slice(lo, hi))
        copies.append(pltpu.make_async_copy(result.at[here], out_ref.at[here], sems.at[i]))
        copies[-1].start()
    for copy in copies:
        copy.wait()


def solution(mesh):
    tiles, grps = mesh.shape["tile"], mesh.shape["grp"]
    axes = ("tile", "grp")
    vmem = pl.BlockSpec(memory_space=pltpu.VMEM)
    hbm = pl.BlockSpec(memory_space=pltpu.HBM)
    placed = pltpu.with_memory_space_constraint

    def exchange(array, way, by):
        pairs = []
        for t in range(tiles):
            to = (t, t ^ 1, ((t + 1) ^ 1) - 1)[way]
            for g in range(grps):
                if 0 <= to < tiles:
                    goal = to * grps + (g + by) % grps
                else:
                    goal = t * grps + (g + max(by, 1)) % grps
                pairs.append((t * grps + g, goal))
        return lax.ppermute(array, axes, pairs)

    def call(kernel, name, inputs, **kw):
        return pl.pallas_call(
            kernel,
            in_specs=[vmem] * len(inputs),
            compiler_params=pltpu.CompilerParams(vmem_limit_bytes=32 << 20),
            name=name,
            **kw,
        )(*[placed(x, pltpu.VMEM) for x in inputs])

    def on_device(traces, validity, boundary_rows, boundary_count, pair_mask):
        per, seg, samples = traces.shape
        lines = per * seg
        columns = pair_mask.shape[1]
        starts, stretches = fourier_rows(samples)
        lag_basis = jnp.asarray(lag_table(samples))
        payload = pltpu.VMEM((lines, WIDE), BF16)
        sent = [(3, d) for d in range(1, grps)] + [(2, d) for d in reversed(range(grps))]
        soon = [(1, d) for d in range(1, grps)]
        late = [(2, d) for d in reversed(range(grps))] + [(1, 0)] + [(0, d) for d in range(1, grps)]
        inputs = [boundary_rows, boundary_count, validity, traces.reshape(lines, samples), lag_basis, pair_mask]
        mine, near, *rest, basis, mask = pl.pallas_call(
            lambda *refs: spectra_kernel(
                per, seg, samples, [1] + [way for way, _ in sent], starts, stretches, *refs
            ),
            out_shape=(payload,) * (2 + len(sent))
            + (pltpu.VMEM(lag_basis.shape, BF16), pltpu.VMEM(pair_mask.shape, jnp.int32)),
            in_specs=[hbm] * len(inputs),
            out_specs=(vmem,) * (4 + len(sent)),
            scratch_shapes=[
                pltpu.SMEM(boundary_rows.shape, jnp.int32),
                pltpu.SMEM(boundary_count.shape, jnp.int32),
                pltpu.VMEM(validity.shape, jnp.int32),
                pltpu.VMEM((lines, samples), F32),
                pltpu.VMEM((starts[-1], WIDE), F32),
                pltpu.VMEM((3 * STEP, WIDE), BF16),
                pltpu.VMEM((2 * LANE, 2 * LANE), BF16),
                pltpu.VMEM((per, seg, WIDE), F32),
                pltpu.VMEM((3, lines, LANE), F32),
                pltpu.SemaphoreType.DMA((6,)),
            ],
            compiler_params=pltpu.CompilerParams(vmem_limit_bytes=32 << 20),
            name="spectra",
        )(*[placed(x, pltpu.HBM) for x in inputs])
        came = [exchange(array, min(way, 4 - way), by) for (way, by), array in zip(sent, rest)]
        aside, far = came[: grps - 1], came[grps - 1 :]
        rows = per * columns
        spread, first = call(
            lambda *refs: ready_kernel(per, seg, *refs),
            "ready",
            [mine],
            out_shape=(
                pltpu.VMEM((per * lines, WIDE + LANE), F32),
                pltpu.VMEM((per * 8, WIDE + LANE), F32),
            ),
            out_specs=(vmem,) * 2,
        )
        passed = call(
            pass_kernel,
            "pass",
            [first, near, *aside],
            out_shape=(payload,) * grps,
            out_specs=(vmem,) * grps,
        )
        passed = [exchange(array, 1, 0) for array in passed]
        early, keep = call(
            lambda *refs: early_kernel(per, seg, grps, tiles, soon, *refs),
            "early",
            [mask, spread, first, *aside],
            out_shape=(pltpu.VMEM((rows, WIDE), F32), pltpu.VMEM((rows, LANE), F32)),
            out_specs=(vmem,) * 2,
            scratch_shapes=[pltpu.VMEM((max(len(soon), 1), lines, WIDE), F32)],
            cost_estimate=pl.CostEstimate(flops=100000000000, transcendentals=0, bytes_accessed=1000000000),
        )
        series = call(
            lambda *refs: middle_kernel(per, seg, grps, tiles, late[grps:], *refs),
            "middle",
            [basis, keep, spread, early, *passed],
            out_shape=pltpu.VMEM((rows, LAGS), F32),
            out_specs=vmem,
        )
        return call(
            lambda *refs: lags_kernel(per, seg, grps, tiles, late[:grps], *refs),
            "lags",
            [basis, keep, spread, series, *far],
            out_shape=jax.ShapeDtypeStruct((per, columns, LAGS), BF16),
            out_specs=hbm,
            scratch_shapes=[
                pltpu.VMEM((per, columns, LAGS), BF16),
                pltpu.SemaphoreType.DMA((pl.cdiv(LAGS, LAG_STEP),)),
            ],
        )

    return jax.shard_map(
        on_device,
        mesh=mesh,
        in_specs=(P(axes, None, None), P(axes, None), P(axes, None, None), P(axes, None), P(axes, None)),
        out_specs=P(axes, None, None),
        check_vma=False,
    )
```
